32 devices in a mesh: pos: 4 (over y, x), slab: 8 (over z, core).
Axes of the slice: x: 2, y: 2, z: 4, core: 2. Of those that a mesh axis runs over, the one named last changes fastest.
Arguments:
- labels: int32 [16, 256, 256], P('slab'), may hold values from 0 to 3
- magnet_mask: int32 [16, 256, 256], P('slab'), may hold values 0 or 1
- reluctivity: float32 [4], replicated, may hold values from 0.3 to 3
- rotor_shift: int32 [4], P('pos'), may hold values from 0 to 255
- potential: float32 [4, 16, 256, 256], P('pos', 'slab'), may hold values from -6 to 6
- adjoint_load: float32 [4, 16, 256, 256], P('pos', 'slab'), may hold values from -40 to 40
Outputs:
- shape_gradient: float32 [16, 256, 256], P('slab')
- adjoint: float32 [4, 16, 256, 256], P('pos', 'slab')
The draws below stay inside these ranges and needn't reach their ends.
All inputs are finite; a program needn't handle non-finite values. No bound on the sum of `magnet_mask` on one device may be relied on, other than what follows from the above.
Results may differ from the reference program's by a relative error of at most 0.0003.
Values sent between devices are 32-bit elements; how exact they have to be, the bound alone decides.
No kernel may reach another device: no remote copies, remote signals or barrier semaphores. Data moves between devices by JAX's collectives and lax.ppermute only.
A program may use at most 64 MiB of HBM per device.

```python
import math
import jax
import jax.numpy as jnp

CX = 256
CY = 256
ITERS = 2
MATERIALS = 4
NZ = 16
N_POS = 4


def draw_adjoint_load(key, part):
    first_key = jax.random.fold_in(jax.random.fold_in(key, 11), 0)
    base = jax.random.truncated_normal(first_key, -4.0, 4.0, (N_POS, NZ, CX, CY), jnp.float32)
    depth = jnp.arange(NZ, dtype=jnp.float32) / max(NZ - 1, 1)
    rising = jnp.exp(jnp.log(3.0) * depth)[None, :, None, None]
    return base * rising


def with_ends(drawn, stream_key, least, high):
    spot = [jax.random.randint(jax.random.fold_in(stream_key, axis), (), 0, length) for axis, length in enumerate(drawn.shape)]
    widest = drawn.shape.index(max(drawn.shape))
    neighbour = spot[:widest] + [(spot[widest] + 1) % drawn.shape[widest]] + spot[widest + 1:]
    return drawn.at[tuple(spot)].set(least).at[tuple(neighbour)].set(high)


def block_levels(own_key, extent, cuts, smallest, high):
    loudness = 1.0
    for axis_at, blocks in cuts:
        heights = jax.random.uniform(jax.random.fold_in(jax.random.fold_in(own_key, 6), axis_at), (blocks,), jnp.float32, smallest / len(cuts), high / len(cuts))
        loudness = loudness * jnp.repeat(jnp.exp(heights), extent[axis_at] // blocks).reshape((-1,) + (1,) * (len(extent) - 1 - axis_at))
    return loudness


def scatter_about(key, extent, width, limit, pieces=(), held_as=jnp.bfloat16):
    loudness = block_levels(key, extent, pieces, -0.22, 0.18) if pieces else 1.0
    values = jax.random.normal(key, extent, jnp.float32) * width * loudness
    return jnp.minimum(jnp.maximum(values, -limit), limit).astype(held_as)


def setup_inputs(seed: int = 0) -> dict:
    key_list = jax.random.split(jax.random.key(seed), 7)
    return {
        "labels": with_ends(jax.random.randint(key_list[0], (NZ, CX, CY), 0, 4), jax.random.fold_in(key_list[0], 1), 0, 3).astype(jnp.int32),
        "magnet_mask": with_ends((jax.random.randint(key_list[1], (NZ, CX, CY), 0, 2) < 1).astype(jnp.int32), jax.random.fold_in(key_list[1], 1), 0, 1),
        "reluctivity": jnp.clip(jnp.exp(jax.random.uniform(key_list[2], (MATERIALS,), jnp.float32, math.log(0.3), math.log(3.0))), 0.3, 3.0),
        "rotor_shift": with_ends(jax.random.randint(key_list[3], (N_POS,), 0, CY), jax.random.fold_in(key_list[3], 1), 0, CY - 1).astype(jnp.int32),
        "potential": scatter_about(key_list[4], (N_POS, NZ, CX, CY), 1.0, 6.0, ((0, 4), (1, 8)), jnp.float32),
        "adjoint_load": draw_adjoint_load(jax.random.fold_in(key_list[6], 71), 0),
    }


diagonal_shift = 0.5


def material_field(labels, reluctivity, offset):
    rotated = jnp.roll(labels, offset, axis=2)
    radial = jax.lax.broadcasted_iota(jnp.int32, labels.shape, 1)
    material = jnp.where(radial < labels.shape[1] // 2, rotated, labels)
    result = jnp.zeros(labels.shape, jnp.float32)
    for index in range(4):
        result = result + (material == index).astype(jnp.float32) * reluctivity[index]
    return result


def apply_operator(field, padded_field, relief, padded_relief):
    result = diagonal_shift * field
    result = result + 0.5 * (relief + padded_relief[2:]) * (field - padded_field[2:])
    result = result + 0.5 * (relief + padded_relief[:-2]) * (field - padded_field[:-2])
    radial_field = jnp.pad(field, ((0, 0), (1, 1), (0, 0)))
    radial_relief = jnp.pad(relief, ((0, 0), (1, 1), (0, 0)))
    result = result + 0.5 * (relief + radial_relief[:, 2:]) * (field - radial_field[:, 2:])
    result = result + 0.5 * (relief + radial_relief[:, :-2]) * (field - radial_field[:, :-2])
    for offset in (1, -1):
        result = result + 0.5 * (relief + jnp.roll(relief, offset, 2)) * (field - jnp.roll(field, offset, 2))
    return result


def gradient_term(stacked, padded_stack, relief, magnet_mask):
    axial = 0.5 * (padded_stack[:, 2:] - padded_stack[:, :-2])
    radial_pad = jnp.pad(stacked, ((0, 0), (0, 0), (1, 1), (0, 0)))
    radial = 0.5 * (radial_pad[:, :, 2:] - radial_pad[:, :, :-2])
    angular = 0.5 * (jnp.roll(stacked, -1, 3) - jnp.roll(stacked, 1, 3))
    inner = axial[0] * axial[1] + radial[0] * radial[1] + angular[0] * angular[1]
    square = axial[0] * axial[0] + radial[0] * radial[0] + angular[0] * angular[0]
    return magnet_mask.astype(jnp.float32) * relief * (inner + 0.5 * square)


def reference(labels, magnet_mask, reluctivity, rotor_shift, potential, adjoint_load):
    summed = jnp.zeros(labels.shape, jnp.float32)
    adjoints = []
    for position in range(N_POS):
        relief = material_field(labels, reluctivity, rotor_shift[position])
        padded_relief = jnp.pad(relief, ((1, 1), (0, 0), (0, 0)))

        def operate(field):
            return apply_operator(field, jnp.pad(field, ((1, 1), (0, 0), (0, 0))), relief, padded_relief)

        solution = jnp.zeros(relief.shape, jnp.float32)
        residual = adjoint_load[position]
        direction = residual
        norm_now = jnp.sum(residual * residual)
        for iteration in range(ITERS):
            image = operate(direction)
            alpha = norm_now / jnp.sum(direction * image)
            solution = solution + alpha * direction
            residual = residual - alpha * image
            norm_next = jnp.sum(residual * residual)
            direction = residual + (norm_next / norm_now) * direction
            norm_now = norm_next
        adjoints.append(solution)
        stacked = jnp.stack([potential[position], solution])
        padded_stack = jnp.pad(stacked, ((0, 0), (1, 1), (0, 0), (0, 0)))
        summed = summed + gradient_term(stacked, padded_stack, relief, magnet_mask)
    return summed / N_POS, jnp.stack(adjoints)
```

```python
import functools

import jax
import jax.numpy as jnp
from jax import lax
from jax.experimental import pallas as pl
from jax.experimental.pallas import tpu as pltpu
from jax.sharding import PartitionSpec as P


ROWS = 16
VMEM = pltpu.VMEM
SMEM = pltpu.SMEM
SUMS = 5


def params(**kw):
    return pltpu.CompilerParams(vmem_limit_bytes=40 * 1024 * 1024, **kw)


def shifted(ref, index, start, offset):
    total, columns = ref.shape[-2:]
    zero = jnp.zeros((1, columns), jnp.float32)
    if start + offset < 0:
        return jnp.concatenate([zero, ref[index, 0 : ROWS - 1, :]], axis=0)
    if start + offset + ROWS > total:
        return jnp.concatenate([ref[index, start + 1 : total, :], zero], axis=0)
    return ref[index, start + offset : start + offset + ROWS, :]


def turn(value, offset):
    return pltpu.roll(value, offset % value.shape[1], 1)


def in_plane(nu_ref, nu_index, ref, index, start):
    nu = nu_ref[nu_index, start : start + ROWS, :]
    v = ref[index, start : start + ROWS, :]
    flux = (nu + turn(nu, -1)) * (v - turn(v, -1))
    total = flux - turn(flux, 1)
    for offset in (-1, 1):
        total = total + (nu + shifted(nu_ref, nu_index, start, offset)) * (
            v - shifted(ref, index, start, offset)
        )
    return nu, v, total


def place():
    slab = lax.axis_index("slab")
    return slab, lax.rem(slab, 2)


def open_kernel(reluctivity, shift, labels, load, potential, far, near, far_potential):
    _, even = place()
    total = labels.shape[1]
    r0, r1, r2, r3 = (reluctivity[i] for i in range(4))
    offset = shift[0]
    for layer, out in ((even, far), (1 - even, near)):
        for start in range(0, total, ROWS):
            rows = slice(start, start + ROWS)
            material = labels[layer, rows, :]
            if start < total // 2:
                material = pltpu.roll(material, offset, 1)
            out[0, rows, :] = jnp.where(
                material < 2,
                jnp.where(material == 0, r0, r1),
                jnp.where(material == 2, r2, r3),
            )
            out[1, rows, :] = load[layer, rows, :]
            moved = potential[layer, rows, :]
            if out is far:
                far_potential[0, rows, :] = moved
            else:
                out[3, rows, :] = moved
    for own, other in ((far, near), (near, far)):
        for start in range(0, total, ROWS):
            rows = slice(start, start + ROWS)
            nu, v, total_flux = in_plane(own, 0, own, 1, start)
            total_flux = total_flux + (nu + other[0, rows, :]) * (v - other[1, rows, :])
            own[2, rows, :] = 0.5 * (v + total_flux)


def fold(value):
    return jnp.sum(value.reshape(ROWS // 8, 8, value.shape[1]), axis=0)


def sums_kernel(far, near, far_in, near_in, image, image_in, sums):
    slab, _ = place()
    count = lax.axis_size("slab")
    total, columns = far.shape[1:]
    beyond = jnp.where((slab > 0) & (slab < count - 1), 1.0, 0.0).astype(jnp.float32)
    sides = ((far, far_in, beyond), (near, near_in, None))
    nil = jnp.zeros((8, columns), jnp.float32)
    m0, m1 = nil, nil
    for side, (own, halo, keep) in enumerate(sides):
        for start in range(0, total, ROWS):
            rows = slice(start, start + ROWS)
            v = own[1, rows, :]
            flux = 0.5 * (own[0, rows, :] + halo[0, rows, :]) * (v - halo[1, rows, :])
            y = own[2, rows, :] + flux
            outer = halo[2, rows, :] - flux
            image[side, rows, :] = y
            image_in[side, rows, :] = outer if keep is None else keep * outer
            m0 = m0 + fold(v * v)
            m1 = m1 + fold(v * y)
    m0 = jnp.sum(m0, keepdims=True)
    m1 = jnp.sum(m1, keepdims=True)
    c = jnp.where(m0 > 0, m1 / m0, 0.0)
    q, s, t = nil, nil, nil
    for side, (own, halo, _) in enumerate(sides):
        for start in range(0, total, ROWS):
            rows = slice(start, start + ROWS)
            nu, y, total_flux = in_plane(own, 0, image, side, start)
            other = (near, far)[side]
            total_flux = total_flux + (nu + other[0, rows, :]) * (y - image[1 - side, rows, :])
            total_flux = total_flux + (nu + halo[0, rows, :]) * (y - image_in[side, rows, :])
            z = 0.5 * (y + total_flux)
            v = own[1, rows, :]
            w = y - c * v
            u = z - c * y
            q = q + fold(w * w)
            s = s + fold(w * u)
            t = t + fold(v * u)
    here = lax.broadcasted_iota(jnp.int32, sums.shape[1:], 0) == slab
    for index, value in enumerate((m0, m1, q, s, t)):
        value = jnp.sum(value, keepdims=True) if index > 1 else value
        sums[index] = jnp.where(here, value, 0.0)


def finish_kernel(
    sums, far, near, far_in, near_in, image, image_in, potential, far_potential, mask, adjoint, term, mixed, mixed_in
):
    _, even = place()
    total = far.shape[1]
    m0_d, m1_d, q_d, s_d, t_d = (sums[i] for i in range(SUMS))
    m0 = jnp.sum(m0_d, axis=0, keepdims=True)
    m1 = jnp.sum(m1_d, axis=0, keepdims=True)
    c = m1 / m0
    delta = jnp.where(m0_d > 0, m1_d / m0_d, 0.0) - c
    ww = jnp.sum(q_d + delta * delta * m0_d, axis=0, keepdims=True)
    waw = jnp.sum(s_d + delta * (q_d + t_d) + delta * delta * m1_d, axis=0, keepdims=True)
    alpha0 = m0 / m1
    beta = alpha0 * (ww * alpha0 / m0)
    divisor = waw - ww * (ww / m1)
    alpha1 = jnp.where(divisor == 0, 0.0, ww / divisor)
    a = (alpha0 + alpha1 * (1.0 + beta))[:, 0:1]
    b = (-alpha1 * alpha0)[:, 0:1]
    scale = 0.25 / lax.axis_size("pos")
    sides = ((far, even, far_in, far_potential, 0), (near, 1 - even, near_in, near_in, 3))
    for side, (own, layer, halo, halo_potential, at) in enumerate(sides):
        for start in range(0, total, ROWS):
            rows = slice(start, start + ROWS)
            out = a * own[1, rows, :] + b * image[side, rows, :]
            adjoint[layer, rows, :] = out
            mixed[side, rows, :] = out + 0.5 * potential[layer, rows, :]
            outer = a * halo[1, rows, :] + b * image_in[side, rows, :]
            mixed_in[side, rows, :] = outer + 0.5 * halo_potential[at, rows, :]
    for side, (own, layer, halo, halo_potential, at) in enumerate(sides):
        for start in range(0, total, ROWS):
            rows = slice(start, start + ROWS)
            g = potential[layer, rows, :]
            f = mixed[side, rows, :]
            result = (halo_potential[at, rows, :] - potential[1 - layer, rows, :]) * (
                mixed_in[side, rows, :] - mixed[1 - side, rows, :]
            )
            result = result + (turn(g, -1) - turn(g, 1)) * (turn(f, -1) - turn(f, 1))
            result = result + (
                shifted(potential, layer, start, 1) - shifted(potential, layer, start, -1)
            ) * (shifted(mixed, side, start, 1) - shifted(mixed, side, start, -1))
            weight = mask[layer, rows, :].astype(jnp.float32) * own[0, rows, :]
            term[layer, rows, :] = weight * (scale * result)


def pairs(size, first):
    out = []
    for i in range(first, size - 1, 2):
        out += [(i, i + 1), (i + 1, i)]
    return out


def gather_sums(sums, axis, size):
    if size & (size - 1):
        return lax.psum(sums, axis)
    step = 1
    while step < size:
        sums = sums + lax.ppermute(sums, axis, [(i, i ^ step) for i in range(size)])
        step *= 2
    return sums


def sum_positions(term, positions, slabs):
    if positions & (positions - 1):
        return lax.psum(term, "pos")
    bits = positions.bit_length() - 1
    for step in range(bits):
        route = []
        for p in range(positions):
            for s in range(slabs):
                bit = step if s % 2 == 0 else bits - 1 - step
                route.append((p * slabs + s, (p ^ (1 << bit)) * slabs + s))
        term = term + lax.ppermute(term, ("pos", "slab"), route)
    return term


def local(labels, magnet_mask, reluctivity, rotor_shift, potential, adjoint_load):
    layers, radial, angular = labels.shape
    positions, slabs = lax.axis_size("pos"), lax.axis_size("slab")
    if layers != 2 or slabs % 2 or radial % (2 * ROWS):
        raise ValueError("unsupported sizes")
    potential, load = potential[0], adjoint_load[0]
    f32 = functools.partial(jax.ShapeDtypeStruct, dtype=jnp.float32)
    plane = (radial, angular)
    vmem = pl.BlockSpec(memory_space=VMEM)
    smem = pl.BlockSpec(memory_space=SMEM)
    far, near, far_potential = pl.pallas_call(
        open_kernel,
        out_shape=(f32((3,) + plane), f32((4,) + plane), f32((1,) + plane)),
        in_specs=[smem, smem, vmem, vmem, vmem],
        out_specs=(vmem,) * 3,
        compiler_params=params(),
        name="open",
    )(reluctivity, rotor_shift, labels, load, potential)
    far_in = lax.ppermute(far, "slab", pairs(slabs, 1))
    near_in = lax.ppermute(near, "slab", pairs(slabs, 0))
    far_potential = lax.ppermute(far_potential, "slab", pairs(slabs, 1))
    image, image_in, sums = pl.pallas_call(
        sums_kernel,
        out_shape=(f32((2,) + plane), f32((2,) + plane), f32((SUMS, slabs, 128))),
        in_specs=[vmem] * 4,
        out_specs=(vmem,) * 3,
        compiler_params=params(),
        name="sums",
    )(far, near, far_in, near_in)
    sums = gather_sums(sums, "slab", slabs)
    adjoint, term = pl.pallas_call(
        finish_kernel,
        out_shape=(f32((2,) + plane), f32((2,) + plane)),
        in_specs=[vmem] * 10,
        out_specs=(vmem,) * 2,
        scratch_shapes=[VMEM((2,) + plane, jnp.float32)] * 2,
        compiler_params=params(),
        name="finish",
    )(sums, far, near, far_in, near_in, image, image_in, potential, far_potential, magnet_mask)
    return sum_positions(term, positions, slabs), adjoint[None]


def solution(mesh):
    return jax.shard_map(
        local,
        mesh=mesh,
        in_specs=(
            P("slab", None, None),
            P("slab", None, None),
            P(),
            P("pos"),
            P("pos", "slab", None, None),
            P("pos", "slab", None, None),
        ),
        out_specs=(P("slab", None, None), P("pos", "slab", None, None)),
        check_vma=False,
    )
```

```python
import functools

import jax
import jax.numpy as jnp
from jax import lax
from jax.experimental import pallas as pl
from jax.experimental.pallas import tpu as pltpu
from jax.sharding import PartitionSpec as P


ROWS = 16
VMEM = pltpu.VMEM
SMEM = pltpu.SMEM
SUMS = 5
CHUNKS = 2


def params():
    return pltpu.CompilerParams(vmem_limit_bytes=40 * 1024 * 1024)


def shifted(ref, index, start, offset):
    total, columns = ref.shape[-2:]
    zero = jnp.zeros((1, columns), jnp.float32)
    if start + offset < 0:
        return jnp.concatenate([zero, ref[index, 0 : ROWS - 1, :]], axis=0)
    if start + offset + ROWS > total:
        return jnp.concatenate([ref[index, start + 1 : total, :], zero], axis=0)
    return ref[index, start + offset : start + offset + ROWS, :]


def turn(value, offset):
    return pltpu.roll(value, offset % value.shape[1], 1)


def in_plane(nu_ref, nu_index, ref, index, start):
    nu = nu_ref[nu_index, start : start + ROWS, :]
    v = ref[index, start : start + ROWS, :]
    flux = (nu + turn(nu, -1)) * (v - turn(v, -1))
    total = flux - turn(flux, 1)
    for offset in (-1, 1):
        total = total + (nu + shifted(nu_ref, nu_index, start, offset)) * (
            v - shifted(ref, index, start, offset)
        )
    return nu, v, total


def place():
    slab = lax.axis_index("slab")
    return slab, lax.rem(slab, 2)


def open_kernel(reluctivity, shift, labels, load, potential, far, near, far_potential, held, table, sems):
    _, even = place()
    odd = 1 - even
    total = labels.shape[1]
    moves = (
        (labels.at[even], held.at[0]),
        (labels.at[odd], held.at[1]),
        (load.at[even], far.at[1]),
        (load.at[odd], near.at[1]),
        (potential.at[even], far_potential.at[0]),
        (potential.at[odd], near.at[3]),
        (reluctivity, table),
    )
    copies = [pltpu.make_async_copy(src, dst, sems.at[i]) for i, (src, dst) in enumerate(moves)]
    for copy in copies:
        copy.start()
    copies[-1].wait()
    r0, r1, r2, r3 = (table[i] for i in range(4))
    offset = shift[0]
    for side, out in enumerate((far, near)):
        copies[side].wait()
        for start in range(0, total, ROWS):
            rows = slice(start, start + ROWS)
            material = held[side, rows, :]
            if start < total // 2:
                material = pltpu.roll(material, offset, 1)
            out[0, rows, :] = jnp.where(
                material < 2,
                jnp.where(material == 0, r0, r1),
                jnp.where(material == 2, r2, r3),
            )
    for copy in copies[2:-1]:
        copy.wait()
    for own, other in ((far, near), (near, far)):
        for start in range(0, total, ROWS):
            rows = slice(start, start + ROWS)
            nu, v, total_flux = in_plane(own, 0, own, 1, start)
            total_flux = total_flux + (nu + other[0, rows, :]) * (v - other[1, rows, :])
            own[2, rows, :] = 0.5 * (v + total_flux)


def fold(value):
    return jnp.sum(value.reshape(ROWS // 8, 8, value.shape[1]), axis=0)


def sums_kernel(far, near, far_in, near_in, image, image_in, sums):
    slab, _ = place()
    count = lax.axis_size("slab")
    total, columns = far.shape[1:]
    beyond = jnp.where((slab > 0) & (slab < count - 1), 1.0, 0.0).astype(jnp.float32)
    sides = ((far, far_in, beyond), (near, near_in, None))
    nil = jnp.zeros((8, columns), jnp.float32)
    m0, m1 = nil, nil
    for side, (own, halo, keep) in enumerate(sides):
        for start in range(0, total, ROWS):
            rows = slice(start, start + ROWS)
            v = own[1, rows, :]
            flux = 0.5 * (own[0, rows, :] + halo[0, rows, :]) * (v - halo[1, rows, :])
            y = own[2, rows, :] + flux
            outer = halo[2, rows, :] - flux
            image[side, rows, :] = y
            image_in[side, rows, :] = outer if keep is None else keep * outer
            m0 = m0 + fold(v * v)
            m1 = m1 + fold(v * y)
    m0 = jnp.sum(m0, keepdims=True)
    m1 = jnp.sum(m1, keepdims=True)
    c = jnp.where(m0 > 0, m1 / m0, 0.0)
    q, s, t = nil, nil, nil
    for side, (own, halo, _) in enumerate(sides):
        for start in range(0, total, ROWS):
            rows = slice(start, start + ROWS)
            nu, y, total_flux = in_plane(own, 0, image, side, start)
            other = (near, far)[side]
            total_flux = total_flux + (nu + other[0, rows, :]) * (y - image[1 - side, rows, :])
            total_flux = total_flux + (nu + halo[0, rows, :]) * (y - image_in[side, rows, :])
            z = 0.5 * (y + total_flux)
            v = own[1, rows, :]
            w = y - c * v
            u = z - c * y
            q = q + fold(w * w)
            s = s + fold(w * u)
            t = t + fold(v * u)
    here = lax.broadcasted_iota(jnp.int32, sums.shape[1:], 0) == slab
    for index, value in enumerate((m0, m1, q, s, t)):
        value = jnp.sum(value, keepdims=True) if index > 1 else value
        sums[index] = jnp.where(here, value, 0.0)


def finish_kernel(
    sums, far, near, far_in, near_in, image, image_in, potential, far_potential, mask, adjoint, *rest
):
    *terms, mixed, mixed_in = rest
    _, even = place()
    total = far.shape[1]
    m0_d, m1_d, q_d, s_d, t_d = (sums[i] for i in range(SUMS))
    m0 = jnp.sum(m0_d, axis=0, keepdims=True)
    m1 = jnp.sum(m1_d, axis=0, keepdims=True)
    c = m1 / m0
    delta = jnp.where(m0_d > 0, m1_d / m0_d, 0.0) - c
    ww = jnp.sum(q_d + delta * delta * m0_d, axis=0, keepdims=True)
    waw = jnp.sum(s_d + delta * (q_d + t_d) + delta * delta * m1_d, axis=0, keepdims=True)
    alpha0 = m0 / m1
    beta = alpha0 * (ww * alpha0 / m0)
    divisor = waw - ww * (ww / m1)
    alpha1 = jnp.where(divisor == 0, 0.0, ww / divisor)
    a = (alpha0 + alpha1 * (1.0 + beta))[:, 0:1]
    b = (-alpha1 * alpha0)[:, 0:1]
    scale = 0.25 / lax.axis_size("pos")
    sides = ((far, even, far_in, far_potential, 0), (near, 1 - even, near_in, near_in, 3))
    for side, (own, layer, halo, halo_potential, at) in enumerate(sides):
        for start in range(0, total, ROWS):
            rows = slice(start, start + ROWS)
            out = a * own[1, rows, :] + b * image[side, rows, :]
            adjoint[layer, rows, :] = out
            mixed[side, rows, :] = out + 0.5 * potential[layer, rows, :]
            outer = a * halo[1, rows, :] + b * image_in[side, rows, :]
            mixed_in[side, rows, :] = outer + 0.5 * halo_potential[at, rows, :]
    for side, (own, layer, halo, halo_potential, at) in enumerate(sides):
        for start in range(0, total, ROWS):
            rows = slice(start, start + ROWS)
            g = potential[layer, rows, :]
            f = mixed[side, rows, :]
            result = (halo_potential[at, rows, :] - potential[1 - layer, rows, :]) * (
                mixed_in[side, rows, :] - mixed[1 - side, rows, :]
            )
            result = result + (turn(g, -1) - turn(g, 1)) * (turn(f, -1) - turn(f, 1))
            result = result + (
                shifted(potential, layer, start, 1) - shifted(potential, layer, start, -1)
            ) * (shifted(mixed, side, start, 1) - shifted(mixed, side, start, -1))
            weight = mask[layer, rows, :].astype(jnp.float32) * own[0, rows, :]
            span = total // CHUNKS
            terms[start // span][layer, start % span : start % span + ROWS, :] = weight * (scale * result)


def in_hbm(x):
    return pltpu.with_memory_space_constraint(x, pltpu.HBM)


def pairs(size, first):
    out = []
    for i in range(first, size - 1, 2):
        out += [(i, i + 1), (i + 1, i)]
    return out


def gather_sums(sums, axis, size):
    if size & (size - 1):
        return lax.psum(sums, axis)
    step = 1
    while step < size:
        sums = sums + lax.ppermute(sums, axis, [(i, i ^ step) for i in range(size)])
        step *= 2
    return sums


def sum_positions(term, positions, slabs):
    if positions & (positions - 1):
        return lax.psum(term, "pos")
    bits = positions.bit_length() - 1
    for step in range(bits):
        route = []
        for p in range(positions):
            for s in range(slabs):
                bit = step if s % 2 == 0 else bits - 1 - step
                route.append((p * slabs + s, (p ^ (1 << bit)) * slabs + s))
        term = term + lax.ppermute(term, ("pos", "slab"), route)
    return term


def local(labels, magnet_mask, reluctivity, rotor_shift, potential, adjoint_load):
    layers, radial, angular = labels.shape
    positions, slabs = lax.axis_size("pos"), lax.axis_size("slab")
    if layers != 2 or slabs % 2 or radial % (2 * CHUNKS * ROWS):
        raise ValueError("unsupported sizes")
    potential, load = potential[0], adjoint_load[0]
    f32 = functools.partial(jax.ShapeDtypeStruct, dtype=jnp.float32)
    plane = (radial, angular)
    vmem = pl.BlockSpec(memory_space=VMEM)
    smem = pl.BlockSpec(memory_space=SMEM)
    hbm = pl.BlockSpec(memory_space=pltpu.HBM)
    far, near, far_potential = pl.pallas_call(
        open_kernel,
        out_shape=tuple(pltpu.VMEM((k,) + plane, jnp.float32) for k in (3, 4, 1)),
        in_specs=[hbm, smem, hbm, hbm, hbm],
        out_specs=(vmem,) * 3,
        scratch_shapes=[
            VMEM((2,) + plane, jnp.int32),
            SMEM(reluctivity.shape, jnp.float32),
            pltpu.SemaphoreType.DMA((7,)),
        ],
        compiler_params=params(),
        name="open",
    )(in_hbm(reluctivity), rotor_shift, in_hbm(labels), in_hbm(load), in_hbm(potential))
    far_in = lax.ppermute(far, "slab", pairs(slabs, 1))
    near_in = lax.ppermute(near, "slab", pairs(slabs, 0))
    far_potential = lax.ppermute(far_potential, "slab", pairs(slabs, 1))
    image, image_in, sums = pl.pallas_call(
        sums_kernel,
        out_shape=(f32((2,) + plane), f32((2,) + plane), f32((SUMS, slabs, 128))),
        in_specs=[vmem] * 4,
        out_specs=(vmem,) * 3,
        compiler_params=params(),
        name="sums",
    )(far, near, far_in, near_in)
    sums = gather_sums(sums, "slab", slabs)
    adjoint, *terms = pl.pallas_call(
        finish_kernel,
        out_shape=(pltpu.VMEM((2,) + plane, jnp.float32),)
        + (f32((2, radial // CHUNKS, angular)),) * CHUNKS,
        in_specs=[vmem] * 10,
        out_specs=(vmem,) * (1 + CHUNKS),
        scratch_shapes=[VMEM((2,) + plane, jnp.float32)] * 2,
        compiler_params=params(),
        name="finish",
    )(sums, far, near, far_in, near_in, image, image_in, potential, far_potential, magnet_mask)
    gradient = [sum_positions(term, positions, slabs) for term in terms]
    return jnp.concatenate(gradient, axis=1), adjoint[None]


def solution(mesh):
    return jax.shard_map(
        local,
        mesh=mesh,
        in_specs=(
            P("slab", None, None),
            P("slab", None, None),
            P(),
            P("pos"),
            P("pos", "slab", None, None),
            P("pos", "slab", None, None),
        ),
        out_specs=(P("slab", None, None), P("pos", "slab", None, None)),
        check_vma=False,
    )
```

```python
import functools

import jax
import jax.numpy as jnp
from jax import lax
from jax.experimental import pallas as pl
from jax.experimental.pallas import tpu as pltpu
from jax.sharding import PartitionSpec as P


ROWS = 16
VMEM = pltpu.VMEM
SMEM = pltpu.SMEM
SUMS = 5
CHUNKS = 2


def params():
    return pltpu.CompilerParams(vmem_limit_bytes=40 * 1024 * 1024)


def shifted(ref, index, start, offset):
    total, columns = ref.shape[-2:]
    zero = jnp.zeros((1, columns), jnp.float32)
    if start + offset < 0:
        return jnp.concatenate([zero, ref[index, 0 : ROWS - 1, :]], axis=0)
    if start + offset + ROWS > total:
        return jnp.concatenate([ref[index, start + 1 : total, :], zero], axis=0)
    return ref[index, start + offset : start + offset + ROWS, :]


def turn(value, offset):
    return pltpu.roll(value, offset % value.shape[1], 1)


def in_plane(nu_ref, nu_index, ref, index, start):
    nu = nu_ref[nu_index, start : start + ROWS, :]
    v = ref[index, start : start + ROWS, :]
    flux = (nu + turn(nu, -1)) * (v - turn(v, -1))
    total = flux - turn(flux, 1)
    for offset in (-1, 1):
        total = total + (nu + shifted(nu_ref, nu_index, start, offset)) * (
            v - shifted(ref, index, start, offset)
        )
    return nu, v, total


def place():
    slab = lax.axis_index("slab")
    return slab, lax.rem(slab, 2)


def open_kernel(reluctivity, shift, labels, load, potential, far, near, far_potential, held, table, sems):
    _, even = place()
    odd = 1 - even
    total = labels.shape[1]
    moves = (
        (labels.at[even], held.at[0]),
        (labels.at[odd], held.at[1]),
        (load.at[even], far.at[1]),
        (load.at[odd], near.at[1]),
        (potential.at[even], far_potential.at[0]),
        (potential.at[odd], near.at[3]),
        (reluctivity, table),
    )
    copies = [pltpu.make_async_copy(src, dst, sems.at[i]) for i, (src, dst) in enumerate(moves)]
    for copy in copies:
        copy.start()
    copies[-1].wait()
    r0, r1, r2, r3 = (table[i] for i in range(4))
    offset = shift[0]
    for side, out in enumerate((far, near)):
        copies[side].wait()
        for start in range(0, total, ROWS):
            rows = slice(start, start + ROWS)
            material = held[side, rows, :]
            if start < total // 2:
                material = pltpu.roll(material, offset, 1)
            out[0, rows, :] = jnp.where(
                material < 2,
                jnp.where(material == 0, r0, r1),
                jnp.where(material == 2, r2, r3),
            )
    for copy in copies[2:-1]:
        copy.wait()
    for own, other in ((far, near), (near, far)):
        for start in range(0, total, ROWS):
            rows = slice(start, start + ROWS)
            nu, v, total_flux = in_plane(own, 0, own, 1, start)
            total_flux = total_flux + (nu + other[0, rows, :]) * (v - other[1, rows, :])
            own[2, rows, :] = 0.5 * (v + total_flux)


def fold(value):
    return jnp.sum(value.reshape(ROWS // 8, 8, value.shape[1]), axis=0)


def sums_kernel(far, near, far_in, near_in, image, image_in, sums):
    slab, _ = place()
    count = lax.axis_size("slab")
    total, columns = far.shape[1:]
    beyond = jnp.where((slab > 0) & (slab < count - 1), 1.0, 0.0).astype(jnp.float32)
    sides = ((far, far_in, beyond), (near, near_in, None))
    nil = jnp.zeros((8, columns), jnp.float32)
    m0, m1 = nil, nil
    for side, (own, halo, keep) in enumerate(sides):
        for start in range(0, total, ROWS):
            rows = slice(start, start + ROWS)
            v = own[1, rows, :]
            flux = 0.5 * (own[0, rows, :] + halo[0, rows, :]) * (v - halo[1, rows, :])
            y = own[2, rows, :] + flux
            outer = halo[2, rows, :] - flux
            image[side, rows, :] = y
            image_in[side, rows, :] = outer if keep is None else keep * outer
            m0 = m0 + fold(v * v)
            m1 = m1 + fold(v * y)
    m0 = jnp.sum(m0, keepdims=True)
    m1 = jnp.sum(m1, keepdims=True)
    c = jnp.where(m0 > 0, m1 / m0, 0.0)
    q, s, t = nil, nil, nil
    for side, (own, halo, _) in enumerate(sides):
        for start in range(0, total, ROWS):
            rows = slice(start, start + ROWS)
            nu, y, total_flux = in_plane(own, 0, image, side, start)
            other = (near, far)[side]
            total_flux = total_flux + (nu + other[0, rows, :]) * (y - image[1 - side, rows, :])
            total_flux = total_flux + (nu + halo[0, rows, :]) * (y - image_in[side, rows, :])
            z = 0.5 * (y + total_flux)
            v = own[1, rows, :]
            w = y - c * v
            u = z - c * y
            q = q + fold(w * w)
            s = s + fold(w * u)
            t = t + fold(v * u)
    for index, value in enumerate((m0, m1, q, s, t)):
        value = jnp.sum(value, keepdims=True) if index > 1 else value
        sums[:, index : index + 1, :] = jnp.broadcast_to(value[None], (sums.shape[0], 1, sums.shape[2]))


def finish_kernel(
    sums, far, near, far_in, near_in, image, image_in, potential, far_potential, mask, adjoint, *rest
):
    *terms, mixed, mixed_in = rest
    _, even = place()
    total = far.shape[1]
    m0_d, m1_d, q_d, s_d, t_d = (sums[:, i, :] for i in range(SUMS))
    m0 = jnp.sum(m0_d, axis=0, keepdims=True)
    m1 = jnp.sum(m1_d, axis=0, keepdims=True)
    c = m1 / m0
    delta = jnp.where(m0_d > 0, m1_d / m0_d, 0.0) - c
    ww = jnp.sum(q_d + delta * delta * m0_d, axis=0, keepdims=True)
    waw = jnp.sum(s_d + delta * (q_d + t_d) + delta * delta * m1_d, axis=0, keepdims=True)
    alpha0 = m0 / m1
    beta = alpha0 * (ww * alpha0 / m0)
    divisor = waw - ww * (ww / m1)
    alpha1 = jnp.where(divisor == 0, 0.0, ww / divisor)
    a = (alpha0 + alpha1 * (1.0 + beta))[:, 0:1]
    b = (-alpha1 * alpha0)[:, 0:1]
    scale = 0.25 / lax.axis_size("pos")
    sides = ((far, even, far_in, far_potential, 0), (near, 1 - even, near_in, near_in, 3))
    for side, (own, layer, halo, halo_potential, at) in enumerate(sides):
        for start in range(0, total, ROWS):
            rows = slice(start, start + ROWS)
            out = a * own[1, rows, :] + b * image[side, rows, :]
            adjoint[layer, rows, :] = out
            mixed[side, rows, :] = out + 0.5 * potential[layer, rows, :]
            outer = a * halo[1, rows, :] + b * image_in[side, rows, :]
            mixed_in[side, rows, :] = outer + 0.5 * halo_potential[at, rows, :]
    for side, (own, layer, halo, halo_potential, at) in enumerate(sides):
        for start in range(0, total, ROWS):
            rows = slice(start, start + ROWS)
            g = potential[layer, rows, :]
            f = mixed[side, rows, :]
            result = (halo_potential[at, rows, :] - potential[1 - layer, rows, :]) * (
                mixed_in[side, rows, :] - mixed[1 - side, rows, :]
            )
            result = result + (turn(g, -1) - turn(g, 1)) * (turn(f, -1) - turn(f, 1))
            result = result + (
                shifted(potential, layer, start, 1) - shifted(potential, layer, start, -1)
            ) * (shifted(mixed, side, start, 1) - shifted(mixed, side, start, -1))
            weight = mask[layer, rows, :].astype(jnp.float32) * own[0, rows, :]
            span = total // CHUNKS
            terms[start // span][layer, start % span : start % span + ROWS, :] = weight * (scale * result)


def in_hbm(x):
    return pltpu.with_memory_space_constraint(x, pltpu.HBM)


def pairs(size, first):
    out = []
    for i in range(first, size - 1, 2):
        out += [(i, i + 1), (i + 1, i)]
    return out


def sum_positions(term, positions, slabs):
    if positions & (positions - 1):
        return lax.psum(term, "pos")
    bits = positions.bit_length() - 1
    for step in range(bits):
        route = []
        for p in range(positions):
            for s in range(slabs):
                bit = step if s % 2 == 0 else bits - 1 - step
                route.append((p * slabs + s, (p ^ (1 << bit)) * slabs + s))
        term = term + lax.ppermute(term, ("pos", "slab"), route)
    return term


def local(labels, magnet_mask, reluctivity, rotor_shift, potential, adjoint_load):
    layers, radial, angular = labels.shape
    positions, slabs = lax.axis_size("pos"), lax.axis_size("slab")
    if layers != 2 or slabs % 2 or radial % (2 * CHUNKS * ROWS):
        raise ValueError("unsupported sizes")
    potential, load = potential[0], adjoint_load[0]
    f32 = functools.partial(jax.ShapeDtypeStruct, dtype=jnp.float32)
    plane = (radial, angular)
    vmem = pl.BlockSpec(memory_space=VMEM)
    smem = pl.BlockSpec(memory_space=SMEM)
    hbm = pl.BlockSpec(memory_space=pltpu.HBM)
    far, near, far_potential = pl.pallas_call(
        open_kernel,
        out_shape=tuple(pltpu.VMEM((k,) + plane, jnp.float32) for k in (3, 4, 1)),
        in_specs=[hbm, smem, hbm, hbm, hbm],
        out_specs=(vmem,) * 3,
        scratch_shapes=[
            VMEM((2,) + plane, jnp.int32),
            SMEM(reluctivity.shape, jnp.float32),
            pltpu.SemaphoreType.DMA((7,)),
        ],
        compiler_params=params(),
        name="open",
    )(in_hbm(reluctivity), rotor_shift, in_hbm(labels), in_hbm(load), in_hbm(potential))
    far_in = lax.ppermute(far, "slab", pairs(slabs, 1))
    near_in = lax.ppermute(near, "slab", pairs(slabs, 0))
    far_potential = lax.ppermute(far_potential, "slab", pairs(slabs, 1))
    image, image_in, sums = pl.pallas_call(
        sums_kernel,
        out_shape=(f32((2,) + plane), f32((2,) + plane), f32((slabs, 8, 128))),
        in_specs=[vmem] * 4,
        out_specs=(vmem,) * 3,
        compiler_params=params(),
        name="sums",
    )(far, near, far_in, near_in)
    sums = lax.all_to_all(sums, "slab", 0, 0, tiled=True)
    adjoint, *terms = pl.pallas_call(
        finish_kernel,
        out_shape=(pltpu.VMEM((2,) + plane, jnp.float32),)
        + (f32((2, radial // CHUNKS, angular)),) * CHUNKS,
        in_specs=[vmem] * 10,
        out_specs=(vmem,) * (1 + CHUNKS),
        scratch_shapes=[VMEM((2,) + plane, jnp.float32)] * 2,
        compiler_params=params(),
        name="finish",
    )(sums, far, near, far_in, near_in, image, image_in, potential, far_potential, magnet_mask)
    gradient = [sum_positions(term, positions, slabs) for term in terms]
    return jnp.concatenate(gradient, axis=1), adjoint[None]


def solution(mesh):
    return jax.shard_map(
        local,
        mesh=mesh,
        in_specs=(
            P("slab", None, None),
            P("slab", None, None),
            P(),
            P("pos"),
            P("pos", "slab", None, None),
            P("pos", "slab", None, None),
        ),
        out_specs=(P("slab", None, None), P("pos", "slab", None, None)),
        check_vma=False,
    )
```

```python
import functools

import jax
import jax.numpy as jnp
from jax import lax
from jax.experimental import pallas as pl
from jax.experimental.pallas import tpu as pltpu
from jax.sharding import PartitionSpec as P


ROWS = 16
VMEM = pltpu.VMEM
SMEM = pltpu.SMEM
SUMS = 5
CHUNKS = 4


def params():
    return pltpu.CompilerParams(vmem_limit_bytes=40 * 1024 * 1024)


def shifted(ref, index, start, offset):
    total, columns = ref.shape[-2:]
    zero = jnp.zeros((1, columns), jnp.float32)
    if start + offset < 0:
        return jnp.concatenate([zero, ref[index, 0 : ROWS - 1, :]], axis=0)
    if start + offset + ROWS > total:
        return jnp.concatenate([ref[index, start + 1 : total, :], zero], axis=0)
    return ref[index, start + offset : start + offset + ROWS, :]


def turn(value, offset):
    return pltpu.roll(value, offset % value.shape[1], 1)


def in_plane(nu_ref, nu_index, ref, index, start):
    nu = nu_ref[nu_index, start : start + ROWS, :]
    v = ref[index, start : start + ROWS, :]
    flux = (nu + turn(nu, -1)) * (v - turn(v, -1))
    total = flux - turn(flux, 1)
    for offset in (-1, 1):
        total = total + (nu + shifted(nu_ref, nu_index, start, offset)) * (
            v - shifted(ref, index, start, offset)
        )
    return nu, v, total


def place():
    slab = lax.axis_index("slab")
    return slab, lax.rem(slab, 2)


def open_kernel(reluctivity, shift, labels, load, potential, far, near, far_potential, held, table, sems):
    _, even = place()
    odd = 1 - even
    total = labels.shape[1]
    moves = (
        (labels.at[even], held.at[0]),
        (labels.at[odd], held.at[1]),
        (load.at[even], far.at[1]),
        (load.at[odd], near.at[1]),
        (potential.at[even], far_potential.at[0]),
        (potential.at[odd], near.at[2]),
        (reluctivity, table),
    )
    copies = [pltpu.make_async_copy(src, dst, sems.at[i]) for i, (src, dst) in enumerate(moves)]
    for copy in copies:
        copy.start()
    copies[-1].wait()
    r0, r1, r2, r3 = (table[i] for i in range(4))
    offset = shift[0]
    for side, out in enumerate((far, near)):
        copies[side].wait()
        for start in range(0, total, ROWS):
            rows = slice(start, start + ROWS)
            material = held[side, rows, :]
            if start < total // 2:
                material = pltpu.roll(material, offset, 1)
            out[0, rows, :] = jnp.where(
                material < 2,
                jnp.where(material == 0, r0, r1),
                jnp.where(material == 2, r2, r3),
            )
    for copy in copies[2:-1]:
        copy.wait()


def part_kernel(far, near, far_part, near_part):
    total = far.shape[1]
    for own, other, out in ((far, near, far_part), (near, far, near_part)):
        for start in range(0, total, ROWS):
            rows = slice(start, start + ROWS)
            nu, v, total_flux = in_plane(own, 0, own, 1, start)
            total_flux = total_flux + (nu + other[0, rows, :]) * (v - other[1, rows, :])
            out[0, rows, :] = 0.5 * (v + total_flux)


def fold(value):
    return jnp.sum(value.reshape(ROWS // 8, 8, value.shape[1]), axis=0)


def sums_kernel(far, near, far_part, near_part, far_in, near_in, far_part_in, near_part_in, image, image_in, sums):
    slab, _ = place()
    count = lax.axis_size("slab")
    total, columns = far.shape[1:]
    beyond = jnp.where((slab > 0) & (slab < count - 1), 1.0, 0.0).astype(jnp.float32)
    sides = ((far, far_part, far_in, far_part_in, beyond), (near, near_part, near_in, near_part_in, None))
    nil = jnp.zeros((8, columns), jnp.float32)
    m0, m1 = nil, nil
    for side, (own, part, halo, part_in, keep) in enumerate(sides):
        for start in range(0, total, ROWS):
            rows = slice(start, start + ROWS)
            v = own[1, rows, :]
            flux = 0.5 * (own[0, rows, :] + halo[0, rows, :]) * (v - halo[1, rows, :])
            y = part[0, rows, :] + flux
            outer = part_in[0, rows, :] - flux
            image[side, rows, :] = y
            image_in[side, rows, :] = outer if keep is None else keep * outer
            m0 = m0 + fold(v * v)
            m1 = m1 + fold(v * y)
    m0 = jnp.sum(m0, keepdims=True)
    m1 = jnp.sum(m1, keepdims=True)
    c = jnp.where(m0 > 0, m1 / m0, 0.0)
    q, s, t = nil, nil, nil
    for side, (own, _, halo, _, _) in enumerate(sides):
        for start in range(0, total, ROWS):
            rows = slice(start, start + ROWS)
            nu, y, total_flux = in_plane(own, 0, image, side, start)
            other = (near, far)[side]
            total_flux = total_flux + (nu + other[0, rows, :]) * (y - image[1 - side, rows, :])
            total_flux = total_flux + (nu + halo[0, rows, :]) * (y - image_in[side, rows, :])
            z = 0.5 * (y + total_flux)
            v = own[1, rows, :]
            w = y - c * v
            u = z - c * y
            q = q + fold(w * w)
            s = s + fold(w * u)
            t = t + fold(v * u)
    here = lax.broadcasted_iota(jnp.int32, sums.shape[1:], 0) == slab
    for index, value in enumerate((m0, m1, q, s, t)):
        value = jnp.sum(value, keepdims=True) if index > 1 else value
        sums[index] = jnp.where(here, value, 0.0)


def finish_kernel(
    sums, far, near, far_in, near_in, image, image_in, potential, far_potential, mask, adjoint, *rest
):
    *terms, mixed, mixed_in = rest
    _, even = place()
    total = far.shape[1]
    m0_d, m1_d, q_d, s_d, t_d = (sums[i] for i in range(SUMS))
    m0 = jnp.sum(m0_d, axis=0, keepdims=True)
    m1 = jnp.sum(m1_d, axis=0, keepdims=True)
    c = m1 / m0
    delta = jnp.where(m0_d > 0, m1_d / m0_d, 0.0) - c
    ww = jnp.sum(q_d + delta * delta * m0_d, axis=0, keepdims=True)
    waw = jnp.sum(s_d + delta * (q_d + t_d) + delta * delta * m1_d, axis=0, keepdims=True)
    alpha0 = m0 / m1
    beta = alpha0 * (ww * alpha0 / m0)
    divisor = waw - ww * (ww / m1)
    alpha1 = jnp.where(divisor == 0, 0.0, ww / divisor)
    a = (alpha0 + alpha1 * (1.0 + beta))[:, 0:1]
    b = (-alpha1 * alpha0)[:, 0:1]
    scale = 0.25 / lax.axis_size("pos")
    sides = ((far, even, far_in, far_potential, 0), (near, 1 - even, near_in, near_in, 2))
    for side, (own, layer, halo, halo_potential, at) in enumerate(sides):
        for start in range(0, total, ROWS):
            rows = slice(start, start + ROWS)
            out = a * own[1, rows, :] + b * image[side, rows, :]
            adjoint[layer, rows, :] = out
            mixed[side, rows, :] = out + 0.5 * potential[layer, rows, :]
            outer = a * halo[1, rows, :] + b * image_in[side, rows, :]
            mixed_in[side, rows, :] = outer + 0.5 * halo_potential[at, rows, :]
    for side, (own, layer, halo, halo_potential, at) in enumerate(sides):
        for start in range(0, total, ROWS):
            rows = slice(start, start + ROWS)
            g = potential[layer, rows, :]
            f = mixed[side, rows, :]
            result = (halo_potential[at, rows, :] - potential[1 - layer, rows, :]) * (
                mixed_in[side, rows, :] - mixed[1 - side, rows, :]
            )
            result = result + (turn(g, -1) - turn(g, 1)) * (turn(f, -1) - turn(f, 1))
            result = result + (
                shifted(potential, layer, start, 1) - shifted(potential, layer, start, -1)
            ) * (shifted(mixed, side, start, 1) - shifted(mixed, side, start, -1))
            weight = mask[layer, rows, :].astype(jnp.float32) * own[0, rows, :]
            span = total // CHUNKS
            terms[start // span][layer, start % span : start % span + ROWS, :] = weight * (scale * result)


def in_hbm(x):
    return pltpu.with_memory_space_constraint(x, pltpu.HBM)


def close_kernel(start, total, arrived, *rest):
    gradient, held, sem = rest[-3:]
    held[...] = total[...] + arrived[...]
    copy = pltpu.make_async_copy(held, gradient.at[:, pl.ds(start, total.shape[1]), :], sem)
    copy.start()
    copy.wait()


def pairs(size, first):
    out = []
    for i in range(first, size - 1, 2):
        out += [(i, i + 1), (i + 1, i)]
    return out


def gather_sums(sums, axis, size):
    if size & (size - 1):
        return lax.psum(sums, axis)
    step = 1
    while step < size:
        sums = sums + lax.ppermute(sums, axis, [(i, i ^ step) for i in range(size)])
        step *= 2
    return sums


def sum_positions(term, positions, slabs):
    if positions & (positions - 1) or positions == 1:
        return lax.psum(term, "pos"), jnp.zeros_like(term)
    bits = positions.bit_length() - 1
    arrived = None
    for step in range(bits):
        term = term if arrived is None else term + arrived
        route = []
        for p in range(positions):
            for s in range(slabs):
                bit = step if s % 2 == 0 else bits - 1 - step
                route.append((p * slabs + s, (p ^ (1 << bit)) * slabs + s))
        arrived = lax.ppermute(term, ("pos", "slab"), route)
    return term, arrived


def local(labels, magnet_mask, reluctivity, rotor_shift, potential, adjoint_load):
    layers, radial, angular = labels.shape
    positions, slabs = lax.axis_size("pos"), lax.axis_size("slab")
    if layers != 2 or slabs % 2 or radial % (2 * CHUNKS * ROWS):
        raise ValueError("unsupported sizes")
    potential, load = potential[0], adjoint_load[0]
    f32 = functools.partial(jax.ShapeDtypeStruct, dtype=jnp.float32)
    plane = (radial, angular)
    vmem = pl.BlockSpec(memory_space=VMEM)
    smem = pl.BlockSpec(memory_space=SMEM)
    hbm = pl.BlockSpec(memory_space=pltpu.HBM)
    far, near, far_potential = pl.pallas_call(
        open_kernel,
        out_shape=tuple(pltpu.VMEM((k,) + plane, jnp.float32) for k in (2, 3, 1)),
        in_specs=[hbm, smem, hbm, hbm, hbm],
        out_specs=(vmem,) * 3,
        scratch_shapes=[
            VMEM((2,) + plane, jnp.int32),
            SMEM(reluctivity.shape, jnp.float32),
            pltpu.SemaphoreType.DMA((7,)),
        ],
        compiler_params=params(),
        name="open",
    )(in_hbm(reluctivity), rotor_shift, in_hbm(labels), in_hbm(load), in_hbm(potential))
    far_in = lax.ppermute(far, "slab", pairs(slabs, 1))
    near_in = lax.ppermute(near, "slab", pairs(slabs, 0))
    far_part, near_part = pl.pallas_call(
        part_kernel,
        out_shape=(pltpu.VMEM((1,) + plane, jnp.float32),) * 2,
        in_specs=[vmem] * 2,
        out_specs=(vmem,) * 2,
        compiler_params=params(),
        name="part",
    )(far, near)
    far_part_in = lax.ppermute(far_part, "slab", pairs(slabs, 1))
    near_part_in = lax.ppermute(near_part, "slab", pairs(slabs, 0))
    far_potential = lax.ppermute(far_potential, "slab", pairs(slabs, 1))
    image, image_in, sums = pl.pallas_call(
        sums_kernel,
        out_shape=(f32((2,) + plane), f32((2,) + plane), f32((SUMS, slabs, 128))),
        in_specs=[vmem] * 8,
        out_specs=(vmem,) * 3,
        compiler_params=params(),
        name="sums",
    )(far, near, far_part, near_part, far_in, near_in, far_part_in, near_part_in)
    sums = gather_sums(sums, "slab", slabs)
    adjoint, *terms = pl.pallas_call(
        finish_kernel,
        out_shape=(pltpu.VMEM((2,) + plane, jnp.float32),)
        + (f32((2, radial // CHUNKS, angular)),) * CHUNKS,
        in_specs=[vmem] * 10,
        out_specs=(vmem,) * (1 + CHUNKS),
        scratch_shapes=[VMEM((2,) + plane, jnp.float32)] * 2,
        compiler_params=params(),
        name="finish",
    )(sums, far, near, far_in, near_in, image, image_in, potential, far_potential, magnet_mask)
    span = radial // CHUNKS
    gradient = ()
    for index, (total, arrived) in enumerate([sum_positions(term, positions, slabs) for term in terms]):
        gradient = pl.pallas_call(
            functools.partial(close_kernel, index * span),
            out_shape=pltpu.HBM((2,) + plane, jnp.float32),
            in_specs=[vmem] * 2 + [hbm] * (index > 0),
            out_specs=hbm,
            scratch_shapes=[VMEM((2, span, angular), jnp.float32), pltpu.SemaphoreType.DMA(())],
            input_output_aliases={2: 0} if index else {},
            compiler_params=params(),
            name="close",
        )(total, arrived, *((gradient,) if index else ()))
    return gradient, adjoint[None]


def solution(mesh):
    return jax.shard_map(
        local,
        mesh=mesh,
        in_specs=(
            P("slab", None, None),
            P("slab", None, None),
            P(),
            P("pos"),
            P("pos", "slab", None, None),
            P("pos", "slab", None, None),
        ),
        out_specs=(P("slab", None, None), P("pos", "slab", None, None)),
        check_vma=False,
    )
```

```python
import functools

import jax
import jax.numpy as jnp
from jax import lax
from jax.experimental import pallas as pl
from jax.experimental.pallas import tpu as pltpu
from jax.sharding import PartitionSpec as P


ROWS = 16
VMEM = pltpu.VMEM
SMEM = pltpu.SMEM
SUMS = 5
CHUNKS = 2


def params():
    return pltpu.CompilerParams(vmem_limit_bytes=40 * 1024 * 1024)


def shifted(ref, index, start, offset):
    total, columns = ref.shape[-2:]
    zero = jnp.zeros((1, columns), jnp.float32)
    if start + offset < 0:
        return jnp.concatenate([zero, ref[index, 0 : ROWS - 1, :]], axis=0)
    if start + offset + ROWS > total:
        return jnp.concatenate([ref[index, start + 1 : total, :], zero], axis=0)
    return ref[index, start + offset : start + offset + ROWS, :]


def turn(value, offset):
    return pltpu.roll(value, offset % value.shape[1], 1)


def in_plane(nu_ref, nu_index, ref, index, start):
    nu = nu_ref[nu_index, start : start + ROWS, :]
    v = ref[index, start : start + ROWS, :]
    flux = (nu + turn(nu, -1)) * (v - turn(v, -1))
    total = flux - turn(flux, 1)
    for offset in (-1, 1):
        total = total + (nu + shifted(nu_ref, nu_index, start, offset)) * (
            v - shifted(ref, index, start, offset)
        )
    return nu, v, total


def place():
    slab = lax.axis_index("slab")
    return slab, lax.rem(slab, 2)


def open_kernel(reluctivity, shift, labels, load, potential, far, near, far_potential, held, table, sems):
    _, even = place()
    odd = 1 - even
    total = labels.shape[1]
    moves = (
        (labels.at[even], held.at[0]),
        (labels.at[odd], held.at[1]),
        (load.at[even], far.at[1]),
        (load.at[odd], near.at[1]),
        (potential.at[even], far_potential.at[0]),
        (potential.at[odd], near.at[2]),
        (reluctivity, table),
    )
    copies = [pltpu.make_async_copy(src, dst, sems.at[i]) for i, (src, dst) in enumerate(moves)]
    for copy in copies:
        copy.start()
    copies[-1].wait()
    r0, r1, r2, r3 = (table[i] for i in range(4))
    offset = shift[0]
    for side, out in enumerate((far, near)):
        copies[side].wait()
        for start in range(0, total, ROWS):
            rows = slice(start, start + ROWS)
            material = held[side, rows, :]
            if start < total // 2:
                material = pltpu.roll(material, offset, 1)
            out[0, rows, :] = jnp.where(
                material < 2,
                jnp.where(material == 0, r0, r1),
                jnp.where(material == 2, r2, r3),
            )
    for copy in copies[2:-1]:
        copy.wait()


def part_kernel(far, near, far_part, near_part):
    total = far.shape[1]
    for own, other, out in ((far, near, far_part), (near, far, near_part)):
        for start in range(0, total, ROWS):
            rows = slice(start, start + ROWS)
            nu, v, total_flux = in_plane(own, 0, own, 1, start)
            total_flux = total_flux + (nu + other[0, rows, :]) * (v - other[1, rows, :])
            out[0, rows, :] = 0.5 * (v + total_flux)


def fold(value):
    return jnp.sum(value.reshape(ROWS // 8, 8, value.shape[1]), axis=0)


def sums_kernel(far, near, far_part, near_part, far_in, near_in, near_part_in, image, near_image_in, sums):
    total, columns = far.shape[1:]
    sides = ((far, far_part, far_in), (near, near_part, near_in))
    nil = jnp.zeros((8, columns), jnp.float32)
    m0, m1 = nil, nil
    for side, (own, part, halo) in enumerate(sides):
        for start in range(0, total, ROWS):
            rows = slice(start, start + ROWS)
            v = own[1, rows, :]
            flux = 0.5 * (own[0, rows, :] + halo[0, rows, :]) * (v - halo[1, rows, :])
            y = part[0, rows, :] + flux
            image[side, rows, :] = y
            if own is near:
                near_image_in[0, rows, :] = near_part_in[0, rows, :] - flux
            m0 = m0 + fold(v * v)
            m1 = m1 + fold(v * y)
    m0 = jnp.sum(m0, keepdims=True)
    m1 = jnp.sum(m1, keepdims=True)
    c = jnp.where(m0 > 0, m1 / m0, 0.0)
    q, s, t = nil, nil, nil
    for side, (own, _, halo) in enumerate(sides):
        for start in range(0, total, ROWS):
            rows = slice(start, start + ROWS)
            nu, y, total_flux = in_plane(own, 0, image, side, start)
            other = (near, far)[side]
            total_flux = total_flux + (nu + other[0, rows, :]) * (y - image[1 - side, rows, :])
            if own is near:
                total_flux = total_flux + (nu + halo[0, rows, :]) * (y - near_image_in[0, rows, :])
            z = 0.5 * (y + total_flux)
            v = own[1, rows, :]
            w = y - c * v
            u = z - c * y
            q = q + fold(w * w)
            s = s + fold(w * u)
            t = t + fold(v * u)
    for index, value in enumerate((m0, m1, q, s, t, c)):
        value = jnp.sum(value, keepdims=True) if value.shape[0] > 1 else value
        sums[index : index + 1, :] = jnp.broadcast_to(value, (1, sums.shape[1]))


def face_kernel(far, far_in, far_part_in, image, own_sums, far_image_in, sums):
    slab, _ = place()
    count = lax.axis_size("slab")
    total, columns = far.shape[1:]
    beyond = jnp.where((slab > 0) & (slab < count - 1), 1.0, 0.0).astype(jnp.float32)
    c = own_sums[SUMS : SUMS + 1, 0:1]
    s = jnp.zeros((8, columns), jnp.float32)
    t = s
    for start in range(0, total, ROWS):
        rows = slice(start, start + ROWS)
        v = far[1, rows, :]
        y = image[0, rows, :]
        weight = 0.5 * (far[0, rows, :] + far_in[0, rows, :])
        outer = beyond * (far_part_in[0, rows, :] - weight * (v - far_in[1, rows, :]))
        far_image_in[0, rows, :] = outer
        flux = weight * (y - outer)
        s = s + fold((y - c * v) * flux)
        t = t + fold(v * flux)
    here = lax.broadcasted_iota(jnp.int32, sums.shape[1:], 0) == slab
    added = (None, None, None, s, t)
    for index in range(SUMS):
        value = own_sums[index : index + 1, :]
        if added[index] is not None:
            value = value + jnp.sum(added[index], keepdims=True)
        sums[index] = jnp.where(here, value, 0.0)


def finish_kernel(
    sums, far, near, far_in, near_in, image, far_image_in, near_image_in, potential, far_potential, mask, adjoint, *rest
):
    *pieces, mixed, mixed_in, term = rest
    _, even = place()
    total = far.shape[1]
    m0_d, m1_d, q_d, s_d, t_d = (sums[i] for i in range(SUMS))
    m0 = jnp.sum(m0_d, axis=0, keepdims=True)
    m1 = jnp.sum(m1_d, axis=0, keepdims=True)
    c = m1 / m0
    delta = jnp.where(m0_d > 0, m1_d / m0_d, 0.0) - c
    ww = jnp.sum(q_d + delta * delta * m0_d, axis=0, keepdims=True)
    waw = jnp.sum(s_d + delta * (q_d + t_d) + delta * delta * m1_d, axis=0, keepdims=True)
    alpha0 = m0 / m1
    beta = alpha0 * (ww * alpha0 / m0)
    divisor = waw - ww * (ww / m1)
    alpha1 = jnp.where(divisor == 0, 0.0, ww / divisor)
    a = (alpha0 + alpha1 * (1.0 + beta))[:, 0:1]
    b = (-alpha1 * alpha0)[:, 0:1]
    scale = 0.25 / lax.axis_size("pos")
    sides = ((far, even, far_in, far_image_in, far_potential, 0), (near, 1 - even, near_in, near_image_in, near_in, 2))
    for side, (own, layer, halo, image_in, halo_potential, at) in enumerate(sides):
        for start in range(0, total, ROWS):
            rows = slice(start, start + ROWS)
            out = a * own[1, rows, :] + b * image[side, rows, :]
            adjoint[layer, rows, :] = out
            mixed[side, rows, :] = out + 0.5 * potential[layer, rows, :]
            outer = a * halo[1, rows, :] + b * image_in[0, rows, :]
            mixed_in[side, rows, :] = outer + 0.5 * halo_potential[at, rows, :]
    for side, (own, layer, halo, image_in, halo_potential, at) in enumerate(sides):
        for start in range(0, total, ROWS):
            rows = slice(start, start + ROWS)
            g = potential[layer, rows, :]
            f = mixed[side, rows, :]
            result = (halo_potential[at, rows, :] - potential[1 - layer, rows, :]) * (
                mixed_in[side, rows, :] - mixed[1 - side, rows, :]
            )
            result = result + (turn(g, -1) - turn(g, 1)) * (turn(f, -1) - turn(f, 1))
            result = result + (
                shifted(potential, layer, start, 1) - shifted(potential, layer, start, -1)
            ) * (shifted(mixed, side, start, 1) - shifted(mixed, side, start, -1))
            weight = mask[layer, rows, :].astype(jnp.float32) * own[0, rows, :]
            term[layer, rows, :] = weight * (scale * result)
    first = own_half()
    span = pieces[0].shape[1]
    for index, piece in enumerate(pieces):
        half = first if index < CHUNKS else 1 - first
        base = pl.multiple_of(half * (total // 2) + index % CHUNKS * span, 8)
        for layer in range(2):
            piece[layer] = term[layer, pl.ds(base, span), :]


def in_hbm(x):
    return pltpu.with_memory_space_constraint(x, pltpu.HBM)


def own_half():
    bits = lax.axis_size("pos").bit_length() - 1
    position = lax.axis_index("pos")
    _, even = place()
    return jnp.where(even == 0, lax.rem(position, 2), lax.rem(lax.div(position, 2 ** (bits - 1)), 2))


def close_kernel(given, first_chunk, *rest):
    gradient, sems = rest[-2:]
    count = sems.shape[0]
    span = rest[0].shape[1]
    half = 1 - own_half() if given else own_half()
    copies = []
    for index in range(count):
        base = pl.multiple_of(half * (gradient.shape[1] // 2) + (first_chunk + index) * span, 8)
        copies.append(pltpu.make_async_copy(rest[index], gradient.at[:, pl.ds(base, span), :], sems.at[index]))
    for copy in copies:
        copy.start()
    for copy in copies:
        copy.wait()


def pairs(size, first):
    out = []
    for i in range(first, size - 1, 2):
        out += [(i, i + 1), (i + 1, i)]
    return out


def gather_sums(sums, axis, size):
    if size & (size - 1):
        return lax.psum(sums, axis)
    step = 1
    while step < size:
        sums = sums + lax.ppermute(sums, axis, [(i, i ^ step) for i in range(size)])
        step *= 2
    return sums


def partners(step, positions, slabs):
    bits = positions.bit_length() - 1
    route = []
    for p in range(positions):
        for s in range(slabs):
            bit = step if s % 2 == 0 else bits - 1 - step
            route.append((p * slabs + s, (p ^ (1 << bit)) * slabs + s))
    return route


def sum_positions(keep, give, positions, slabs):
    bits = positions.bit_length() - 1
    total = keep + lax.ppermute(give, ("pos", "slab"), partners(0, positions, slabs))
    for step in range(1, bits):
        total = total + lax.ppermute(total, ("pos", "slab"), partners(step, positions, slabs))
    return total, lax.ppermute(total, ("pos", "slab"), partners(0, positions, slabs))


def local(labels, magnet_mask, reluctivity, rotor_shift, potential, adjoint_load):
    layers, radial, angular = labels.shape
    positions, slabs = lax.axis_size("pos"), lax.axis_size("slab")
    if layers != 2 or slabs % 2 or radial % (2 * CHUNKS * ROWS) or positions < 2 or positions & (positions - 1):
        raise ValueError("unsupported sizes")
    potential, load = potential[0], adjoint_load[0]
    f32 = functools.partial(jax.ShapeDtypeStruct, dtype=jnp.float32)
    plane = (radial, angular)
    vmem = pl.BlockSpec(memory_space=VMEM)
    smem = pl.BlockSpec(memory_space=SMEM)
    hbm = pl.BlockSpec(memory_space=pltpu.HBM)
    far, near, far_potential = pl.pallas_call(
        open_kernel,
        out_shape=tuple(pltpu.VMEM((k,) + plane, jnp.float32) for k in (2, 3, 1)),
        in_specs=[hbm, smem, hbm, hbm, hbm],
        out_specs=(vmem,) * 3,
        scratch_shapes=[
            VMEM((2,) + plane, jnp.int32),
            SMEM(reluctivity.shape, jnp.float32),
            pltpu.SemaphoreType.DMA((7,)),
        ],
        compiler_params=params(),
        name="open",
    )(in_hbm(reluctivity), rotor_shift, in_hbm(labels), in_hbm(load), in_hbm(potential))
    far_in = lax.ppermute(far, "slab", pairs(slabs, 1))
    near_in = lax.ppermute(near, "slab", pairs(slabs, 0))
    far_part, near_part = pl.pallas_call(
        part_kernel,
        out_shape=(pltpu.VMEM((1,) + plane, jnp.float32),) * 2,
        in_specs=[vmem] * 2,
        out_specs=(vmem,) * 2,
        compiler_params=params(),
        name="part",
    )(far, near)
    far_part_in = lax.ppermute(far_part, "slab", pairs(slabs, 1))
    near_part_in = lax.ppermute(near_part, "slab", pairs(slabs, 0))
    far_potential = lax.ppermute(far_potential, "slab", pairs(slabs, 1))
    image, near_image_in, own_sums = pl.pallas_call(
        sums_kernel,
        out_shape=(f32((2,) + plane), f32((1,) + plane), f32((8, 128))),
        in_specs=[vmem] * 7,
        out_specs=(vmem,) * 3,
        compiler_params=params(),
        name="sums",
    )(far, near, far_part, near_part, far_in, near_in, near_part_in)
    far_image_in, sums = pl.pallas_call(
        face_kernel,
        out_shape=(f32((1,) + plane), f32((SUMS, slabs, 128))),
        in_specs=[vmem] * 5,
        out_specs=(vmem,) * 2,
        compiler_params=params(),
        name="face",
    )(far, far_in, far_part_in, image, own_sums)
    sums = gather_sums(sums, "slab", slabs)
    span = radial // 2 // CHUNKS
    adjoint, *pieces = pl.pallas_call(
        finish_kernel,
        out_shape=(pltpu.VMEM((2,) + plane, jnp.float32),) + (f32((2, span, angular)),) * (2 * CHUNKS),
        in_specs=[vmem] * 11,
        out_specs=(vmem,) * (1 + 2 * CHUNKS),
        scratch_shapes=[VMEM((2,) + plane, jnp.float32)] * 3,
        compiler_params=params(),
        name="finish",
    )(sums, far, near, far_in, near_in, image, far_image_in, near_image_in, potential, far_potential, magnet_mask)
    halves = [sum_positions(pieces[i], pieces[CHUNKS + i], positions, slabs) for i in range(CHUNKS)]
    gradient = ()
    for given, first_chunk, chunks in (
        (False, 0, [kept for kept, _ in halves]),
        *((True, i, [given]) for i, (_, given) in enumerate(halves)),
    ):
        gradient = pl.pallas_call(
            functools.partial(close_kernel, given, first_chunk),
            out_shape=pltpu.HBM((2,) + plane, jnp.float32),
            in_specs=[vmem] * len(chunks) + [hbm] * given,
            out_specs=hbm,
            scratch_shapes=[pltpu.SemaphoreType.DMA((len(chunks),))],
            input_output_aliases={len(chunks): 0} if given else {},
            compiler_params=params(),
            name="close",
        )(*chunks, *((gradient,) if given else ()))
    return gradient, adjoint[None]


def solution(mesh):
    return jax.shard_map(
        local,
        mesh=mesh,
        in_specs=(
            P("slab", None, None),
            P("slab", None, None),
            P(),
            P("pos"),
            P("pos", "slab", None, None),
            P("pos", "slab", None, None),
        ),
        out_specs=(P("slab", None, None), P("pos", "slab", None, None)),
        check_vma=False,
    )
```

```python
import functools

import jax
import jax.numpy as jnp
from jax import lax
from jax.experimental import pallas as pl
from jax.experimental.pallas import tpu as pltpu
from jax.sharding import PartitionSpec as P


ROWS = 16
VMEM = pltpu.VMEM
SMEM = pltpu.SMEM
SUMS = 5
EIGHTHS = (3, 3, 2)


def params():
    return pltpu.CompilerParams(vmem_limit_bytes=40 * 1024 * 1024)


def shifted(ref, index, start, offset):
    total, columns = ref.shape[-2:]
    zero = jnp.zeros((1, columns), jnp.float32)
    if start + offset < 0:
        return jnp.concatenate([zero, ref[index, 0 : ROWS - 1, :]], axis=0)
    if start + offset + ROWS > total:
        return jnp.concatenate([ref[index, start + 1 : total, :], zero], axis=0)
    return ref[index, start + offset : start + offset + ROWS, :]


def turn(value, offset):
    return pltpu.roll(value, offset % value.shape[1], 1)


def in_plane(nu_ref, nu_index, ref, index, start):
    nu = nu_ref[nu_index, start : start + ROWS, :]
    v = ref[index, start : start + ROWS, :]
    flux = (nu + turn(nu, -1)) * (v - turn(v, -1))
    total = flux - turn(flux, 1)
    for offset in (-1, 1):
        total = total + (nu + shifted(nu_ref, nu_index, start, offset)) * (
            v - shifted(ref, index, start, offset)
        )
    return nu, v, total


def place():
    slab = lax.axis_index("slab")
    return slab, lax.rem(slab, 2)


def open_kernel(reluctivity, shift, labels, load, potential, far, near, far_potential, held, table, sems):
    _, even = place()
    odd = 1 - even
    total = labels.shape[1]
    moves = (
        (labels.at[even], held.at[0]),
        (labels.at[odd], held.at[1]),
        (load.at[even], far.at[1]),
        (load.at[odd], near.at[1]),
        (potential.at[even], far_potential.at[0]),
        (potential.at[odd], near.at[2]),
        (reluctivity, table),
    )
    copies = [pltpu.make_async_copy(src, dst, sems.at[i]) for i, (src, dst) in enumerate(moves)]
    for copy in copies:
        copy.start()
    copies[-1].wait()
    r0, r1, r2, r3 = (table[i] for i in range(4))
    offset = shift[0]
    for side, out in enumerate((far, near)):
        copies[side].wait()
        for start in range(0, total, ROWS):
            rows = slice(start, start + ROWS)
            material = held[side, rows, :]
            if start < total // 2:
                material = pltpu.roll(material, offset, 1)
            out[0, rows, :] = jnp.where(
                material < 2,
                jnp.where(material == 0, r0, r1),
                jnp.where(material == 2, r2, r3),
            )
    for copy in copies[2:-1]:
        copy.wait()


def part_kernel(far, near, far_part, near_part):
    total = far.shape[1]
    for own, other, out in ((far, near, far_part), (near, far, near_part)):
        for start in range(0, total, ROWS):
            rows = slice(start, start + ROWS)
            nu, v, total_flux = in_plane(own, 0, own, 1, start)
            total_flux = total_flux + (nu + other[0, rows, :]) * (v - other[1, rows, :])
            out[0, rows, :] = 0.5 * (v + total_flux)


def fold(value):
    return jnp.sum(value.reshape(ROWS // 8, 8, value.shape[1]), axis=0)


def sums_kernel(far, near, far_part, near_part, far_in, near_in, near_part_in, image, near_image_in, sums):
    total, columns = far.shape[1:]
    sides = ((far, far_part, far_in), (near, near_part, near_in))
    nil = jnp.zeros((8, columns), jnp.float32)
    m0, m1 = nil, nil
    for side, (own, part, halo) in enumerate(sides):
        for start in range(0, total, ROWS):
            rows = slice(start, start + ROWS)
            v = own[1, rows, :]
            flux = 0.5 * (own[0, rows, :] + halo[0, rows, :]) * (v - halo[1, rows, :])
            y = part[0, rows, :] + flux
            image[side, rows, :] = y
            if own is near:
                near_image_in[0, rows, :] = near_part_in[0, rows, :] - flux
            m0 = m0 + fold(v * v)
            m1 = m1 + fold(v * y)
    m0 = jnp.sum(m0, keepdims=True)
    m1 = jnp.sum(m1, keepdims=True)
    c = jnp.where(m0 > 0, m1 / m0, 0.0)
    q, s, t = nil, nil, nil
    for side, (own, _, halo) in enumerate(sides):
        for start in range(0, total, ROWS):
            rows = slice(start, start + ROWS)
            nu, y, total_flux = in_plane(own, 0, image, side, start)
            other = (near, far)[side]
            total_flux = total_flux + (nu + other[0, rows, :]) * (y - image[1 - side, rows, :])
            if own is near:
                total_flux = total_flux + (nu + halo[0, rows, :]) * (y - near_image_in[0, rows, :])
            z = 0.5 * (y + total_flux)
            v = own[1, rows, :]
            w = y - c * v
            u = z - c * y
            q = q + fold(w * w)
            s = s + fold(w * u)
            t = t + fold(v * u)
    for index, value in enumerate((m0, m1, q, s, t, c)):
        value = jnp.sum(value, keepdims=True) if value.shape[0] > 1 else value
        sums[index : index + 1, :] = jnp.broadcast_to(value, (1, sums.shape[1]))


def face_kernel(far, far_in, far_part_in, image, own_sums, far_image_in, sums):
    slab, _ = place()
    count = lax.axis_size("slab")
    total, columns = far.shape[1:]
    beyond = jnp.where((slab > 0) & (slab < count - 1), 1.0, 0.0).astype(jnp.float32)
    c = own_sums[SUMS : SUMS + 1, 0:1]
    s = jnp.zeros((8, columns), jnp.float32)
    t = s
    for start in range(0, total, ROWS):
        rows = slice(start, start + ROWS)
        v = far[1, rows, :]
        y = image[0, rows, :]
        weight = 0.5 * (far[0, rows, :] + far_in[0, rows, :])
        outer = beyond * (far_part_in[0, rows, :] - weight * (v - far_in[1, rows, :]))
        far_image_in[0, rows, :] = outer
        flux = weight * (y - outer)
        s = s + fold((y - c * v) * flux)
        t = t + fold(v * flux)
    here = lax.broadcasted_iota(jnp.int32, sums.shape[1:], 0) == slab
    added = (None, None, None, s, t)
    for index in range(SUMS):
        value = own_sums[index : index + 1, :]
        if added[index] is not None:
            value = value + jnp.sum(added[index], keepdims=True)
        sums[index] = jnp.where(here, value, 0.0)


def finish_kernel(
    sums_odd, sums_in, far, near, far_in, near_in, image, far_image_in, near_image_in, potential, far_potential, mask, adjoint, *rest
):
    *terms, mixed, mixed_in = rest
    _, even = place()
    total = far.shape[1]
    odd = even.astype(jnp.float32)
    m0_d, m1_d, q_d, s_d, t_d = (odd * sums_odd[i] + sums_in[i] for i in range(SUMS))
    m0 = jnp.sum(m0_d, axis=0, keepdims=True)
    m1 = jnp.sum(m1_d, axis=0, keepdims=True)
    c = m1 / m0
    delta = jnp.where(m0_d > 0, m1_d / m0_d, 0.0) - c
    ww = jnp.sum(q_d + delta * delta * m0_d, axis=0, keepdims=True)
    waw = jnp.sum(s_d + delta * (q_d + t_d) + delta * delta * m1_d, axis=0, keepdims=True)
    alpha0 = m0 / m1
    beta = alpha0 * (ww * alpha0 / m0)
    divisor = waw - ww * (ww / m1)
    alpha1 = jnp.where(divisor == 0, 0.0, ww / divisor)
    a = (alpha0 + alpha1 * (1.0 + beta))[:, 0:1]
    b = (-alpha1 * alpha0)[:, 0:1]
    scale = 0.25 / lax.axis_size("pos")
    firsts = first_rows(total)
    sides = ((far, even, far_in, far_image_in, far_potential, 0), (near, 1 - even, near_in, near_image_in, near_in, 2))
    for side, (own, layer, halo, image_in, halo_potential, at) in enumerate(sides):
        for start in range(0, total, ROWS):
            rows = slice(start, start + ROWS)
            out = a * own[1, rows, :] + b * image[side, rows, :]
            adjoint[layer, rows, :] = out
            mixed[side, rows, :] = out + 0.5 * potential[layer, rows, :]
            outer = a * halo[1, rows, :] + b * image_in[0, rows, :]
            mixed_in[side, rows, :] = outer + 0.5 * halo_potential[at, rows, :]
    for side, (own, layer, halo, image_in, halo_potential, at) in enumerate(sides):
        for start in range(0, total, ROWS):
            rows = slice(start, start + ROWS)
            g = potential[layer, rows, :]
            f = mixed[side, rows, :]
            result = (halo_potential[at, rows, :] - potential[1 - layer, rows, :]) * (
                mixed_in[side, rows, :] - mixed[1 - side, rows, :]
            )
            result = result + (turn(g, -1) - turn(g, 1)) * (turn(f, -1) - turn(f, 1))
            result = result + (
                shifted(potential, layer, start, 1) - shifted(potential, layer, start, -1)
            ) * (shifted(mixed, side, start, 1) - shifted(mixed, side, start, -1))
            weight = mask[layer, rows, :].astype(jnp.float32) * own[0, rows, :]
            index = max(i for i, first in enumerate(firsts) if first <= start)
            at_row = start - firsts[index]
            terms[index][layer, at_row : at_row + ROWS, :] = weight * (scale * result)


def in_hbm(x):
    return pltpu.with_memory_space_constraint(x, pltpu.HBM)


def first_rows(total):
    return [total // 8 * sum(EIGHTHS[:i]) for i in range(len(EIGHTHS))]


def close_kernel(start, total, arrived, *rest):
    gradient, held, sem = rest[-3:]
    held[...] = total[...] + arrived[...]
    copy = pltpu.make_async_copy(held, gradient.at[:, pl.ds(start, total.shape[1]), :], sem)
    copy.start()
    copy.wait()


def pairs(size, first):
    out = []
    for i in range(first, size - 1, 2):
        out += [(i, i + 1), (i + 1, i)]
    return out


def gather_sums(sums, slabs):
    chip = range(0, slabs, 2)
    sums = sums + lax.ppermute(sums, "slab", [(i, i + 1) for i in chip])
    step = 2
    while step < slabs:
        sums = sums + lax.ppermute(sums, "slab", [(i + 1, (i + 1) ^ step) for i in chip])
        step *= 2
    return sums, lax.ppermute(sums, "slab", [(i + 1, i) for i in chip])


def partners(step, positions, slabs):
    bits = positions.bit_length() - 1
    route = []
    for p in range(positions):
        for s in range(slabs):
            bit = step if s % 2 == 0 else bits - 1 - step
            route.append((p * slabs + s, (p ^ (1 << bit)) * slabs + s))
    return route


def sum_positions(term, positions, slabs):
    arrived = lax.ppermute(term, ("pos", "slab"), partners(0, positions, slabs))
    for step in range(1, positions.bit_length() - 1):
        term = term + arrived
        arrived = lax.ppermute(term, ("pos", "slab"), partners(step, positions, slabs))
    return term, arrived


def local(labels, magnet_mask, reluctivity, rotor_shift, potential, adjoint_load):
    layers, radial, angular = labels.shape
    positions, slabs = lax.axis_size("pos"), lax.axis_size("slab")
    if layers != 2 or slabs % 2 or slabs & (slabs - 1) or radial % (8 * ROWS) or positions < 2 or positions & (positions - 1):
        raise ValueError("unsupported sizes")
    potential, load = potential[0], adjoint_load[0]
    f32 = functools.partial(jax.ShapeDtypeStruct, dtype=jnp.float32)
    plane = (radial, angular)
    vmem = pl.BlockSpec(memory_space=VMEM)
    smem = pl.BlockSpec(memory_space=SMEM)
    hbm = pl.BlockSpec(memory_space=pltpu.HBM)
    far, near, far_potential = pl.pallas_call(
        open_kernel,
        out_shape=tuple(pltpu.VMEM((k,) + plane, jnp.float32) for k in (2, 3, 1)),
        in_specs=[hbm, smem, hbm, hbm, hbm],
        out_specs=(vmem,) * 3,
        scratch_shapes=[
            VMEM((2,) + plane, jnp.int32),
            SMEM(reluctivity.shape, jnp.float32),
            pltpu.SemaphoreType.DMA((7,)),
        ],
        compiler_params=params(),
        name="open",
    )(in_hbm(reluctivity), rotor_shift, in_hbm(labels), in_hbm(load), in_hbm(potential))
    far_in = lax.ppermute(far, "slab", pairs(slabs, 1))
    near_in = lax.ppermute(near, "slab", pairs(slabs, 0))
    far_part, near_part = pl.pallas_call(
        part_kernel,
        out_shape=(pltpu.VMEM((1,) + plane, jnp.float32),) * 2,
        in_specs=[vmem] * 2,
        out_specs=(vmem,) * 2,
        compiler_params=params(),
        name="part",
    )(far, near)
    far_part_in = lax.ppermute(far_part, "slab", pairs(slabs, 1))
    near_part_in = lax.ppermute(near_part, "slab", pairs(slabs, 0))
    far_potential = lax.ppermute(far_potential, "slab", pairs(slabs, 1))
    image, near_image_in, own_sums = pl.pallas_call(
        sums_kernel,
        out_shape=(f32((2,) + plane), f32((1,) + plane), f32((8, 128))),
        in_specs=[vmem] * 7,
        out_specs=(vmem,) * 3,
        compiler_params=params(),
        name="sums",
    )(far, near, far_part, near_part, far_in, near_in, near_part_in)
    far_image_in, sums = pl.pallas_call(
        face_kernel,
        out_shape=(f32((1,) + plane), f32((SUMS, slabs, 128))),
        in_specs=[vmem] * 5,
        out_specs=(vmem,) * 2,
        compiler_params=params(),
        name="face",
    )(far, far_in, far_part_in, image, own_sums)
    sums_odd, sums_in = gather_sums(sums, slabs)
    spans = [radial // 8 * k for k in EIGHTHS]
    adjoint, *terms = pl.pallas_call(
        finish_kernel,
        out_shape=(pltpu.VMEM((2,) + plane, jnp.float32),) + tuple(f32((2, span, angular)) for span in spans),
        in_specs=[vmem] * 12,
        out_specs=(vmem,) * (1 + len(spans)),
        scratch_shapes=[VMEM((2,) + plane, jnp.float32)] * 2,
        compiler_params=params(),
        name="finish",
    )(sums_odd, sums_in, far, near, far_in, near_in, image, far_image_in, near_image_in, potential, far_potential, magnet_mask)
    gradient = ()
    for index, term in enumerate(terms):
        total, arrived = sum_positions(term, positions, slabs)
        gradient = pl.pallas_call(
            functools.partial(close_kernel, first_rows(radial)[index]),
            out_shape=pltpu.HBM((2,) + plane, jnp.float32),
            in_specs=[vmem] * 2 + [hbm] * (index > 0),
            out_specs=hbm,
            scratch_shapes=[VMEM(term.shape, jnp.float32), pltpu.SemaphoreType.DMA(())],
            input_output_aliases={2: 0} if index else {},
            compiler_params=params(),
            name="close",
        )(total, arrived, *((gradient,) if index else ()))
    return gradient, adjoint[None]


def solution(mesh):
    return jax.shard_map(
        local,
        mesh=mesh,
        in_specs=(
            P("slab", None, None),
            P("slab", None, None),
            P(),
            P("pos"),
            P("pos", "slab", None, None),
            P("pos", "slab", None, None),
        ),
        out_specs=(P("slab", None, None), P("pos", "slab", None, None)),
        check_vma=False,
    )
```

```python
import functools

import jax
import jax.numpy as jnp
from jax import lax
from jax.experimental import pallas as pl
from jax.experimental.pallas import tpu as pltpu
from jax.sharding import PartitionSpec as P


ROWS = 16
VMEM = pltpu.VMEM
SMEM = pltpu.SMEM
SUMS = 5
EIGHTHS = (3, 3, 2)


def params():
    return pltpu.CompilerParams(vmem_limit_bytes=40 * 1024 * 1024)


def shifted(ref, index, start, offset):
    total, columns = ref.shape[-2:]
    zero = jnp.zeros((1, columns), jnp.float32)
    if start + offset < 0:
        return jnp.concatenate([zero, ref[index, 0 : ROWS - 1, :]], axis=0)
    if start + offset + ROWS > total:
        return jnp.concatenate([ref[index, start + 1 : total, :], zero], axis=0)
    return ref[index, start + offset : start + offset + ROWS, :]


def turn(value, offset):
    return pltpu.roll(value, offset % value.shape[1], 1)


def in_plane(nu_ref, nu_index, ref, index, start):
    nu = nu_ref[nu_index, start : start + ROWS, :]
    v = ref[index, start : start + ROWS, :]
    flux = (nu + turn(nu, -1)) * (v - turn(v, -1))
    total = flux - turn(flux, 1)
    for offset in (-1, 1):
        total = total + (nu + shifted(nu_ref, nu_index, start, offset)) * (
            v - shifted(ref, index, start, offset)
        )
    return nu, v, total


def place():
    slab = lax.axis_index("slab")
    return slab, lax.rem(slab, 2)


def open_kernel(reluctivity, shift, labels, load, potential, far, near, far_potential, held, table, sems):
    _, even = place()
    odd = 1 - even
    total = labels.shape[1]
    moves = (
        (labels.at[even], held.at[0]),
        (labels.at[odd], held.at[1]),
        (load.at[even], far.at[1]),
        (load.at[odd], near.at[1]),
        (potential.at[even], far_potential.at[0]),
        (potential.at[odd], near.at[2]),
        (reluctivity, table),
    )
    copies = [pltpu.make_async_copy(src, dst, sems.at[i]) for i, (src, dst) in enumerate(moves)]
    for copy in copies:
        copy.start()
    copies[-1].wait()
    r0, r1, r2, r3 = (table[i] for i in range(4))
    offset = shift[0]
    for side, out in enumerate((far, near)):
        copies[side].wait()
        for start in range(0, total, ROWS):
            rows = slice(start, start + ROWS)
            material = held[side, rows, :]
            if start < total // 2:
                material = pltpu.roll(material, offset, 1)
            out[0, rows, :] = jnp.where(
                material < 2,
                jnp.where(material == 0, r0, r1),
                jnp.where(material == 2, r2, r3),
            )
    for copy in copies[2:-1]:
        copy.wait()


def part_kernel(far, near, far_part, near_part):
    total = far.shape[1]
    for own, other, out in ((far, near, far_part), (near, far, near_part)):
        for start in range(0, total, ROWS):
            rows = slice(start, start + ROWS)
            nu, v, total_flux = in_plane(own, 0, own, 1, start)
            total_flux = total_flux + (nu + other[0, rows, :]) * (v - other[1, rows, :])
            out[0, rows, :] = 0.5 * (v + total_flux)


def fold(value):
    return jnp.sum(value.reshape(ROWS // 8, 8, value.shape[1]), axis=0)


def sums_kernel(far, near, far_part, near_part, far_in, near_in, near_part_in, image, near_image_in, sums):
    total, columns = far.shape[1:]
    sides = ((far, far_part, far_in), (near, near_part, near_in))
    nil = jnp.zeros((8, columns), jnp.float32)
    m0, m1 = nil, nil
    for side, (own, part, halo) in enumerate(sides):
        for start in range(0, total, ROWS):
            rows = slice(start, start + ROWS)
            v = own[1, rows, :]
            flux = 0.5 * (own[0, rows, :] + halo[0, rows, :]) * (v - halo[1, rows, :])
            y = part[0, rows, :] + flux
            image[side, rows, :] = y
            if own is near:
                near_image_in[0, rows, :] = near_part_in[0, rows, :] - flux
            m0 = m0 + fold(v * v)
            m1 = m1 + fold(v * y)
    m0 = jnp.sum(m0, keepdims=True)
    m1 = jnp.sum(m1, keepdims=True)
    c = jnp.where(m0 > 0, m1 / m0, 0.0)
    q, s, t = nil, nil, nil
    for side, (own, _, halo) in enumerate(sides):
        for start in range(0, total, ROWS):
            rows = slice(start, start + ROWS)
            nu, y, total_flux = in_plane(own, 0, image, side, start)
            other = (near, far)[side]
            total_flux = total_flux + (nu + other[0, rows, :]) * (y - image[1 - side, rows, :])
            if own is near:
                total_flux = total_flux + (nu + halo[0, rows, :]) * (y - near_image_in[0, rows, :])
            z = 0.5 * (y + total_flux)
            v = own[1, rows, :]
            w = y - c * v
            u = z - c * y
            q = q + fold(w * w)
            s = s + fold(w * u)
            t = t + fold(v * u)
    for index, value in enumerate((m0, m1, q, s, t, c)):
        value = jnp.sum(value, keepdims=True) if value.shape[0] > 1 else value
        sums[index : index + 1, :] = jnp.broadcast_to(value, (1, sums.shape[1]))


def face_kernel(far, far_in, far_part_in, image, own_sums, far_image_in, sums):
    slab, _ = place()
    count = lax.axis_size("slab")
    total, columns = far.shape[1:]
    beyond = jnp.where((slab > 0) & (slab < count - 1), 1.0, 0.0).astype(jnp.float32)
    c = own_sums[SUMS : SUMS + 1, 0:1]
    s = jnp.zeros((8, columns), jnp.float32)
    t = s
    for start in range(0, total, ROWS):
        rows = slice(start, start + ROWS)
        v = far[1, rows, :]
        y = image[0, rows, :]
        weight = 0.5 * (far[0, rows, :] + far_in[0, rows, :])
        outer = beyond * (far_part_in[0, rows, :] - weight * (v - far_in[1, rows, :]))
        far_image_in[0, rows, :] = outer
        flux = weight * (y - outer)
        s = s + fold((y - c * v) * flux)
        t = t + fold(v * flux)
    here = lax.broadcasted_iota(jnp.int32, sums.shape[1:], 0) == slab
    added = (None, None, None, s, t)
    for index in range(SUMS):
        value = own_sums[index : index + 1, :]
        if added[index] is not None:
            value = value + jnp.sum(added[index], keepdims=True)
        sums[index] = jnp.where(here, value, 0.0)


def finish_kernel(
    sums, far, near, far_in, near_in, image, far_image_in, near_image_in, potential, far_potential, mask, adjoint, *rest
):
    *terms, mixed, mixed_in = rest
    _, even = place()
    total = far.shape[1]
    m0_d, m1_d, q_d, s_d, t_d = (sums[i] for i in range(SUMS))
    m0 = jnp.sum(m0_d, axis=0, keepdims=True)
    m1 = jnp.sum(m1_d, axis=0, keepdims=True)
    c = m1 / m0
    delta = jnp.where(m0_d > 0, m1_d / m0_d, 0.0) - c
    ww = jnp.sum(q_d + delta * delta * m0_d, axis=0, keepdims=True)
    waw = jnp.sum(s_d + delta * (q_d + t_d) + delta * delta * m1_d, axis=0, keepdims=True)
    alpha0 = m0 / m1
    beta = alpha0 * (ww * alpha0 / m0)
    divisor = waw - ww * (ww / m1)
    alpha1 = jnp.where(divisor == 0, 0.0, ww / divisor)
    a = (alpha0 + alpha1 * (1.0 + beta))[:, 0:1]
    b = (-alpha1 * alpha0)[:, 0:1]
    scale = 0.25 / lax.axis_size("pos")
    firsts = first_rows(total)
    sides = ((far, even, far_in, far_image_in, far_potential, 0), (near, 1 - even, near_in, near_image_in, near_in, 2))
    for side, (own, layer, halo, image_in, halo_potential, at) in enumerate(sides):
        for start in range(0, total, ROWS):
            rows = slice(start, start + ROWS)
            out = a * own[1, rows, :] + b * image[side, rows, :]
            adjoint[layer, rows, :] = out
            mixed[side, rows, :] = out + 0.5 * potential[layer, rows, :]
            outer = a * halo[1, rows, :] + b * image_in[0, rows, :]
            mixed_in[side, rows, :] = outer + 0.5 * halo_potential[at, rows, :]
    for side, (own, layer, halo, image_in, halo_potential, at) in enumerate(sides):
        for start in range(0, total, ROWS):
            rows = slice(start, start + ROWS)
            g = potential[layer, rows, :]
            f = mixed[side, rows, :]
            result = (halo_potential[at, rows, :] - potential[1 - layer, rows, :]) * (
                mixed_in[side, rows, :] - mixed[1 - side, rows, :]
            )
            result = result + (turn(g, -1) - turn(g, 1)) * (turn(f, -1) - turn(f, 1))
            result = result + (
                shifted(potential, layer, start, 1) - shifted(potential, layer, start, -1)
            ) * (shifted(mixed, side, start, 1) - shifted(mixed, side, start, -1))
            weight = mask[layer, rows, :].astype(jnp.float32) * own[0, rows, :]
            index = max(i for i, first in enumerate(firsts) if first <= start)
            at_row = start - firsts[index]
            terms[index][layer, at_row : at_row + ROWS, :] = weight * (scale * result)


def in_hbm(x):
    return pltpu.with_memory_space_constraint(x, pltpu.HBM)


def first_rows(total):
    return [total // 8 * sum(EIGHTHS[:i]) for i in range(len(EIGHTHS))]


def close_kernel(start, total, arrived, *rest):
    gradient, held, sem = rest[-3:]
    held[...] = total[...] + arrived[...]
    copy = pltpu.make_async_copy(held, gradient.at[:, pl.ds(start, total.shape[1]), :], sem)
    copy.start()
    copy.wait()


def pairs(size, first):
    out = []
    for i in range(first, size - 1, 2):
        out += [(i, i + 1), (i + 1, i)]
    return out


def gather_sums(sums, slabs):
    steps = [2**k for k in range(1, slabs.bit_length() - 1)] + [1]
    for step in steps:
        sums = sums + lax.ppermute(sums, "slab", [(i, i ^ step) for i in range(slabs)])
    return sums


def partners(step, positions, slabs):
    bits = positions.bit_length() - 1
    route = []
    for p in range(positions):
        for s in range(slabs):
            bit = step if s % 2 == 0 else bits - 1 - step
            route.append((p * slabs + s, (p ^ (1 << bit)) * slabs + s))
    return route


def sum_positions(term, positions, slabs):
    arrived = lax.ppermute(term, ("pos", "slab"), partners(0, positions, slabs))
    for step in range(1, positions.bit_length() - 1):
        term = term + arrived
        arrived = lax.ppermute(term, ("pos", "slab"), partners(step, positions, slabs))
    return term, arrived


def local(labels, magnet_mask, reluctivity, rotor_shift, potential, adjoint_load):
    layers, radial, angular = labels.shape
    positions, slabs = lax.axis_size("pos"), lax.axis_size("slab")
    if layers != 2 or slabs % 2 or slabs & (slabs - 1) or radial % (8 * ROWS) or positions < 2 or positions & (positions - 1):
        raise ValueError("unsupported sizes")
    potential, load = potential[0], adjoint_load[0]
    f32 = functools.partial(jax.ShapeDtypeStruct, dtype=jnp.float32)
    plane = (radial, angular)
    vmem = pl.BlockSpec(memory_space=VMEM)
    smem = pl.BlockSpec(memory_space=SMEM)
    hbm = pl.BlockSpec(memory_space=pltpu.HBM)
    far, near, far_potential = pl.pallas_call(
        open_kernel,
        out_shape=tuple(pltpu.VMEM((k,) + plane, jnp.float32) for k in (2, 3, 1)),
        in_specs=[hbm, smem, hbm, hbm, hbm],
        out_specs=(vmem,) * 3,
        scratch_shapes=[
            VMEM((2,) + plane, jnp.int32),
            SMEM(reluctivity.shape, jnp.float32),
            pltpu.SemaphoreType.DMA((7,)),
        ],
        compiler_params=params(),
        name="open",
    )(in_hbm(reluctivity), rotor_shift, in_hbm(labels), in_hbm(load), in_hbm(potential))
    far_in = lax.ppermute(far, "slab", pairs(slabs, 1))
    near_in = lax.ppermute(near, "slab", pairs(slabs, 0))
    far_part, near_part = pl.pallas_call(
        part_kernel,
        out_shape=(pltpu.VMEM((1,) + plane, jnp.float32),) * 2,
        in_specs=[vmem] * 2,
        out_specs=(vmem,) * 2,
        compiler_params=params(),
        name="part",
    )(far, near)
    far_part_in = lax.ppermute(far_part, "slab", pairs(slabs, 1))
    near_part_in = lax.ppermute(near_part, "slab", pairs(slabs, 0))
    far_potential = lax.ppermute(far_potential, "slab", pairs(slabs, 1))
    image, near_image_in, own_sums = pl.pallas_call(
        sums_kernel,
        out_shape=(f32((2,) + plane), f32((1,) + plane), f32((8, 128))),
        in_specs=[vmem] * 7,
        out_specs=(vmem,) * 3,
        compiler_params=params(),
        name="sums",
    )(far, near, far_part, near_part, far_in, near_in, near_part_in)
    far_image_in, sums = pl.pallas_call(
        face_kernel,
        out_shape=(f32((1,) + plane), f32((SUMS, slabs, 128))),
        in_specs=[vmem] * 5,
        out_specs=(vmem,) * 2,
        compiler_params=params(),
        name="face",
    )(far, far_in, far_part_in, image, own_sums)
    sums = gather_sums(sums, slabs)
    spans = [radial // 8 * k for k in EIGHTHS]
    adjoint, *terms = pl.pallas_call(
        finish_kernel,
        out_shape=(pltpu.VMEM((2,) + plane, jnp.float32),) + tuple(f32((2, span, angular)) for span in spans),
        in_specs=[vmem] * 11,
        out_specs=(vmem,) * (1 + len(spans)),
        scratch_shapes=[VMEM((2,) + plane, jnp.float32)] * 2,
        compiler_params=params(),
        name="finish",
    )(sums, far, near, far_in, near_in, image, far_image_in, near_image_in, potential, far_potential, magnet_mask)
    gradient = ()
    for index, term in enumerate(terms):
        total, arrived = sum_positions(term, positions, slabs)
        gradient = pl.pallas_call(
            functools.partial(close_kernel, first_rows(radial)[index]),
            out_shape=pltpu.HBM((2,) + plane, jnp.float32),
            in_specs=[vmem] * 2 + [hbm] * (index > 0),
            out_specs=hbm,
            scratch_shapes=[VMEM(term.shape, jnp.float32), pltpu.SemaphoreType.DMA(())],
            input_output_aliases={2: 0} if index else {},
            compiler_params=params(),
            name="close",
        )(total, arrived, *((gradient,) if index else ()))
    return gradient, adjoint[None]


def solution(mesh):
    return jax.shard_map(
        local,
        mesh=mesh,
        in_specs=(
            P("slab", None, None),
            P("slab", None, None),
            P(),
            P("pos"),
            P("pos", "slab", None, None),
            P("pos", "slab", None, None),
        ),
        out_specs=(P("slab", None, None), P("pos", "slab", None, None)),
        check_vma=False,
    )
```

```python
import functools

import jax
import jax.numpy as jnp
from jax import lax
from jax.experimental import pallas as pl
from jax.experimental.pallas import tpu as pltpu
from jax.sharding import PartitionSpec as P


ROWS = 16
VMEM = pltpu.VMEM
SMEM = pltpu.SMEM
SUMS = 5
EIGHTHS = (3, 3, 2)


def params():
    return pltpu.CompilerParams(vmem_limit_bytes=40 * 1024 * 1024)


def shifted(ref, index, start, offset):
    total, columns = ref.shape[-2:]
    zero = jnp.zeros((1, columns), jnp.float32)
    if start + offset < 0:
        return jnp.concatenate([zero, ref[index, 0 : ROWS - 1, :]], axis=0)
    if start + offset + ROWS > total:
        return jnp.concatenate([ref[index, start + 1 : total, :], zero], axis=0)
    return ref[index, start + offset : start + offset + ROWS, :]


def turn(value, offset):
    return pltpu.roll(value, offset % value.shape[1], 1)


def in_plane(nu_ref, nu_index, ref, index, start):
    nu = nu_ref[nu_index, start : start + ROWS, :]
    v = ref[index, start : start + ROWS, :]
    flux = (nu + turn(nu, -1)) * (v - turn(v, -1))
    total = flux - turn(flux, 1)
    for offset in (-1, 1):
        total = total + (nu + shifted(nu_ref, nu_index, start, offset)) * (
            v - shifted(ref, index, start, offset)
        )
    return nu, v, total


def place():
    slab = lax.axis_index("slab")
    return slab, lax.rem(slab, 2)


def open_kernel(reluctivity, shift, labels, load, potential, far, near, far_potential, held, table, sems):
    _, even = place()
    odd = 1 - even
    total = labels.shape[1]
    moves = (
        (labels.at[even], held.at[0]),
        (labels.at[odd], held.at[1]),
        (load.at[even], far.at[1]),
        (load.at[odd], near.at[1]),
        (potential.at[even], far_potential.at[0]),
        (potential.at[odd], near.at[2]),
        (reluctivity, table),
    )
    copies = [pltpu.make_async_copy(src, dst, sems.at[i]) for i, (src, dst) in enumerate(moves)]
    for copy in copies:
        copy.start()
    copies[-1].wait()
    r0, r1, r2, r3 = (table[i] for i in range(4))
    offset = shift[0]
    for side, out in enumerate((far, near)):
        copies[side].wait()
        for start in range(0, total, ROWS):
            rows = slice(start, start + ROWS)
            material = held[side, rows, :]
            if start < total // 2:
                material = pltpu.roll(material, offset, 1)
            out[0, rows, :] = jnp.where(
                material < 2,
                jnp.where(material == 0, r0, r1),
                jnp.where(material == 2, r2, r3),
            )
    for copy in copies[2:-1]:
        copy.wait()


def part_kernel(far, near, far_part, near_part):
    total = far.shape[1]
    for own, other, out in ((far, near, far_part), (near, far, near_part)):
        for start in range(0, total, ROWS):
            rows = slice(start, start + ROWS)
            nu, v, total_flux = in_plane(own, 0, own, 1, start)
            total_flux = total_flux + (nu + other[0, rows, :]) * (v - other[1, rows, :])
            out[0, rows, :] = 0.5 * (v + total_flux)


def fold(value):
    return jnp.sum(value.reshape(ROWS // 8, 8, value.shape[1]), axis=0)


def sums_kernel(far, near, far_part, near_part, far_in, near_in, near_part_in, image, near_image_in, sums):
    total, columns = far.shape[1:]
    sides = ((far, far_part, far_in), (near, near_part, near_in))
    nil = jnp.zeros((8, columns), jnp.float32)
    m0, m1 = nil, nil
    for side, (own, part, halo) in enumerate(sides):
        for start in range(0, total, ROWS):
            rows = slice(start, start + ROWS)
            v = own[1, rows, :]
            flux = 0.5 * (own[0, rows, :] + halo[0, rows, :]) * (v - halo[1, rows, :])
            y = part[0, rows, :] + flux
            image[side, rows, :] = y
            if own is near:
                near_image_in[0, rows, :] = near_part_in[0, rows, :] - flux
            m0 = m0 + fold(v * v)
            m1 = m1 + fold(v * y)
    m0 = jnp.sum(m0, keepdims=True)
    m1 = jnp.sum(m1, keepdims=True)
    c = jnp.where(m0 > 0, m1 / m0, 0.0)
    q, s, t = nil, nil, nil
    for side, (own, _, halo) in enumerate(sides):
        for start in range(0, total, ROWS):
            rows = slice(start, start + ROWS)
            nu, y, total_flux = in_plane(own, 0, image, side, start)
            other = (near, far)[side]
            total_flux = total_flux + (nu + other[0, rows, :]) * (y - image[1 - side, rows, :])
            if own is near:
                total_flux = total_flux + (nu + halo[0, rows, :]) * (y - near_image_in[0, rows, :])
            z = 0.5 * (y + total_flux)
            v = own[1, rows, :]
            w = y - c * v
            u = z - c * y
            q = q + fold(w * w)
            s = s + fold(w * u)
            t = t + fold(v * u)
    for index, value in enumerate((m0, m1, q, s, t, c)):
        value = jnp.sum(value, keepdims=True) if value.shape[0] > 1 else value
        sums[index : index + 1, :] = jnp.broadcast_to(value, (1, sums.shape[1]))


def face_kernel(far, far_in, far_part_in, image, own_sums, far_image_in, sums):
    slab, _ = place()
    count = lax.axis_size("slab")
    total, columns = far.shape[1:]
    beyond = jnp.where((slab > 0) & (slab < count - 1), 1.0, 0.0).astype(jnp.float32)
    c = own_sums[SUMS : SUMS + 1, 0:1]
    s = jnp.zeros((8, columns), jnp.float32)
    t = s
    for start in range(0, total, ROWS):
        rows = slice(start, start + ROWS)
        v = far[1, rows, :]
        y = image[0, rows, :]
        weight = 0.5 * (far[0, rows, :] + far_in[0, rows, :])
        outer = beyond * (far_part_in[0, rows, :] - weight * (v - far_in[1, rows, :]))
        far_image_in[0, rows, :] = outer
        flux = weight * (y - outer)
        s = s + fold((y - c * v) * flux)
        t = t + fold(v * flux)
    here = lax.broadcasted_iota(jnp.int32, sums.shape[1:], 0) == slab
    added = (None, None, None, s, t)
    for index in range(SUMS):
        value = own_sums[index : index + 1, :]
        if added[index] is not None:
            value = value + jnp.sum(added[index], keepdims=True)
        sums[index] = jnp.where(here, value, 0.0)


def fields_kernel(
    far, near, far_in, near_in, image, far_image_in, near_image_in, potential, far_potential, mask, u1, u2, u3
):
    _, even = place()
    total = far.shape[1]
    scale = 0.25 / lax.axis_size("pos")
    sides = ((far, even, far_in, far_image_in, far_potential, 0), (near, 1 - even, near_in, near_image_in, near_in, 2))
    for side, (own, layer, halo, image_in, halo_potential, at) in enumerate(sides):
        other = (near, far)[side]
        for start in range(0, total, ROWS):
            rows = slice(start, start + ROWS)
            slopes = []
            for ref, index, beyond, inner in (
                (potential, layer, halo_potential[at, rows, :], potential[1 - layer, rows, :]),
                (own, 1, halo[1, rows, :], other[1, rows, :]),
                (image, side, image_in[0, rows, :], image[1 - side, rows, :]),
            ):
                field = ref[index, rows, :]
                slopes.append(
                    (
                        beyond - inner,
                        turn(field, -1) - turn(field, 1),
                        shifted(ref, index, start, 1) - shifted(ref, index, start, -1),
                    )
                )
            weight = scale * (mask[layer, rows, :].astype(jnp.float32) * own[0, rows, :])
            g = [weight * slope for slope in slopes[0]]
            for out, factor, slope in ((u1, 1.0, slopes[1]), (u2, 1.0, slopes[2]), (u3, 0.5, slopes[0])):
                out[layer, rows, :] = factor * (g[0] * slope[0] + g[1] * slope[1] + g[2] * slope[2])


def coefficients(sums):
    m0_d, m1_d, q_d, s_d, t_d = (sums[i] for i in range(SUMS))
    m0 = jnp.sum(m0_d, axis=0, keepdims=True)
    m1 = jnp.sum(m1_d, axis=0, keepdims=True)
    c = m1 / m0
    delta = jnp.where(m0_d > 0, m1_d / m0_d, 0.0) - c
    ww = jnp.sum(q_d + delta * delta * m0_d, axis=0, keepdims=True)
    waw = jnp.sum(s_d + delta * (q_d + t_d) + delta * delta * m1_d, axis=0, keepdims=True)
    alpha0 = m0 / m1
    beta = alpha0 * (ww * alpha0 / m0)
    divisor = waw - ww * (ww / m1)
    alpha1 = jnp.where(divisor == 0, 0.0, ww / divisor)
    return (alpha0 + alpha1 * (1.0 + beta))[:, 0:1], (-alpha1 * alpha0)[:, 0:1]


def term_kernel(sums, u1, u2, u3, *terms):
    a, b = coefficients(sums)
    for term, first in zip(terms, first_rows(u1.shape[1])):
        for layer in range(2):
            for start in range(0, term.shape[1], ROWS):
                rows = slice(first + start, first + start + ROWS)
                term[layer, start : start + ROWS, :] = (
                    a * u1[layer, rows, :] + b * u2[layer, rows, :] + u3[layer, rows, :]
                )


def adjoint_kernel(sums, far, near, image, adjoint, held, sem):
    _, even = place()
    a, b = coefficients(sums)
    for side, (own, layer) in enumerate(((far, even), (near, 1 - even))):
        for start in range(0, far.shape[1], ROWS):
            rows = slice(start, start + ROWS)
            held[layer, rows, :] = a * own[1, rows, :] + b * image[side, rows, :]
    copy = pltpu.make_async_copy(held, adjoint, sem)
    copy.start()
    copy.wait()


def in_hbm(x):
    return pltpu.with_memory_space_constraint(x, pltpu.HBM)


def first_rows(total):
    return [total // 8 * sum(EIGHTHS[:i]) for i in range(len(EIGHTHS))]


def close_kernel(start, total, arrived, *rest):
    gradient, held, sem = rest[-3:]
    held[...] = total[...] + arrived[...]
    copy = pltpu.make_async_copy(held, gradient.at[:, pl.ds(start, total.shape[1]), :], sem)
    copy.start()
    copy.wait()


def pairs(size, first):
    out = []
    for i in range(first, size - 1, 2):
        out += [(i, i + 1), (i + 1, i)]
    return out


def gather_sums(sums, fields, slabs):
    steps = [2**k for k in range(1, slabs.bit_length() - 1)] + [1]
    for step in steps:
        arrived = lax.ppermute(sums, "slab", [(i, i ^ step) for i in range(slabs)])
        if step == steps[-2]:
            arrived, *fields = lax.optimization_barrier((arrived, *fields))
        sums = sums + arrived
    return sums, fields


def partners(step, positions, slabs):
    bits = positions.bit_length() - 1
    route = []
    for p in range(positions):
        for s in range(slabs):
            bit = step if s % 2 == 0 else bits - 1 - step
            route.append((p * slabs + s, (p ^ (1 << bit)) * slabs + s))
    return route


def sum_positions(term, positions, slabs):
    arrived = lax.ppermute(term, ("pos", "slab"), partners(0, positions, slabs))
    for step in range(1, positions.bit_length() - 1):
        term = term + arrived
        arrived = lax.ppermute(term, ("pos", "slab"), partners(step, positions, slabs))
    return term, arrived


def local(labels, magnet_mask, reluctivity, rotor_shift, potential, adjoint_load):
    layers, radial, angular = labels.shape
    positions, slabs = lax.axis_size("pos"), lax.axis_size("slab")
    if layers != 2 or slabs < 4 or slabs & (slabs - 1) or radial % (8 * ROWS) or positions < 2 or positions & (positions - 1):
        raise ValueError("unsupported sizes")
    potential, load = potential[0], adjoint_load[0]
    f32 = functools.partial(jax.ShapeDtypeStruct, dtype=jnp.float32)
    plane = (radial, angular)
    vmem = pl.BlockSpec(memory_space=VMEM)
    smem = pl.BlockSpec(memory_space=SMEM)
    hbm = pl.BlockSpec(memory_space=pltpu.HBM)
    far, near, far_potential = pl.pallas_call(
        open_kernel,
        out_shape=tuple(pltpu.VMEM((k,) + plane, jnp.float32) for k in (2, 3, 1)),
        in_specs=[hbm, smem, hbm, hbm, hbm],
        out_specs=(vmem,) * 3,
        scratch_shapes=[
            VMEM((2,) + plane, jnp.int32),
            SMEM(reluctivity.shape, jnp.float32),
            pltpu.SemaphoreType.DMA((7,)),
        ],
        compiler_params=params(),
        name="open",
    )(in_hbm(reluctivity), rotor_shift, in_hbm(labels), in_hbm(load), in_hbm(potential))
    far_in = lax.ppermute(far, "slab", pairs(slabs, 1))
    near_in = lax.ppermute(near, "slab", pairs(slabs, 0))
    far_part, near_part = pl.pallas_call(
        part_kernel,
        out_shape=(pltpu.VMEM((1,) + plane, jnp.float32),) * 2,
        in_specs=[vmem] * 2,
        out_specs=(vmem,) * 2,
        compiler_params=params(),
        name="part",
    )(far, near)
    far_part_in = lax.ppermute(far_part, "slab", pairs(slabs, 1))
    near_part_in = lax.ppermute(near_part, "slab", pairs(slabs, 0))
    far_potential = lax.ppermute(far_potential, "slab", pairs(slabs, 1))
    image, near_image_in, own_sums = pl.pallas_call(
        sums_kernel,
        out_shape=(f32((2,) + plane), f32((1,) + plane), f32((8, 128))),
        in_specs=[vmem] * 7,
        out_specs=(vmem,) * 3,
        compiler_params=params(),
        name="sums",
    )(far, near, far_part, near_part, far_in, near_in, near_part_in)
    far_image_in, sums = pl.pallas_call(
        face_kernel,
        out_shape=(f32((1,) + plane), f32((SUMS, slabs, 128))),
        in_specs=[vmem] * 5,
        out_specs=(vmem,) * 2,
        compiler_params=params(),
        name="face",
    )(far, far_in, far_part_in, image, own_sums)
    fields = pl.pallas_call(
        fields_kernel,
        out_shape=(f32((2,) + plane),) * 3,
        in_specs=[vmem] * 10,
        out_specs=(vmem,) * 3,
        compiler_params=params(),
        name="fields",
    )(far, near, far_in, near_in, image, far_image_in, near_image_in, potential, far_potential, magnet_mask)
    sums, fields = gather_sums(sums, fields, slabs)
    spans = [radial // 8 * k for k in EIGHTHS]
    terms = pl.pallas_call(
        term_kernel,
        out_shape=tuple(f32((2, span, angular)) for span in spans),
        in_specs=[vmem] * 4,
        out_specs=(vmem,) * len(spans),
        compiler_params=params(),
        name="term",
    )(sums, *fields)
    adjoint = pl.pallas_call(
        adjoint_kernel,
        out_shape=pltpu.HBM((2,) + plane, jnp.float32),
        in_specs=[vmem] * 4,
        out_specs=hbm,
        scratch_shapes=[VMEM((2,) + plane, jnp.float32), pltpu.SemaphoreType.DMA(())],
        compiler_params=params(),
        name="adjoint",
    )(sums, far, near, image)
    gradient = ()
    for index, term in enumerate(terms):
        total, arrived = sum_positions(term, positions, slabs)
        gradient = pl.pallas_call(
            functools.partial(close_kernel, first_rows(radial)[index]),
            out_shape=pltpu.HBM((2,) + plane, jnp.float32),
            in_specs=[vmem] * 2 + [hbm] * (index > 0),
            out_specs=hbm,
            scratch_shapes=[VMEM(term.shape, jnp.float32), pltpu.SemaphoreType.DMA(())],
            input_output_aliases={2: 0} if index else {},
            compiler_params=params(),
            name="close",
        )(total, arrived, *((gradient,) if index else ()))
    return gradient, adjoint[None]


def solution(mesh):
    return jax.shard_map(
        local,
        mesh=mesh,
        in_specs=(
            P("slab", None, None),
            P("slab", None, None),
            P(),
            P("pos"),
            P("pos", "slab", None, None),
            P("pos", "slab", None, None),
        ),
        out_specs=(P("slab", None, None), P("pos", "slab", None, None)),
        check_vma=False,
    )
```

```python
import functools

import jax
import jax.numpy as jnp
from jax import lax
from jax.experimental import pallas as pl
from jax.experimental.pallas import tpu as pltpu
from jax.sharding import PartitionSpec as P


ROWS = 16
VMEM = pltpu.VMEM
SMEM = pltpu.SMEM
SUMS = 5
EIGHTHS = (3, 3, 2)


def params():
    return pltpu.CompilerParams(vmem_limit_bytes=40 * 1024 * 1024)


def shifted(ref, index, start, offset):
    total, columns = ref.shape[-2:]
    zero = jnp.zeros((1, columns), jnp.float32)
    if start + offset < 0:
        return jnp.concatenate([zero, ref[index, 0 : ROWS - 1, :]], axis=0)
    if start + offset + ROWS > total:
        return jnp.concatenate([ref[index, start + 1 : total, :], zero], axis=0)
    return ref[index, start + offset : start + offset + ROWS, :]


def turn(value, offset):
    return pltpu.roll(value, offset % value.shape[1], 1)


def in_plane(nu_ref, nu_index, ref, index, start):
    nu = nu_ref[nu_index, start : start + ROWS, :]
    v = ref[index, start : start + ROWS, :]
    total = None
    for offset in (-1, 1):
        across = (nu + turn(nu, offset)) * (v - turn(v, offset))
        total = across if total is None else total + across
        total = total + (nu + shifted(nu_ref, nu_index, start, offset)) * (
            v - shifted(ref, index, start, offset)
        )
    return nu, v, total


def beyond_far():
    slab, _ = place()
    inside = (slab > 0) & (slab < lax.axis_size("slab") - 1)
    return jnp.where(inside, 1.0, 0.0).astype(jnp.float32)


def place():
    slab = lax.axis_index("slab")
    return slab, lax.rem(slab, 2)


def open_kernel(reluctivity, shift, labels, load, potential, far, near, far_potential, near_potential, held, table, sems):
    _, even = place()
    odd = 1 - even
    total = labels.shape[1]
    moves = (
        (labels.at[even], held.at[0]),
        (labels.at[odd], held.at[1]),
        (load.at[even], far.at[1]),
        (load.at[odd], near.at[1]),
        (potential.at[even], far_potential.at[0]),
        (potential.at[odd], near_potential.at[0]),
        (reluctivity, table),
    )
    copies = [pltpu.make_async_copy(src, dst, sems.at[i]) for i, (src, dst) in enumerate(moves)]
    for copy in copies:
        copy.start()
    copies[-1].wait()
    r0, r1, r2, r3 = (table[i] for i in range(4))
    offset = shift[0]
    for side, out in enumerate((far, near)):
        copies[side].wait()
        for start in range(0, total, ROWS):
            rows = slice(start, start + ROWS)
            material = held[side, rows, :]
            if start < total // 2:
                material = pltpu.roll(material, offset, 1)
            out[0, rows, :] = jnp.where(
                material < 2,
                jnp.where(material == 0, r0, r1),
                jnp.where(material == 2, r2, r3),
            )
    for copy in copies[2:-1]:
        copy.wait()


def part_kernel(far, near, far_potential, far_part, near_part, far_early, far_late):
    _, even = place()
    total = far.shape[1]
    half = total // 2
    for own, other, out in ((far, near, far_part), (near, far, near_part)):
        for start in range(0, total, ROWS):
            rows = slice(start, start + ROWS)
            nu, v, total_flux = in_plane(own, 0, own, 1, start)
            total_flux = total_flux + (nu + other[0, rows, :]) * (v - other[1, rows, :])
            out[0, rows, :] = 0.5 * (v + total_flux)
    far_early[0] = far_part[0, pl.ds(pl.multiple_of((1 - even) * half, 8), half), :]
    far_late[0, 0:half, :] = far_part[0, pl.ds(pl.multiple_of(even * half, 8), half), :]
    far_late[0, half : half + total, :] = far_potential[0]


def fold(value):
    return jnp.sum(value.reshape(ROWS // 8, 8, value.shape[1]), axis=0)


def sums_kernel(far, near, far_part, near_part, far_in, near_in, near_part_in, image, near_image_in, sums):
    total, columns = far.shape[1:]
    sides = ((far, far_part, far_in), (near, near_part, near_in))
    end = 1.0 - beyond_far()
    nil = jnp.zeros((8, columns), jnp.float32)
    m0, m1 = nil, nil
    for side, (own, part, halo) in enumerate(sides):
        for start in range(0, total, ROWS):
            rows = slice(start, start + ROWS)
            v = own[1, rows, :]
            flux = 0.5 * (own[0, rows, :] + halo[0, rows, :]) * (v - halo[1, rows, :])
            y = part[0, rows, :] + flux
            image[side, rows, :] = y
            if own is near:
                near_image_in[0, rows, :] = near_part_in[0, rows, :] - flux
            m0 = m0 + fold(v * v)
            m1 = m1 + fold(v * y)
    m0 = jnp.sum(m0, keepdims=True)
    m1 = jnp.sum(m1, keepdims=True)
    c = jnp.where(m0 > 0, m1 / m0, 0.0)
    q, s, t = nil, nil, nil
    for side, (own, _, halo) in enumerate(sides):
        for start in range(0, total, ROWS):
            rows = slice(start, start + ROWS)
            nu, y, total_flux = in_plane(own, 0, image, side, start)
            other = (near, far)[side]
            total_flux = total_flux + (nu + other[0, rows, :]) * (y - image[1 - side, rows, :])
            if own is near:
                total_flux = total_flux + (nu + halo[0, rows, :]) * (y - near_image_in[0, rows, :])
            else:
                total_flux = total_flux + end * (nu * y)
            z = 0.5 * (y + total_flux)
            v = own[1, rows, :]
            w = y - c * v
            u = z - c * y
            q = q + fold(w * w)
            s = s + fold(w * u)
            t = t + fold(v * u)
    for index, value in enumerate((m0, m1, q, s, t, c)):
        value = jnp.sum(value, keepdims=True) if value.shape[0] > 1 else value
        sums[index : index + 1, :] = jnp.broadcast_to(value, (1, sums.shape[1]))


def face_kernel(far, far_in, far_early_in, image, own_sums, sums):
    slab, even = place()
    total, columns = far.shape[1:]
    half = total // 2
    beyond = beyond_far()
    c = own_sums[SUMS : SUMS + 1, 0:1]
    s = jnp.zeros((8, columns), jnp.float32)
    t = s
    for start in range(0, half, ROWS):
        rows = pl.ds(pl.multiple_of(even * half + start, 8), ROWS)
        v = far[1, rows, :]
        y = image[0, rows, :]
        outer_v = far_in[1, rows, :]
        step = v - outer_v
        weight = 0.5 * (far[0, rows, :] + far_in[0, rows, :])
        outer = far_early_in[0, start : start + ROWS, :] - weight * step
        flux = beyond * (weight * (y - outer))
        s = s + fold(((y - c * v) - (outer - c * outer_v)) * flux)
        t = t + fold(step * flux)
    here = lax.broadcasted_iota(jnp.int32, sums.shape[1:], 0) == slab
    added = (None, None, None, s, t)
    for index in range(SUMS):
        value = own_sums[index : index + 1, :]
        if added[index] is not None:
            value = value + jnp.sum(added[index], keepdims=True)
        sums[index] = jnp.where(here, value, 0.0)


def fields_kernel(
    far, near, far_in, near_in, image, far_early_in, far_late_in, near_image_in, potential, near_potential, mask, u1, u2, u3
):
    _, even = place()
    total = far.shape[1]
    scale = 0.25 / lax.axis_size("pos")
    half = total // 2
    beyond_end = beyond_far()
    sides = ((far, even, far_in), (near, 1 - even, near_in))
    for side, (own, layer, halo) in enumerate(sides):
        other = (near, far)[side]
        for start in range(0, total, ROWS):
            rows = slice(start, start + ROWS)
            if own is far:
                piece = slice(start % half, start % half + ROWS)
                early = even == start // half
                part = jnp.where(early, far_early_in[0, piece, :], far_late_in[0, piece, :])
                weight = 0.5 * (far[0, rows, :] + far_in[0, rows, :])
                image_in = beyond_end * (part - weight * (far[1, rows, :] - far_in[1, rows, :]))
                potential_in = far_late_in[0, half + start : half + start + ROWS, :]
            else:
                image_in = near_image_in[0, rows, :]
                potential_in = near_potential[0, rows, :]
            slopes = []
            for ref, index, beyond, inner in (
                (potential, layer, potential_in, potential[1 - layer, rows, :]),
                (own, 1, halo[1, rows, :], other[1, rows, :]),
                (image, side, image_in, image[1 - side, rows, :]),
            ):
                field = ref[index, rows, :]
                slopes.append(
                    (
                        beyond - inner,
                        turn(field, -1) - turn(field, 1),
                        shifted(ref, index, start, 1) - shifted(ref, index, start, -1),
                    )
                )
            weight = scale * (mask[layer, rows, :].astype(jnp.float32) * own[0, rows, :])
            g = [weight * slope for slope in slopes[0]]
            for out, factor, slope in ((u1, 1.0, slopes[1]), (u2, 1.0, slopes[2]), (u3, 0.5, slopes[0])):
                out[layer, rows, :] = factor * (g[0] * slope[0] + g[1] * slope[1] + g[2] * slope[2])


def coefficients(sums):
    m0_d, m1_d, q_d, s_d, t_d = (sums[i] for i in range(SUMS))
    m0 = jnp.sum(m0_d, axis=0, keepdims=True)
    m1 = jnp.sum(m1_d, axis=0, keepdims=True)
    c = m1 / m0
    delta = jnp.where(m0_d > 0, m1_d / m0_d, 0.0) - c
    ww = jnp.sum(q_d + delta * delta * m0_d, axis=0, keepdims=True)
    waw = jnp.sum(s_d + delta * (q_d + t_d) + delta * delta * m1_d, axis=0, keepdims=True)
    alpha0 = m0 / m1
    beta = alpha0 * (ww * alpha0 / m0)
    divisor = waw - ww * (ww / m1)
    alpha1 = jnp.where(divisor == 0, 0.0, ww / divisor)
    return (alpha0 + alpha1 * (1.0 + beta))[:, 0:1], (-alpha1 * alpha0)[:, 0:1]


def term_kernel(sums, u1, u2, u3, *terms):
    a, b = coefficients(sums)
    for term, first in zip(terms, first_rows(u1.shape[1])):
        for layer in range(2):
            for start in range(0, term.shape[1], ROWS):
                rows = slice(first + start, first + start + ROWS)
                term[layer, start : start + ROWS, :] = (
                    a * u1[layer, rows, :] + b * u2[layer, rows, :] + u3[layer, rows, :]
                )


def adjoint_kernel(sums, far, near, image, adjoint, held, sem):
    _, even = place()
    a, b = coefficients(sums)
    for side, (own, layer) in enumerate(((far, even), (near, 1 - even))):
        for start in range(0, far.shape[1], ROWS):
            rows = slice(start, start + ROWS)
            held[layer, rows, :] = a * own[1, rows, :] + b * image[side, rows, :]
    copy = pltpu.make_async_copy(held, adjoint, sem)
    copy.start()
    copy.wait()


def in_hbm(x):
    return pltpu.with_memory_space_constraint(x, pltpu.HBM)


def first_rows(total):
    return [total // 8 * sum(EIGHTHS[:i]) for i in range(len(EIGHTHS))]


def close_kernel(start, total, arrived, *rest):
    gradient, held, sem = rest[-3:]
    held[...] = total[...] + arrived[...]
    copy = pltpu.make_async_copy(held, gradient.at[:, pl.ds(start, total.shape[1]), :], sem)
    copy.start()
    copy.wait()


def pairs(size, first):
    out = []
    for i in range(first, size - 1, 2):
        out += [(i, i + 1), (i + 1, i)]
    return out


def gather_sums(sums, fields, slabs):
    steps = [2**k for k in range(1, slabs.bit_length() - 1)] + [1]
    for step in steps:
        arrived = lax.ppermute(sums, "slab", [(i, i ^ step) for i in range(slabs)])
        if step == steps[-2]:
            arrived, *fields = lax.optimization_barrier((arrived, *fields))
        sums = sums + arrived
    return sums, fields


def partners(step, positions, slabs):
    bits = positions.bit_length() - 1
    route = []
    for p in range(positions):
        for s in range(slabs):
            bit = step if s % 2 == 0 else bits - 1 - step
            route.append((p * slabs + s, (p ^ (1 << bit)) * slabs + s))
    return route


def sum_positions(term, positions, slabs):
    arrived = lax.ppermute(term, ("pos", "slab"), partners(0, positions, slabs))
    for step in range(1, positions.bit_length() - 1):
        term = term + arrived
        arrived = lax.ppermute(term, ("pos", "slab"), partners(step, positions, slabs))
    return term, arrived


def local(labels, magnet_mask, reluctivity, rotor_shift, potential, adjoint_load):
    layers, radial, angular = labels.shape
    positions, slabs = lax.axis_size("pos"), lax.axis_size("slab")
    if layers != 2 or slabs < 4 or slabs & (slabs - 1) or radial % (8 * ROWS) or positions < 2 or positions & (positions - 1):
        raise ValueError("unsupported sizes")
    potential, load = potential[0], adjoint_load[0]
    f32 = functools.partial(jax.ShapeDtypeStruct, dtype=jnp.float32)
    plane = (radial, angular)
    vmem = pl.BlockSpec(memory_space=VMEM)
    smem = pl.BlockSpec(memory_space=SMEM)
    hbm = pl.BlockSpec(memory_space=pltpu.HBM)
    far, near, far_potential, near_potential = pl.pallas_call(
        open_kernel,
        out_shape=tuple(pltpu.VMEM((k,) + plane, jnp.float32) for k in (2, 2, 1, 1)),
        in_specs=[hbm, smem, hbm, hbm, hbm],
        out_specs=(vmem,) * 4,
        scratch_shapes=[
            VMEM((2,) + plane, jnp.int32),
            SMEM(reluctivity.shape, jnp.float32),
            pltpu.SemaphoreType.DMA((7,)),
        ],
        compiler_params=params(),
        name="open",
    )(in_hbm(reluctivity), rotor_shift, in_hbm(labels), in_hbm(load), in_hbm(potential))
    far_in = lax.ppermute(far, "slab", pairs(slabs, 1))
    near_in = lax.ppermute(near, "slab", pairs(slabs, 0))
    half = radial // 2
    far_part, near_part, far_early, far_late = pl.pallas_call(
        part_kernel,
        out_shape=tuple(pltpu.VMEM((1, rows, angular), jnp.float32) for rows in (radial, radial, half, half + radial)),
        in_specs=[vmem] * 3,
        out_specs=(vmem,) * 4,
        compiler_params=params(),
        name="part",
    )(far, near, far_potential)
    far_early_in = lax.ppermute(far_early, "slab", pairs(slabs, 1))
    near_part_in = lax.ppermute(near_part, "slab", pairs(slabs, 0))
    far_late_in = lax.ppermute(far_late, "slab", pairs(slabs, 1))
    image, near_image_in, own_sums = pl.pallas_call(
        sums_kernel,
        out_shape=(f32((2,) + plane), f32((1,) + plane), f32((8, 128))),
        in_specs=[vmem] * 7,
        out_specs=(vmem,) * 3,
        compiler_params=params(),
        name="sums",
    )(far, near, far_part, near_part, far_in, near_in, near_part_in)
    sums = pl.pallas_call(
        face_kernel,
        out_shape=f32((SUMS, slabs, 128)),
        in_specs=[vmem] * 5,
        out_specs=vmem,
        compiler_params=params(),
        name="face",
    )(far, far_in, far_early_in, image, own_sums)
    near_potential, sums = lax.optimization_barrier((near_potential, sums))
    near_potential = lax.ppermute(near_potential, "slab", pairs(slabs, 0))
    fields = pl.pallas_call(
        fields_kernel,
        out_shape=(f32((2,) + plane),) * 3,
        in_specs=[vmem] * 11,
        out_specs=(vmem,) * 3,
        compiler_params=params(),
        name="fields",
    )(far, near, far_in, near_in, image, far_early_in, far_late_in, near_image_in, potential, near_potential, magnet_mask)
    sums, fields = gather_sums(sums, fields, slabs)
    spans = [radial // 8 * k for k in EIGHTHS]
    terms = pl.pallas_call(
        term_kernel,
        out_shape=tuple(f32((2, span, angular)) for span in spans),
        in_specs=[vmem] * 4,
        out_specs=(vmem,) * len(spans),
        compiler_params=params(),
        name="term",
    )(sums, *fields)
    adjoint = pl.pallas_call(
        adjoint_kernel,
        out_shape=pltpu.HBM((2,) + plane, jnp.float32),
        in_specs=[vmem] * 4,
        out_specs=hbm,
        scratch_shapes=[VMEM((2,) + plane, jnp.float32), pltpu.SemaphoreType.DMA(())],
        compiler_params=params(),
        name="adjoint",
    )(sums, far, near, image)
    gradient = ()
    for index, term in enumerate(terms):
        total, arrived = sum_positions(term, positions, slabs)
        gradient = pl.pallas_call(
            functools.partial(close_kernel, first_rows(radial)[index]),
            out_shape=pltpu.HBM((2,) + plane, jnp.float32),
            in_specs=[vmem] * 2 + [hbm] * (index > 0),
            out_specs=hbm,
            scratch_shapes=[VMEM(term.shape, jnp.float32), pltpu.SemaphoreType.DMA(())],
            input_output_aliases={2: 0} if index else {},
            compiler_params=params(),
            name="close",
        )(total, arrived, *((gradient,) if index else ()))
    return gradient, adjoint[None]


def solution(mesh):
    return jax.shard_map(
        local,
        mesh=mesh,
        in_specs=(
            P("slab", None, None),
            P("slab", None, None),
            P(),
            P("pos"),
            P("pos", "slab", None, None),
            P("pos", "slab", None, None),
        ),
        out_specs=(P("slab", None, None), P("pos", "slab", None, None)),
        check_vma=False,
    )
```

```python
import functools

import jax
import jax.numpy as jnp
from jax import lax
from jax.experimental import pallas as pl
from jax.experimental.pallas import tpu as pltpu
from jax.sharding import PartitionSpec as P


ROWS = 16
VMEM = pltpu.VMEM
SMEM = pltpu.SMEM
SUMS = 5
EIGHTHS = (3, 3, 2)


def params():
    return pltpu.CompilerParams(vmem_limit_bytes=40 * 1024 * 1024)


def shifted(ref, index, start, offset):
    total, columns = ref.shape[-2:]
    zero = jnp.zeros((1, columns), jnp.float32)
    if start + offset < 0:
        return jnp.concatenate([zero, ref[index, 0 : ROWS - 1, :]], axis=0)
    if start + offset + ROWS > total:
        return jnp.concatenate([ref[index, start + 1 : total, :], zero], axis=0)
    return ref[index, start + offset : start + offset + ROWS, :]


def turn(value, offset):
    return pltpu.roll(value, offset % value.shape[1], 1)


def in_plane(nu_ref, nu_index, ref, index, start):
    nu = nu_ref[nu_index, start : start + ROWS, :]
    v = ref[index, start : start + ROWS, :]
    total = None
    for offset in (-1, 1):
        across = (nu + turn(nu, offset)) * (v - turn(v, offset))
        total = across if total is None else total + across
        total = total + (nu + shifted(nu_ref, nu_index, start, offset)) * (
            v - shifted(ref, index, start, offset)
        )
    return nu, v, total


def beyond_far():
    slab, _ = place()
    inside = (slab > 0) & (slab < lax.axis_size("slab") - 1)
    return jnp.where(inside, 1.0, 0.0).astype(jnp.float32)


def place():
    slab = lax.axis_index("slab")
    return slab, lax.rem(slab, 2)


def open_kernel(reluctivity, shift, labels, load, potential, far, near, far_potential, near_potential, held, table, sems):
    _, even = place()
    odd = 1 - even
    total = labels.shape[1]
    moves = (
        (labels.at[even], held.at[0]),
        (labels.at[odd], held.at[1]),
        (load.at[even], far.at[1]),
        (load.at[odd], near.at[1]),
        (potential.at[even], far_potential.at[0]),
        (potential.at[odd], near_potential.at[0]),
        (reluctivity, table),
    )
    copies = [pltpu.make_async_copy(src, dst, sems.at[i]) for i, (src, dst) in enumerate(moves)]
    for copy in copies:
        copy.start()
    copies[-1].wait()
    r0, r1, r2, r3 = (table[i] for i in range(4))
    offset = shift[0]
    for side, out in enumerate((far, near)):
        copies[side].wait()
        for start in range(0, total, ROWS):
            rows = slice(start, start + ROWS)
            material = held[side, rows, :]
            if start < total // 2:
                material = pltpu.roll(material, offset, 1)
            out[0, rows, :] = jnp.where(
                material < 2,
                jnp.where(material == 0, r0, r1),
                jnp.where(material == 2, r2, r3),
            )
    for copy in copies[2:-1]:
        copy.wait()


def part_kernel(far, near, far_potential, far_part, near_part, far_early, far_late):
    _, even = place()
    total = far.shape[1]
    half = total // 2
    for own, other, out in ((far, near, far_part), (near, far, near_part)):
        for start in range(0, total, ROWS):
            rows = slice(start, start + ROWS)
            nu, v, total_flux = in_plane(own, 0, own, 1, start)
            total_flux = total_flux + (nu + other[0, rows, :]) * (v - other[1, rows, :])
            out[0, rows, :] = 0.5 * (v + total_flux)
    far_early[0] = far_part[0, pl.ds(pl.multiple_of((1 - even) * half, 8), half), :]
    far_late[0, 0:half, :] = far_part[0, pl.ds(pl.multiple_of(even * half, 8), half), :]
    far_late[0, half : half + total, :] = far_potential[0]


def fold(value):
    return jnp.sum(value.reshape(ROWS // 8, 8, value.shape[1]), axis=0)


def sums_kernel(far, near, far_part, near_part, far_in, near_in, near_part_in, image, near_image_in, sums):
    total, columns = far.shape[1:]
    sides = ((far, far_part, far_in), (near, near_part, near_in))
    end = 1.0 - beyond_far()
    nil = jnp.zeros((8, columns), jnp.float32)
    m0, m1 = nil, nil
    for side, (own, part, halo) in enumerate(sides):
        for start in range(0, total, ROWS):
            rows = slice(start, start + ROWS)
            v = own[1, rows, :]
            flux = 0.5 * (own[0, rows, :] + halo[0, rows, :]) * (v - halo[1, rows, :])
            y = part[0, rows, :] + flux
            image[side, rows, :] = y
            if own is near:
                near_image_in[0, rows, :] = near_part_in[0, rows, :] - flux
            m0 = m0 + fold(v * v)
            m1 = m1 + fold(v * y)
    m0 = jnp.sum(m0, keepdims=True)
    m1 = jnp.sum(m1, keepdims=True)
    c = jnp.where(m0 > 0, m1 / m0, 0.0)
    q, s, t = nil, nil, nil
    for side, (own, _, halo) in enumerate(sides):
        for start in range(0, total, ROWS):
            rows = slice(start, start + ROWS)
            nu, y, total_flux = in_plane(own, 0, image, side, start)
            other = (near, far)[side]
            total_flux = total_flux + (nu + other[0, rows, :]) * (y - image[1 - side, rows, :])
            if own is near:
                total_flux = total_flux + (nu + halo[0, rows, :]) * (y - near_image_in[0, rows, :])
            else:
                total_flux = total_flux + end * (nu * y)
            z = 0.5 * (y + total_flux)
            v = own[1, rows, :]
            w = y - c * v
            u = z - c * y
            q = q + fold(w * w)
            s = s + fold(w * u)
            t = t + fold(v * u)
    for index, value in enumerate((m0, m1, q, s, t, c)):
        value = jnp.sum(value, keepdims=True) if value.shape[0] > 1 else value
        sums[index : index + 1, :] = jnp.broadcast_to(value, (1, sums.shape[1]))


def face_kernel(far, far_in, far_early_in, image, own_sums, sums):
    slab, even = place()
    total, columns = far.shape[1:]
    half = total // 2
    beyond = beyond_far()
    c = own_sums[SUMS : SUMS + 1, 0:1]
    s = jnp.zeros((8, columns), jnp.float32)
    t = s
    for start in range(0, half, ROWS):
        rows = pl.ds(pl.multiple_of(even * half + start, 8), ROWS)
        v = far[1, rows, :]
        y = image[0, rows, :]
        outer_v = far_in[1, rows, :]
        step = v - outer_v
        weight = 0.5 * (far[0, rows, :] + far_in[0, rows, :])
        outer = far_early_in[0, start : start + ROWS, :] - weight * step
        flux = beyond * (weight * (y - outer))
        s = s + fold(((y - c * v) - (outer - c * outer_v)) * flux)
        t = t + fold(step * flux)
    here = lax.broadcasted_iota(jnp.int32, sums.shape[1:], 0) == slab
    added = (None, None, None, s, t)
    for index in range(SUMS):
        value = own_sums[index : index + 1, :]
        if added[index] is not None:
            value = value + jnp.sum(added[index], keepdims=True)
        sums[index] = jnp.where(here, value, 0.0)


def fields_kernel(
    far, near, far_in, near_in, image, far_early_in, far_late_in, near_image_in, potential, near_potential, mask, u1, u2, u3
):
    _, even = place()
    total = far.shape[1]
    scale = 0.25 / lax.axis_size("pos")
    half = total // 2
    beyond_end = beyond_far()
    sides = ((far, even, far_in), (near, 1 - even, near_in))
    for side, (own, layer, halo) in enumerate(sides):
        other = (near, far)[side]
        for start in range(0, total, ROWS):
            rows = slice(start, start + ROWS)
            if own is far:
                piece = slice(start % half, start % half + ROWS)
                early = even == start // half
                part = jnp.where(early, far_early_in[0, piece, :], far_late_in[0, piece, :])
                weight = 0.5 * (far[0, rows, :] + far_in[0, rows, :])
                image_in = beyond_end * (part - weight * (far[1, rows, :] - far_in[1, rows, :]))
                potential_in = far_late_in[0, half + start : half + start + ROWS, :]
            else:
                image_in = near_image_in[0, rows, :]
                potential_in = near_potential[0, rows, :]
            slopes = []
            for ref, index, beyond, inner in (
                (potential, layer, potential_in, potential[1 - layer, rows, :]),
                (own, 1, halo[1, rows, :], other[1, rows, :]),
                (image, side, image_in, image[1 - side, rows, :]),
            ):
                field = ref[index, rows, :]
                slopes.append(
                    (
                        beyond - inner,
                        turn(field, -1) - turn(field, 1),
                        shifted(ref, index, start, 1) - shifted(ref, index, start, -1),
                    )
                )
            weight = scale * (mask[layer, rows, :].astype(jnp.float32) * own[0, rows, :])
            g = [weight * slope for slope in slopes[0]]
            for out, factor, slope in ((u1, 1.0, slopes[1]), (u2, 1.0, slopes[2]), (u3, 0.5, slopes[0])):
                out[layer, rows, :] = factor * (g[0] * slope[0] + g[1] * slope[1] + g[2] * slope[2])


def coefficients(sums):
    m0_d, m1_d, q_d, s_d, t_d = (sums[i] for i in range(SUMS))
    m0 = jnp.sum(m0_d, axis=0, keepdims=True)
    m1 = jnp.sum(m1_d, axis=0, keepdims=True)
    c = m1 / m0
    delta = jnp.where(m0_d > 0, m1_d / m0_d, 0.0) - c
    ww = jnp.sum(q_d + delta * delta * m0_d, axis=0, keepdims=True)
    waw = jnp.sum(s_d + delta * (q_d + t_d) + delta * delta * m1_d, axis=0, keepdims=True)
    alpha0 = m0 / m1
    beta = alpha0 * (ww * alpha0 / m0)
    divisor = waw - ww * (ww / m1)
    alpha1 = jnp.where(divisor == 0, 0.0, ww / divisor)
    return (alpha0 + alpha1 * (1.0 + beta))[:, 0:1], (-alpha1 * alpha0)[:, 0:1]


def term_kernel(sums, u1, u2, u3, *terms):
    a, b = coefficients(sums)
    for term, first in zip(terms, first_rows(u1.shape[1])):
        for layer in range(2):
            for start in range(0, term.shape[1], ROWS):
                rows = slice(first + start, first + start + ROWS)
                term[layer, start : start + ROWS, :] = (
                    a * u1[layer, rows, :] + b * u2[layer, rows, :] + u3[layer, rows, :]
                )


def adjoint_kernel(sums, far, near, image, adjoint, held, sem):
    _, even = place()
    a, b = coefficients(sums)
    for side, (own, layer) in enumerate(((far, even), (near, 1 - even))):
        for start in range(0, far.shape[1], ROWS):
            rows = slice(start, start + ROWS)
            held[layer, rows, :] = a * own[1, rows, :] + b * image[side, rows, :]
    copy = pltpu.make_async_copy(held, adjoint, sem)
    copy.start()
    copy.wait()


def in_hbm(x):
    return pltpu.with_memory_space_constraint(x, pltpu.HBM)


def first_rows(total):
    return [total // 8 * sum(EIGHTHS[:i]) for i in range(len(EIGHTHS))]


def close_kernel(start, total, arrived, *rest):
    gradient, held, sem = rest[-3:]
    held[...] = total[...] + arrived[...]
    copy = pltpu.make_async_copy(held, gradient.at[:, pl.ds(start, total.shape[1]), :], sem)
    copy.start()
    copy.wait()


def pairs(size, first):
    out = []
    for i in range(first, size - 1, 2):
        out += [(i, i + 1), (i + 1, i)]
    return out


def gather_sums(sums, fields, slabs):
    steps = [2**k for k in range(2, slabs.bit_length() - 1)] + [1]
    for step in steps:
        arrived = lax.ppermute(sums, "slab", [(i, i ^ step) for i in range(slabs)])
        if step == steps[-2]:
            arrived, *fields = lax.optimization_barrier((arrived, *fields))
        sums = sums + arrived
    return sums, fields


def partners(step, positions, slabs):
    bits = positions.bit_length() - 1
    route = []
    for p in range(positions):
        for s in range(slabs):
            bit = step if s % 2 == 0 else bits - 1 - step
            route.append((p * slabs + s, (p ^ (1 << bit)) * slabs + s))
    return route


def sum_positions(term, positions, slabs):
    arrived = lax.ppermute(term, ("pos", "slab"), partners(0, positions, slabs))
    for step in range(1, positions.bit_length() - 1):
        term = term + arrived
        arrived = lax.ppermute(term, ("pos", "slab"), partners(step, positions, slabs))
    return term, arrived


def local(labels, magnet_mask, reluctivity, rotor_shift, potential, adjoint_load):
    layers, radial, angular = labels.shape
    positions, slabs = lax.axis_size("pos"), lax.axis_size("slab")
    if layers != 2 or slabs < 8 or slabs & (slabs - 1) or radial % (8 * ROWS) or positions < 2 or positions & (positions - 1):
        raise ValueError("unsupported sizes")
    potential, load = potential[0], adjoint_load[0]
    f32 = functools.partial(jax.ShapeDtypeStruct, dtype=jnp.float32)
    plane = (radial, angular)
    vmem = pl.BlockSpec(memory_space=VMEM)
    smem = pl.BlockSpec(memory_space=SMEM)
    hbm = pl.BlockSpec(memory_space=pltpu.HBM)
    far, near, far_potential, near_potential = pl.pallas_call(
        open_kernel,
        out_shape=tuple(pltpu.VMEM((k,) + plane, jnp.float32) for k in (2, 2, 1, 1)),
        in_specs=[hbm, smem, hbm, hbm, hbm],
        out_specs=(vmem,) * 4,
        scratch_shapes=[
            VMEM((2,) + plane, jnp.int32),
            SMEM(reluctivity.shape, jnp.float32),
            pltpu.SemaphoreType.DMA((7,)),
        ],
        compiler_params=params(),
        name="open",
    )(in_hbm(reluctivity), rotor_shift, in_hbm(labels), in_hbm(load), in_hbm(potential))
    far_in = lax.ppermute(far, "slab", pairs(slabs, 1))
    near_in = lax.ppermute(near, "slab", pairs(slabs, 0))
    half = radial // 2
    far_part, near_part, far_early, far_late = pl.pallas_call(
        part_kernel,
        out_shape=tuple(pltpu.VMEM((1, rows, angular), jnp.float32) for rows in (radial, radial, half, half + radial)),
        in_specs=[vmem] * 3,
        out_specs=(vmem,) * 4,
        compiler_params=params(),
        name="part",
    )(far, near, far_potential)
    far_early_in = lax.ppermute(far_early, "slab", pairs(slabs, 1))
    near_part_in = lax.ppermute(near_part, "slab", pairs(slabs, 0))
    far_late_in = lax.ppermute(far_late, "slab", pairs(slabs, 1))
    image, near_image_in, own_sums = pl.pallas_call(
        sums_kernel,
        out_shape=(f32((2,) + plane), f32((1,) + plane), f32((8, 128))),
        in_specs=[vmem] * 7,
        out_specs=(vmem,) * 3,
        compiler_params=params(),
        name="sums",
    )(far, near, far_part, near_part, far_in, near_in, near_part_in)
    sums = pl.pallas_call(
        face_kernel,
        out_shape=f32((SUMS, slabs, 128)),
        in_specs=[vmem] * 5,
        out_specs=vmem,
        compiler_params=params(),
        name="face",
    )(far, far_in, far_early_in, image, own_sums)
    arrived = lax.ppermute(sums, "slab", [(i, i ^ 2) for i in range(slabs)])
    near_potential, arrived = lax.optimization_barrier((near_potential, arrived))
    near_potential = lax.ppermute(near_potential, "slab", pairs(slabs, 0))
    sums = sums + arrived
    fields = pl.pallas_call(
        fields_kernel,
        out_shape=(f32((2,) + plane),) * 3,
        in_specs=[vmem] * 11,
        out_specs=(vmem,) * 3,
        compiler_params=params(),
        name="fields",
    )(far, near, far_in, near_in, image, far_early_in, far_late_in, near_image_in, potential, near_potential, magnet_mask)
    sums, fields = gather_sums(sums, fields, slabs)
    spans = [radial // 8 * k for k in EIGHTHS]
    terms = pl.pallas_call(
        term_kernel,
        out_shape=tuple(f32((2, span, angular)) for span in spans),
        in_specs=[vmem] * 4,
        out_specs=(vmem,) * len(spans),
        compiler_params=params(),
        name="term",
    )(sums, *fields)
    adjoint = pl.pallas_call(
        adjoint_kernel,
        out_shape=pltpu.HBM((2,) + plane, jnp.float32),
        in_specs=[vmem] * 4,
        out_specs=hbm,
        scratch_shapes=[VMEM((2,) + plane, jnp.float32), pltpu.SemaphoreType.DMA(())],
        compiler_params=params(),
        name="adjoint",
    )(sums, far, near, image)
    gradient = ()
    for index, term in enumerate(terms):
        total, arrived = sum_positions(term, positions, slabs)
        gradient = pl.pallas_call(
            functools.partial(close_kernel, first_rows(radial)[index]),
            out_shape=pltpu.HBM((2,) + plane, jnp.float32),
            in_specs=[vmem] * 2 + [hbm] * (index > 0),
            out_specs=hbm,
            scratch_shapes=[VMEM(term.shape, jnp.float32), pltpu.SemaphoreType.DMA(())],
            input_output_aliases={2: 0} if index else {},
            compiler_params=params(),
            name="close",
        )(total, arrived, *((gradient,) if index else ()))
    return gradient, adjoint[None]


def solution(mesh):
    return jax.shard_map(
        local,
        mesh=mesh,
        in_specs=(
            P("slab", None, None),
            P("slab", None, None),
            P(),
            P("pos"),
            P("pos", "slab", None, None),
            P("pos", "slab", None, None),
        ),
        out_specs=(P("slab", None, None), P("pos", "slab", None, None)),
        check_vma=False,
    )
```

```python
import functools

import jax
import jax.numpy as jnp
from jax import lax
from jax.experimental import pallas as pl
from jax.experimental.pallas import tpu as pltpu
from jax.sharding import PartitionSpec as P


ROWS = 16
VMEM = pltpu.VMEM
SMEM = pltpu.SMEM
SUMS = 5
EIGHTHS = (3, 3, 2)


def params():
    return pltpu.CompilerParams(vmem_limit_bytes=40 * 1024 * 1024)


def shifted(ref, index, start, offset):
    total, columns = ref.shape[-2:]
    zero = jnp.zeros((1, columns), jnp.float32)
    if start + offset < 0:
        return jnp.concatenate([zero, ref[index, 0 : ROWS - 1, :]], axis=0)
    if start + offset + ROWS > total:
        return jnp.concatenate([ref[index, start + 1 : total, :], zero], axis=0)
    return ref[index, start + offset : start + offset + ROWS, :]


def turn(value, offset):
    return pltpu.roll(value, offset % value.shape[1], 1)


def in_plane(nu_ref, nu_index, ref, index, start):
    nu = nu_ref[nu_index, start : start + ROWS, :]
    v = ref[index, start : start + ROWS, :]
    total = None
    for offset in (-1, 1):
        across = (nu + turn(nu, offset)) * (v - turn(v, offset))
        total = across if total is None else total + across
        total = total + (nu + shifted(nu_ref, nu_index, start, offset)) * (
            v - shifted(ref, index, start, offset)
        )
    return nu, v, total


def beyond_far():
    slab, _ = place()
    inside = (slab > 0) & (slab < lax.axis_size("slab") - 1)
    return jnp.where(inside, 1.0, 0.0).astype(jnp.float32)


def place():
    slab = lax.axis_index("slab")
    return slab, lax.rem(slab, 2)


def open_kernel(reluctivity, shift, labels, load, far, near, held, table, sems):
    _, even = place()
    odd = 1 - even
    total = labels.shape[1]
    moves = (
        (labels.at[even], held.at[0]),
        (labels.at[odd], held.at[1]),
        (load.at[even], far.at[1]),
        (load.at[odd], near.at[1]),
        (reluctivity, table),
    )
    copies = [pltpu.make_async_copy(src, dst, sems.at[i]) for i, (src, dst) in enumerate(moves)]
    for copy in copies:
        copy.start()
    copies[-1].wait()
    r0, r1, r2, r3 = (table[i] for i in range(4))
    offset = shift[0]
    for side, out in enumerate((far, near)):
        copies[side].wait()
        for start in range(0, total, ROWS):
            rows = slice(start, start + ROWS)
            material = held[side, rows, :]
            if start < total // 2:
                material = pltpu.roll(material, offset, 1)
            out[0, rows, :] = jnp.where(
                material < 2,
                jnp.where(material == 0, r0, r1),
                jnp.where(material == 2, r2, r3),
            )
    for copy in copies[2:-1]:
        copy.wait()


def part_kernel(far, near, potential, far_part, near_part, far_early, far_late, near_potential, sems):
    _, even = place()
    total = far.shape[1]
    half = total // 2
    copies = (
        pltpu.make_async_copy(potential.at[even], far_late.at[0, pl.ds(half, total), :], sems.at[0]),
        pltpu.make_async_copy(potential.at[1 - even], near_potential.at[0], sems.at[1]),
    )
    for copy in copies:
        copy.start()
    for own, other, out in ((far, near, far_part), (near, far, near_part)):
        for start in range(0, total, ROWS):
            rows = slice(start, start + ROWS)
            nu, v, total_flux = in_plane(own, 0, own, 1, start)
            total_flux = total_flux + (nu + other[0, rows, :]) * (v - other[1, rows, :])
            out[0, rows, :] = 0.5 * (v + total_flux)
    far_early[0] = far_part[0, pl.ds(pl.multiple_of((1 - even) * half, 8), half), :]
    far_late[0, 0:half, :] = far_part[0, pl.ds(pl.multiple_of(even * half, 8), half), :]
    for copy in copies:
        copy.wait()


def fold(value):
    return jnp.sum(value.reshape(ROWS // 8, 8, value.shape[1]), axis=0)


def sums_kernel(far, near, far_part, near_part, far_in, near_in, near_part_in, image, near_image_in, sums):
    total, columns = far.shape[1:]
    sides = ((far, far_part, far_in), (near, near_part, near_in))
    end = 1.0 - beyond_far()
    nil = jnp.zeros((8, columns), jnp.float32)
    m0, m1 = nil, nil
    for side, (own, part, halo) in enumerate(sides):
        for start in range(0, total, ROWS):
            rows = slice(start, start + ROWS)
            v = own[1, rows, :]
            flux = 0.5 * (own[0, rows, :] + halo[0, rows, :]) * (v - halo[1, rows, :])
            y = part[0, rows, :] + flux
            image[side, rows, :] = y
            if own is near:
                near_image_in[0, rows, :] = near_part_in[0, rows, :] - flux
            m0 = m0 + fold(v * v)
            m1 = m1 + fold(v * y)
    m0 = jnp.sum(m0, keepdims=True)
    m1 = jnp.sum(m1, keepdims=True)
    c = jnp.where(m0 > 0, m1 / m0, 0.0)
    q, s, t = nil, nil, nil
    for side, (own, _, halo) in enumerate(sides):
        for start in range(0, total, ROWS):
            rows = slice(start, start + ROWS)
            nu, y, total_flux = in_plane(own, 0, image, side, start)
            other = (near, far)[side]
            total_flux = total_flux + (nu + other[0, rows, :]) * (y - image[1 - side, rows, :])
            if own is near:
                total_flux = total_flux + (nu + halo[0, rows, :]) * (y - near_image_in[0, rows, :])
            else:
                total_flux = total_flux + end * (nu * y)
            z = 0.5 * (y + total_flux)
            v = own[1, rows, :]
            w = y - c * v
            u = z - c * y
            q = q + fold(w * w)
            s = s + fold(w * u)
            t = t + fold(v * u)
    for index, value in enumerate((m0, m1, q, s, t, c)):
        value = jnp.sum(value, keepdims=True) if value.shape[0] > 1 else value
        sums[index : index + 1, :] = jnp.broadcast_to(value, (1, sums.shape[1]))


def face_kernel(far, far_in, far_early_in, image, own_sums, sums):
    slab, even = place()
    total, columns = far.shape[1:]
    half = total // 2
    beyond = beyond_far()
    c = own_sums[SUMS : SUMS + 1, 0:1]
    s = jnp.zeros((8, columns), jnp.float32)
    t = s
    for start in range(0, half, ROWS):
        rows = pl.ds(pl.multiple_of(even * half + start, 8), ROWS)
        v = far[1, rows, :]
        y = image[0, rows, :]
        outer_v = far_in[1, rows, :]
        step = v - outer_v
        weight = 0.5 * (far[0, rows, :] + far_in[0, rows, :])
        outer = far_early_in[0, start : start + ROWS, :] - weight * step
        flux = beyond * (weight * (y - outer))
        s = s + fold(((y - c * v) - (outer - c * outer_v)) * flux)
        t = t + fold(step * flux)
    here = lax.broadcasted_iota(jnp.int32, sums.shape[1:], 0) == slab
    added = (None, None, None, s, t)
    for index in range(SUMS):
        value = own_sums[index : index + 1, :]
        if added[index] is not None:
            value = value + jnp.sum(added[index], keepdims=True)
        sums[index] = jnp.where(here, value, 0.0)


def fields_kernel(
    far, near, far_in, near_in, image, far_early_in, far_late_in, near_image_in, potential, near_potential, mask, u1, u2, u3
):
    _, even = place()
    total = far.shape[1]
    scale = 0.25 / lax.axis_size("pos")
    half = total // 2
    beyond_end = beyond_far()
    sides = ((far, even, far_in), (near, 1 - even, near_in))
    for side, (own, layer, halo) in enumerate(sides):
        other = (near, far)[side]
        for start in range(0, total, ROWS):
            rows = slice(start, start + ROWS)
            if own is far:
                piece = slice(start % half, start % half + ROWS)
                early = even == start // half
                part = jnp.where(early, far_early_in[0, piece, :], far_late_in[0, piece, :])
                weight = 0.5 * (far[0, rows, :] + far_in[0, rows, :])
                image_in = beyond_end * (part - weight * (far[1, rows, :] - far_in[1, rows, :]))
                potential_in = far_late_in[0, half + start : half + start + ROWS, :]
            else:
                image_in = near_image_in[0, rows, :]
                potential_in = near_potential[0, rows, :]
            slopes = []
            for ref, index, beyond, inner in (
                (potential, layer, potential_in, potential[1 - layer, rows, :]),
                (own, 1, halo[1, rows, :], other[1, rows, :]),
                (image, side, image_in, image[1 - side, rows, :]),
            ):
                field = ref[index, rows, :]
                slopes.append(
                    (
                        beyond - inner,
                        turn(field, -1) - turn(field, 1),
                        shifted(ref, index, start, 1) - shifted(ref, index, start, -1),
                    )
                )
            weight = scale * (mask[layer, rows, :].astype(jnp.float32) * own[0, rows, :])
            g = [weight * slope for slope in slopes[0]]
            for out, factor, slope in ((u1, 1.0, slopes[1]), (u2, 1.0, slopes[2]), (u3, 0.5, slopes[0])):
                out[layer, rows, :] = factor * (g[0] * slope[0] + g[1] * slope[1] + g[2] * slope[2])


def coefficients(sums):
    m0_d, m1_d, q_d, s_d, t_d = (sums[i] for i in range(SUMS))
    m0 = jnp.sum(m0_d, axis=0, keepdims=True)
    m1 = jnp.sum(m1_d, axis=0, keepdims=True)
    c = m1 / m0
    delta = jnp.where(m0_d > 0, m1_d / m0_d, 0.0) - c
    ww = jnp.sum(q_d + delta * delta * m0_d, axis=0, keepdims=True)
    waw = jnp.sum(s_d + delta * (q_d + t_d) + delta * delta * m1_d, axis=0, keepdims=True)
    alpha0 = m0 / m1
    beta = alpha0 * (ww * alpha0 / m0)
    divisor = waw - ww * (ww / m1)
    alpha1 = jnp.where(divisor == 0, 0.0, ww / divisor)
    return (alpha0 + alpha1 * (1.0 + beta))[:, 0:1], (-alpha1 * alpha0)[:, 0:1]


def term_kernel(sums, u1, u2, u3, *terms):
    a, b = coefficients(sums)
    for term, first in zip(terms, first_rows(u1.shape[1])):
        for layer in range(2):
            for start in range(0, term.shape[1], ROWS):
                rows = slice(first + start, first + start + ROWS)
                term[layer, start : start + ROWS, :] = (
                    a * u1[layer, rows, :] + b * u2[layer, rows, :] + u3[layer, rows, :]
                )


def adjoint_kernel(sums, far, near, image, adjoint, held, sem):
    _, even = place()
    a, b = coefficients(sums)
    for side, (own, layer) in enumerate(((far, even), (near, 1 - even))):
        for start in range(0, far.shape[1], ROWS):
            rows = slice(start, start + ROWS)
            held[layer, rows, :] = a * own[1, rows, :] + b * image[side, rows, :]
    copy = pltpu.make_async_copy(held, adjoint, sem)
    copy.start()
    copy.wait()


def in_hbm(x):
    return pltpu.with_memory_space_constraint(x, pltpu.HBM)


def first_rows(total):
    return [total // 8 * sum(EIGHTHS[:i]) for i in range(len(EIGHTHS))]


def close_kernel(start, total, arrived, *rest):
    gradient, held, sem = rest[-3:]
    held[...] = total[...] + arrived[...]
    copy = pltpu.make_async_copy(held, gradient.at[:, pl.ds(start, total.shape[1]), :], sem)
    copy.start()
    copy.wait()


def pairs(size, first):
    out = []
    for i in range(first, size - 1, 2):
        out += [(i, i + 1), (i + 1, i)]
    return out


def gather_sums(sums, fields, slabs):
    steps = [2**k for k in range(2, slabs.bit_length() - 1)] + [1]
    for step in steps:
        arrived = lax.ppermute(sums, "slab", [(i, i ^ step) for i in range(slabs)])
        if step == steps[-2]:
            arrived, *fields = lax.optimization_barrier((arrived, *fields))
        sums = sums + arrived
    return sums, fields


def partners(step, positions, slabs):
    bits = positions.bit_length() - 1
    route = []
    for p in range(positions):
        for s in range(slabs):
            bit = step if s % 2 == 0 else bits - 1 - step
            route.append((p * slabs + s, (p ^ (1 << bit)) * slabs + s))
    return route


def sum_positions(term, positions, slabs):
    arrived = lax.ppermute(term, ("pos", "slab"), partners(0, positions, slabs))
    for step in range(1, positions.bit_length() - 1):
        term = term + arrived
        arrived = lax.ppermute(term, ("pos", "slab"), partners(step, positions, slabs))
    return term, arrived


def local(labels, magnet_mask, reluctivity, rotor_shift, potential, adjoint_load):
    layers, radial, angular = labels.shape
    positions, slabs = lax.axis_size("pos"), lax.axis_size("slab")
    if layers != 2 or slabs < 8 or slabs & (slabs - 1) or radial % (8 * ROWS) or positions < 2 or positions & (positions - 1):
        raise ValueError("unsupported sizes")
    potential, load = potential[0], adjoint_load[0]
    f32 = functools.partial(jax.ShapeDtypeStruct, dtype=jnp.float32)
    plane = (radial, angular)
    vmem = pl.BlockSpec(memory_space=VMEM)
    smem = pl.BlockSpec(memory_space=SMEM)
    hbm = pl.BlockSpec(memory_space=pltpu.HBM)
    far, near = pl.pallas_call(
        open_kernel,
        out_shape=tuple(pltpu.VMEM((k,) + plane, jnp.float32) for k in (2, 2)),
        in_specs=[hbm, smem, hbm, hbm],
        out_specs=(vmem,) * 2,
        scratch_shapes=[
            VMEM((2,) + plane, jnp.int32),
            SMEM(reluctivity.shape, jnp.float32),
            pltpu.SemaphoreType.DMA((5,)),
        ],
        compiler_params=params(),
        name="open",
    )(in_hbm(reluctivity), rotor_shift, in_hbm(labels), in_hbm(load))
    far_in = lax.ppermute(far, "slab", pairs(slabs, 1))
    near_in = lax.ppermute(near, "slab", pairs(slabs, 0))
    half = radial // 2
    far_part, near_part, far_early, far_late, near_potential = pl.pallas_call(
        part_kernel,
        out_shape=tuple(pltpu.VMEM((1, rows, angular), jnp.float32) for rows in (radial, radial, half, half + radial, radial)),
        in_specs=[vmem, vmem, hbm],
        out_specs=(vmem,) * 5,
        scratch_shapes=[pltpu.SemaphoreType.DMA((2,))],
        compiler_params=params(),
        name="part",
    )(far, near, in_hbm(potential))
    far_early_in = lax.ppermute(far_early, "slab", pairs(slabs, 1))
    near_part_in = lax.ppermute(near_part, "slab", pairs(slabs, 0))
    far_late_in = lax.ppermute(far_late, "slab", pairs(slabs, 1))
    image, near_image_in, own_sums = pl.pallas_call(
        sums_kernel,
        out_shape=(f32((2,) + plane), f32((1,) + plane), f32((8, 128))),
        in_specs=[vmem] * 7,
        out_specs=(vmem,) * 3,
        compiler_params=params(),
        name="sums",
    )(far, near, far_part, near_part, far_in, near_in, near_part_in)
    sums = pl.pallas_call(
        face_kernel,
        out_shape=f32((SUMS, slabs, 128)),
        in_specs=[vmem] * 5,
        out_specs=vmem,
        compiler_params=params(),
        name="face",
    )(far, far_in, far_early_in, image, own_sums)
    arrived = lax.ppermute(sums, "slab", [(i, i ^ 2) for i in range(slabs)])
    near_potential, arrived = lax.optimization_barrier((near_potential, arrived))
    near_potential = lax.ppermute(near_potential, "slab", pairs(slabs, 0))
    sums = sums + arrived
    fields = pl.pallas_call(
        fields_kernel,
        out_shape=(f32((2,) + plane),) * 3,
        in_specs=[vmem] * 11,
        out_specs=(vmem,) * 3,
        compiler_params=params(),
        name="fields",
    )(far, near, far_in, near_in, image, far_early_in, far_late_in, near_image_in, potential, near_potential, magnet_mask)
    sums, fields = gather_sums(sums, fields, slabs)
    spans = [radial // 8 * k for k in EIGHTHS]
    terms = pl.pallas_call(
        term_kernel,
        out_shape=tuple(f32((2, span, angular)) for span in spans),
        in_specs=[vmem] * 4,
        out_specs=(vmem,) * len(spans),
        compiler_params=params(),
        name="term",
    )(sums, *fields)
    adjoint = pl.pallas_call(
        adjoint_kernel,
        out_shape=pltpu.HBM((2,) + plane, jnp.float32),
        in_specs=[vmem] * 4,
        out_specs=hbm,
        scratch_shapes=[VMEM((2,) + plane, jnp.float32), pltpu.SemaphoreType.DMA(())],
        compiler_params=params(),
        name="adjoint",
    )(sums, far, near, image)
    gradient = ()
    for index, term in enumerate(terms):
        total, arrived = sum_positions(term, positions, slabs)
        if index == len(terms) - 1:
            gradient = lax.dynamic_update_slice(gradient, total + arrived, (0, first_rows(radial)[index], 0))
            break
        gradient = pl.pallas_call(
            functools.partial(close_kernel, first_rows(radial)[index]),
            out_shape=pltpu.HBM((2,) + plane, jnp.float32),
            in_specs=[vmem] * 2 + [hbm] * (index > 0),
            out_specs=hbm,
            scratch_shapes=[VMEM(term.shape, jnp.float32), pltpu.SemaphoreType.DMA(())],
            input_output_aliases={2: 0} if index else {},
            compiler_params=params(),
            name="close",
        )(total, arrived, *((gradient,) if index else ()))
    return gradient, adjoint[None]


def solution(mesh):
    return jax.shard_map(
        local,
        mesh=mesh,
        in_specs=(
            P("slab", None, None),
            P("slab", None, None),
            P(),
            P("pos"),
            P("pos", "slab", None, None),
            P("pos", "slab", None, None),
        ),
        out_specs=(P("slab", None, None), P("pos", "slab", None, None)),
        check_vma=False,
    )
```

```python
import functools

import jax
import jax.numpy as jnp
from jax import lax
from jax.experimental import pallas as pl
from jax.experimental.pallas import tpu as pltpu
from jax.sharding import PartitionSpec as P


ROWS = 16
VMEM = pltpu.VMEM
SMEM = pltpu.SMEM
SUMS = 5
EIGHTHS = (3, 3, 2)


def params():
    return pltpu.CompilerParams(vmem_limit_bytes=40 * 1024 * 1024)


def shifted(ref, index, start, offset):
    total, columns = ref.shape[-2:]
    zero = jnp.zeros((1, columns), jnp.float32)
    if start + offset < 0:
        return jnp.concatenate([zero, ref[index, 0 : ROWS - 1, :]], axis=0)
    if start + offset + ROWS > total:
        return jnp.concatenate([ref[index, start + 1 : total, :], zero], axis=0)
    return ref[index, start + offset : start + offset + ROWS, :]


def turn(value, offset):
    return pltpu.roll(value, offset % value.shape[1], 1)


def in_plane(nu_ref, nu_index, ref, index, start):
    nu = nu_ref[nu_index, start : start + ROWS, :]
    v = ref[index, start : start + ROWS, :]
    total = None
    for offset in (-1, 1):
        across = (nu + turn(nu, offset)) * (v - turn(v, offset))
        total = across if total is None else total + across
        total = total + (nu + shifted(nu_ref, nu_index, start, offset)) * (
            v - shifted(ref, index, start, offset)
        )
    return nu, v, total


def beyond_far():
    slab, _ = place()
    inside = (slab > 0) & (slab < lax.axis_size("slab") - 1)
    return jnp.where(inside, 1.0, 0.0).astype(jnp.float32)


def place():
    slab = lax.axis_index("slab")
    return slab, lax.rem(slab, 2)


def open_kernel(reluctivity, shift, labels, load, potential, far, near, far_potential, near_potential, held, table, sems):
    _, even = place()
    odd = 1 - even
    total = labels.shape[1]
    moves = (
        (labels.at[even], held.at[0]),
        (labels.at[odd], held.at[1]),
        (load.at[even], far.at[1]),
        (load.at[odd], near.at[1]),
        (potential.at[even], far_potential.at[0]),
        (potential.at[odd], near_potential.at[0]),
        (reluctivity, table),
    )
    copies = [pltpu.make_async_copy(src, dst, sems.at[i]) for i, (src, dst) in enumerate(moves)]
    for copy in copies:
        copy.start()
    copies[-1].wait()
    r0, r1, r2, r3 = (table[i] for i in range(4))
    offset = shift[0]
    for side, out in enumerate((far, near)):
        copies[side].wait()
        for start in range(0, total, ROWS):
            rows = slice(start, start + ROWS)
            material = held[side, rows, :]
            if start < total // 2:
                material = pltpu.roll(material, offset, 1)
            out[0, rows, :] = jnp.where(
                material < 2,
                jnp.where(material == 0, r0, r1),
                jnp.where(material == 2, r2, r3),
            )
    for copy in copies[2:-1]:
        copy.wait()


def part_kernel(far, near, far_potential, far_part, near_part, far_early, far_late):
    _, even = place()
    total = far.shape[1]
    half = total // 2
    for own, other, out in ((far, near, far_part), (near, far, near_part)):
        for start in range(0, total, ROWS):
            rows = slice(start, start + ROWS)
            nu, v, total_flux = in_plane(own, 0, own, 1, start)
            total_flux = total_flux + (nu + other[0, rows, :]) * (v - other[1, rows, :])
            out[0, rows, :] = 0.5 * (v + total_flux)
    far_early[0] = far_part[0, pl.ds(pl.multiple_of((1 - even) * half, 8), half), :]
    far_late[0, 0:half, :] = far_part[0, pl.ds(pl.multiple_of(even * half, 8), half), :]
    far_late[0, half : half + total, :] = far_potential[0]


def fold(value):
    return jnp.sum(value.reshape(ROWS // 8, 8, value.shape[1]), axis=0)


def sums_kernel(far, near, far_part, near_part, far_in, near_in, near_part_in, image, near_image_in, sums):
    total, columns = far.shape[1:]
    sides = ((far, far_part, far_in), (near, near_part, near_in))
    end = 1.0 - beyond_far()
    nil = jnp.zeros((8, columns), jnp.float32)
    m0, m1 = nil, nil
    for side, (own, part, halo) in enumerate(sides):
        for start in range(0, total, ROWS):
            rows = slice(start, start + ROWS)
            v = own[1, rows, :]
            flux = 0.5 * (own[0, rows, :] + halo[0, rows, :]) * (v - halo[1, rows, :])
            y = part[0, rows, :] + flux
            image[side, rows, :] = y
            if own is near:
                near_image_in[0, rows, :] = near_part_in[0, rows, :] - flux
            m0 = m0 + fold(v * v)
            m1 = m1 + fold(v * y)
    m0 = jnp.sum(m0, keepdims=True)
    m1 = jnp.sum(m1, keepdims=True)
    c = jnp.where(m0 > 0, m1 / m0, 0.0)
    q, s, t = nil, nil, nil
    for side, (own, _, halo) in enumerate(sides):
        for start in range(0, total, ROWS):
            rows = slice(start, start + ROWS)
            nu, y, total_flux = in_plane(own, 0, image, side, start)
            other = (near, far)[side]
            total_flux = total_flux + (nu + other[0, rows, :]) * (y - image[1 - side, rows, :])
            if own is near:
                total_flux = total_flux + (nu + halo[0, rows, :]) * (y - near_image_in[0, rows, :])
            else:
                total_flux = total_flux + end * (nu * y)
            z = 0.5 * (y + total_flux)
            v = own[1, rows, :]
            w = y - c * v
            u = z - c * y
            q = q + fold(w * w)
            s = s + fold(w * u)
            t = t + fold(v * u)
    for index, value in enumerate((m0, m1, q, s, t, c)):
        value = jnp.sum(value, keepdims=True) if value.shape[0] > 1 else value
        sums[index : index + 1, :] = jnp.broadcast_to(value, (1, sums.shape[1]))


def face_kernel(far, far_in, far_early_in, image, own_sums, sums):
    slab, even = place()
    total, columns = far.shape[1:]
    half = total // 2
    beyond = beyond_far()
    c = own_sums[SUMS : SUMS + 1, 0:1]
    s = jnp.zeros((8, columns), jnp.float32)
    t = s
    for start in range(0, half, ROWS):
        rows = pl.ds(pl.multiple_of(even * half + start, 8), ROWS)
        v = far[1, rows, :]
        y = image[0, rows, :]
        outer_v = far_in[1, rows, :]
        step = v - outer_v
        weight = 0.5 * (far[0, rows, :] + far_in[0, rows, :])
        outer = far_early_in[0, start : start + ROWS, :] - weight * step
        flux = beyond * (weight * (y - outer))
        s = s + fold(((y - c * v) - (outer - c * outer_v)) * flux)
        t = t + fold(step * flux)
    here = lax.broadcasted_iota(jnp.int32, sums.shape[1:], 0) == slab
    added = (None, None, None, s, t)
    for index in range(SUMS):
        value = own_sums[index : index + 1, :]
        if added[index] is not None:
            value = value + jnp.sum(added[index], keepdims=True)
        sums[index] = jnp.where(here, value, 0.0)


def fields_kernel(
    far, near, far_in, near_in, image, far_early_in, far_late_in, near_image_in, potential, near_potential, mask, u1, u2, u3
):
    _, even = place()
    total = far.shape[1]
    scale = 0.25 / lax.axis_size("pos")
    half = total // 2
    beyond_end = beyond_far()
    sides = ((far, even, far_in), (near, 1 - even, near_in))
    for side, (own, layer, halo) in enumerate(sides):
        other = (near, far)[side]
        for start in range(0, total, ROWS):
            rows = slice(start, start + ROWS)
            if own is far:
                piece = slice(start % half, start % half + ROWS)
                early = even == start // half
                part = jnp.where(early, far_early_in[0, piece, :], far_late_in[0, piece, :])
                weight = 0.5 * (far[0, rows, :] + far_in[0, rows, :])
                image_in = beyond_end * (part - weight * (far[1, rows, :] - far_in[1, rows, :]))
                potential_in = far_late_in[0, half + start : half + start + ROWS, :]
            else:
                image_in = near_image_in[0, rows, :]
                potential_in = near_potential[0, rows, :]
            slopes = []
            for ref, index, beyond, inner in (
                (potential, layer, potential_in, potential[1 - layer, rows, :]),
                (own, 1, halo[1, rows, :], other[1, rows, :]),
                (image, side, image_in, image[1 - side, rows, :]),
            ):
                field = ref[index, rows, :]
                slopes.append(
                    (
                        beyond - inner,
                        turn(field, -1) - turn(field, 1),
                        shifted(ref, index, start, 1) - shifted(ref, index, start, -1),
                    )
                )
            weight = scale * (mask[layer, rows, :].astype(jnp.float32) * own[0, rows, :])
            g = [weight * slope for slope in slopes[0]]
            for out, factor, slope in ((u1, 1.0, slopes[1]), (u2, 1.0, slopes[2]), (u3, 0.5, slopes[0])):
                out[layer, rows, :] = factor * (g[0] * slope[0] + g[1] * slope[1] + g[2] * slope[2])


def coefficients(sums):
    m0_d, m1_d, q_d, s_d, t_d = (sums[i] for i in range(SUMS))
    m0 = jnp.sum(m0_d, axis=0, keepdims=True)
    m1 = jnp.sum(m1_d, axis=0, keepdims=True)
    c = m1 / m0
    delta = jnp.where(m0_d > 0, m1_d / m0_d, 0.0) - c
    ww = jnp.sum(q_d + delta * delta * m0_d, axis=0, keepdims=True)
    waw = jnp.sum(s_d + delta * (q_d + t_d) + delta * delta * m1_d, axis=0, keepdims=True)
    alpha0 = m0 / m1
    beta = alpha0 * (ww * alpha0 / m0)
    divisor = waw - ww * (ww / m1)
    alpha1 = jnp.where(divisor == 0, 0.0, ww / divisor)
    return (alpha0 + alpha1 * (1.0 + beta))[:, 0:1], (-alpha1 * alpha0)[:, 0:1]


def term_kernel(sums, u1, u2, u3, *terms):
    a, b = coefficients(sums)
    for term, first in zip(terms, first_rows(u1.shape[1])):
        for layer in range(2):
            for start in range(0, term.shape[1], ROWS):
                rows = slice(first + start, first + start + ROWS)
                term[layer, start : start + ROWS, :] = (
                    a * u1[layer, rows, :] + b * u2[layer, rows, :] + u3[layer, rows, :]
                )


def adjoint_kernel(sums, far, near, image, adjoint, held, sem):
    _, even = place()
    a, b = coefficients(sums)
    for side, (own, layer) in enumerate(((far, even), (near, 1 - even))):
        for start in range(0, far.shape[1], ROWS):
            rows = slice(start, start + ROWS)
            held[layer, rows, :] = a * own[1, rows, :] + b * image[side, rows, :]
    copy = pltpu.make_async_copy(held, adjoint, sem)
    copy.start()
    copy.wait()


def in_hbm(x):
    return pltpu.with_memory_space_constraint(x, pltpu.HBM)


def first_rows(total):
    return [total // 8 * sum(EIGHTHS[:i]) for i in range(len(EIGHTHS))]


def close_kernel(start, total, arrived, *rest):
    gradient, held, sem = rest[-3:]
    held[...] = total[...] + arrived[...]
    copy = pltpu.make_async_copy(held, gradient.at[:, pl.ds(start, total.shape[1]), :], sem)
    copy.start()
    copy.wait()


def pairs(size, first):
    out = []
    for i in range(first, size - 1, 2):
        out += [(i, i + 1), (i + 1, i)]
    return out


def gather_sums(sums, fields, slabs):
    steps = [2**k for k in range(2, slabs.bit_length() - 1)] + [1]
    for step in steps:
        arrived = lax.ppermute(sums, "slab", [(i, i ^ step) for i in range(slabs)])
        if step == steps[-2]:
            arrived, *fields = lax.optimization_barrier((arrived, *fields))
        sums = sums + arrived
    return sums, fields


def partners(step, positions, slabs):
    bits = positions.bit_length() - 1
    route = []
    for p in range(positions):
        for s in range(slabs):
            bit = step if s % 2 == 1 else bits - 1 - step
            route.append((p * slabs + s, (p ^ (1 << bit)) * slabs + s))
    return route


def sum_positions(term, positions, slabs):
    arrived = lax.ppermute(term, ("pos", "slab"), partners(0, positions, slabs))
    for step in range(1, positions.bit_length() - 1):
        term = term + arrived
        arrived = lax.ppermute(term, ("pos", "slab"), partners(step, positions, slabs))
    return term, arrived


def local(labels, magnet_mask, reluctivity, rotor_shift, potential, adjoint_load):
    layers, radial, angular = labels.shape
    positions, slabs = lax.axis_size("pos"), lax.axis_size("slab")
    if layers != 2 or slabs < 8 or slabs & (slabs - 1) or radial % (8 * ROWS) or positions < 2 or positions & (positions - 1):
        raise ValueError("unsupported sizes")
    potential, load = potential[0], adjoint_load[0]
    f32 = functools.partial(jax.ShapeDtypeStruct, dtype=jnp.float32)
    plane = (radial, angular)
    vmem = pl.BlockSpec(memory_space=VMEM)
    smem = pl.BlockSpec(memory_space=SMEM)
    hbm = pl.BlockSpec(memory_space=pltpu.HBM)
    far, near, far_potential, near_potential = pl.pallas_call(
        open_kernel,
        out_shape=tuple(pltpu.VMEM((k,) + plane, jnp.float32) for k in (2, 2, 1, 1)),
        in_specs=[hbm, smem, hbm, hbm, hbm],
        out_specs=(vmem,) * 4,
        scratch_shapes=[
            VMEM((2,) + plane, jnp.int32),
            SMEM(reluctivity.shape, jnp.float32),
            pltpu.SemaphoreType.DMA((7,)),
        ],
        compiler_params=params(),
        name="open",
    )(in_hbm(reluctivity), rotor_shift, in_hbm(labels), in_hbm(load), in_hbm(potential))
    far_in = lax.ppermute(far, "slab", pairs(slabs, 1))
    near_in = lax.ppermute(near, "slab", pairs(slabs, 0))
    half = radial // 2
    far_part, near_part, far_early, far_late = pl.pallas_call(
        part_kernel,
        out_shape=tuple(pltpu.VMEM((1, rows, angular), jnp.float32) for rows in (radial, radial, half, half + radial)),
        in_specs=[vmem] * 3,
        out_specs=(vmem,) * 4,
        compiler_params=params(),
        name="part",
    )(far, near, far_potential)
    far_early_in = lax.ppermute(far_early, "slab", pairs(slabs, 1))
    near_part_in = lax.ppermute(near_part, "slab", pairs(slabs, 0))
    far_late_in = lax.ppermute(far_late, "slab", pairs(slabs, 1))
    image, near_image_in, own_sums = pl.pallas_call(
        sums_kernel,
        out_shape=(f32((2,) + plane), f32((1,) + plane), f32((8, 128))),
        in_specs=[vmem] * 7,
        out_specs=(vmem,) * 3,
        compiler_params=params(),
        name="sums",
    )(far, near, far_part, near_part, far_in, near_in, near_part_in)
    sums = pl.pallas_call(
        face_kernel,
        out_shape=f32((SUMS, slabs, 128)),
        in_specs=[vmem] * 5,
        out_specs=vmem,
        compiler_params=params(),
        name="face",
    )(far, far_in, far_early_in, image, own_sums)
    arrived = lax.ppermute(sums, "slab", [(i, i ^ 2) for i in range(slabs)])
    near_potential, arrived = lax.optimization_barrier((near_potential, arrived))
    near_potential = lax.ppermute(near_potential, "slab", pairs(slabs, 0))
    sums = sums + arrived
    fields = pl.pallas_call(
        fields_kernel,
        out_shape=(f32((2,) + plane),) * 3,
        in_specs=[vmem] * 11,
        out_specs=(vmem,) * 3,
        compiler_params=params(),
        name="fields",
    )(far, near, far_in, near_in, image, far_early_in, far_late_in, near_image_in, potential, near_potential, magnet_mask)
    sums, fields = gather_sums(sums, fields, slabs)
    spans = [radial // 8 * k for k in EIGHTHS]
    terms = pl.pallas_call(
        term_kernel,
        out_shape=tuple(f32((2, span, angular)) for span in spans),
        in_specs=[vmem] * 4,
        out_specs=(vmem,) * len(spans),
        compiler_params=params(),
        name="term",
    )(sums, *fields)
    adjoint = pl.pallas_call(
        adjoint_kernel,
        out_shape=pltpu.HBM((2,) + plane, jnp.float32),
        in_specs=[vmem] * 4,
        out_specs=hbm,
        scratch_shapes=[VMEM((2,) + plane, jnp.float32), pltpu.SemaphoreType.DMA(())],
        compiler_params=params(),
        name="adjoint",
    )(sums, far, near, image)
    gradient = ()
    for index, term in enumerate(terms):
        total, arrived = sum_positions(term, positions, slabs)
        gradient = pl.pallas_call(
            functools.partial(close_kernel, first_rows(radial)[index]),
            out_shape=pltpu.HBM((2,) + plane, jnp.float32),
            in_specs=[vmem] * 2 + [hbm] * (index > 0),
            out_specs=hbm,
            scratch_shapes=[VMEM(term.shape, jnp.float32), pltpu.SemaphoreType.DMA(())],
            input_output_aliases={2: 0} if index else {},
            compiler_params=params(),
            name="close",
        )(total, arrived, *((gradient,) if index else ()))
    return gradient, adjoint[None]


def solution(mesh):
    return jax.shard_map(
        local,
        mesh=mesh,
        in_specs=(
            P("slab", None, None),
            P("slab", None, None),
            P(),
            P("pos"),
            P("pos", "slab", None, None),
            P("pos", "slab", None, None),
        ),
        out_specs=(P("slab", None, None), P("pos", "slab", None, None)),
        check_vma=False,
    )
```

```python
import functools

import jax
import jax.numpy as jnp
from jax import lax
from jax.experimental import pallas as pl
from jax.experimental.pallas import tpu as pltpu
from jax.sharding import PartitionSpec as P


ROWS = 16
VMEM = pltpu.VMEM
SMEM = pltpu.SMEM
SUMS = 5
EIGHTHS = (2, 2, 2, 2)


def params():
    return pltpu.CompilerParams(vmem_limit_bytes=40 * 1024 * 1024)


def shifted(ref, index, start, offset):
    total, columns = ref.shape[-2:]
    zero = jnp.zeros((1, columns), jnp.float32)
    if start + offset < 0:
        return jnp.concatenate([zero, ref[index, 0 : ROWS - 1, :]], axis=0)
    if start + offset + ROWS > total:
        return jnp.concatenate([ref[index, start + 1 : total, :], zero], axis=0)
    return ref[index, start + offset : start + offset + ROWS, :]


def turn(value, offset):
    return pltpu.roll(value, offset % value.shape[1], 1)


def in_plane(nu_ref, nu_index, ref, index, start):
    nu = nu_ref[nu_index, start : start + ROWS, :]
    v = ref[index, start : start + ROWS, :]
    total = None
    for offset in (-1, 1):
        across = (nu + turn(nu, offset)) * (v - turn(v, offset))
        total = across if total is None else total + across
        total = total + (nu + shifted(nu_ref, nu_index, start, offset)) * (
            v - shifted(ref, index, start, offset)
        )
    return nu, v, total


def beyond_far():
    slab, _ = place()
    inside = (slab > 0) & (slab < lax.axis_size("slab") - 1)
    return jnp.where(inside, 1.0, 0.0).astype(jnp.float32)


def place():
    slab = lax.axis_index("slab")
    return slab, lax.rem(slab, 2)


def open_kernel(reluctivity, shift, labels, load, potential, far, near, far_potential, near_potential, held, table, sems):
    _, even = place()
    odd = 1 - even
    total = labels.shape[1]
    moves = (
        (labels.at[even], held.at[0]),
        (labels.at[odd], held.at[1]),
        (load.at[even], far.at[1]),
        (load.at[odd], near.at[1]),
        (potential.at[even], far_potential.at[0]),
        (potential.at[odd], near_potential.at[0]),
        (reluctivity, table),
    )
    copies = [pltpu.make_async_copy(src, dst, sems.at[i]) for i, (src, dst) in enumerate(moves)]
    for copy in copies:
        copy.start()
    copies[-1].wait()
    r0, r1, r2, r3 = (table[i] for i in range(4))
    offset = shift[0]
    for side, out in enumerate((far, near)):
        copies[side].wait()
        for start in range(0, total, ROWS):
            rows = slice(start, start + ROWS)
            material = held[side, rows, :]
            if start < total // 2:
                material = pltpu.roll(material, offset, 1)
            out[0, rows, :] = jnp.where(
                material < 2,
                jnp.where(material == 0, r0, r1),
                jnp.where(material == 2, r2, r3),
            )
    for copy in copies[2:-1]:
        copy.wait()


def part_kernel(far, near, far_potential, far_part, near_part, far_early, far_late):
    _, even = place()
    total = far.shape[1]
    half = total // 2
    for own, other, out in ((far, near, far_part), (near, far, near_part)):
        for start in range(0, total, ROWS):
            rows = slice(start, start + ROWS)
            nu, v, total_flux = in_plane(own, 0, own, 1, start)
            total_flux = total_flux + (nu + other[0, rows, :]) * (v - other[1, rows, :])
            out[0, rows, :] = 0.5 * (v + total_flux)
    far_early[0] = far_part[0, pl.ds(pl.multiple_of((1 - even) * half, 8), half), :]
    far_late[0, 0:half, :] = far_part[0, pl.ds(pl.multiple_of(even * half, 8), half), :]
    far_late[0, half : half + total, :] = far_potential[0]


def fold(value):
    return jnp.sum(value.reshape(ROWS // 8, 8, value.shape[1]), axis=0)


def sums_kernel(far, near, far_part, near_part, far_in, near_in, near_part_in, image, near_image_in, sums):
    total, columns = far.shape[1:]
    sides = ((far, far_part, far_in), (near, near_part, near_in))
    end = 1.0 - beyond_far()
    nil = jnp.zeros((8, columns), jnp.float32)
    m0, m1 = nil, nil
    for side, (own, part, halo) in enumerate(sides):
        for start in range(0, total, ROWS):
            rows = slice(start, start + ROWS)
            v = own[1, rows, :]
            flux = 0.5 * (own[0, rows, :] + halo[0, rows, :]) * (v - halo[1, rows, :])
            y = part[0, rows, :] + flux
            image[side, rows, :] = y
            if own is near:
                near_image_in[0, rows, :] = near_part_in[0, rows, :] - flux
            m0 = m0 + fold(v * v)
            m1 = m1 + fold(v * y)
    m0 = jnp.sum(m0, keepdims=True)
    m1 = jnp.sum(m1, keepdims=True)
    c = jnp.where(m0 > 0, m1 / m0, 0.0)
    q, s, t = nil, nil, nil
    for side, (own, _, halo) in enumerate(sides):
        for start in range(0, total, ROWS):
            rows = slice(start, start + ROWS)
            nu, y, total_flux = in_plane(own, 0, image, side, start)
            other = (near, far)[side]
            total_flux = total_flux + (nu + other[0, rows, :]) * (y - image[1 - side, rows, :])
            if own is near:
                total_flux = total_flux + (nu + halo[0, rows, :]) * (y - near_image_in[0, rows, :])
            else:
                total_flux = total_flux + end * (nu * y)
            z = 0.5 * (y + total_flux)
            v = own[1, rows, :]
            w = y - c * v
            u = z - c * y
            q = q + fold(w * w)
            s = s + fold(w * u)
            t = t + fold(v * u)
    for index, value in enumerate((m0, m1, q, s, t, c)):
        value = jnp.sum(value, keepdims=True) if value.shape[0] > 1 else value
        sums[index : index + 1, :] = jnp.broadcast_to(value, (1, sums.shape[1]))


def face_kernel(far, far_in, far_early_in, image, own_sums, sums):
    slab, even = place()
    total, columns = far.shape[1:]
    half = total // 2
    beyond = beyond_far()
    c = own_sums[SUMS : SUMS + 1, 0:1]
    s = jnp.zeros((8, columns), jnp.float32)
    t = s
    for start in range(0, half, ROWS):
        rows = pl.ds(pl.multiple_of(even * half + start, 8), ROWS)
        v = far[1, rows, :]
        y = image[0, rows, :]
        outer_v = far_in[1, rows, :]
        step = v - outer_v
        weight = 0.5 * (far[0, rows, :] + far_in[0, rows, :])
        outer = far_early_in[0, start : start + ROWS, :] - weight * step
        flux = beyond * (weight * (y - outer))
        s = s + fold(((y - c * v) - (outer - c * outer_v)) * flux)
        t = t + fold(step * flux)
    here = lax.broadcasted_iota(jnp.int32, sums.shape[1:], 0) == slab
    added = (None, None, None, s, t)
    for index in range(SUMS):
        value = own_sums[index : index + 1, :]
        if added[index] is not None:
            value = value + jnp.sum(added[index], keepdims=True)
        sums[index] = jnp.where(here, value, 0.0)


def fields_kernel(
    far, near, far_in, near_in, image, far_early_in, far_late_in, near_image_in, potential, near_potential, mask, u1, u2, u3
):
    _, even = place()
    total = far.shape[1]
    scale = 0.25 / lax.axis_size("pos")
    half = total // 2
    beyond_end = beyond_far()
    sides = ((far, even, far_in), (near, 1 - even, near_in))
    for side, (own, layer, halo) in enumerate(sides):
        other = (near, far)[side]
        for start in range(0, total, ROWS):
            rows = slice(start, start + ROWS)
            if own is far:
                piece = slice(start % half, start % half + ROWS)
                early = even == start // half
                part = jnp.where(early, far_early_in[0, piece, :], far_late_in[0, piece, :])
                weight = 0.5 * (far[0, rows, :] + far_in[0, rows, :])
                image_in = beyond_end * (part - weight * (far[1, rows, :] - far_in[1, rows, :]))
                potential_in = far_late_in[0, half + start : half + start + ROWS, :]
            else:
                image_in = near_image_in[0, rows, :]
                potential_in = near_potential[0, rows, :]
            slopes = []
            for ref, index, beyond, inner in (
                (potential, layer, potential_in, potential[1 - layer, rows, :]),
                (own, 1, halo[1, rows, :], other[1, rows, :]),
                (image, side, image_in, image[1 - side, rows, :]),
            ):
                field = ref[index, rows, :]
                slopes.append(
                    (
                        beyond - inner,
                        turn(field, -1) - turn(field, 1),
                        shifted(ref, index, start, 1) - shifted(ref, index, start, -1),
                    )
                )
            weight = scale * (mask[layer, rows, :].astype(jnp.float32) * own[0, rows, :])
            g = [weight * slope for slope in slopes[0]]
            for out, factor, slope in ((u1, 1.0, slopes[1]), (u2, 1.0, slopes[2]), (u3, 0.5, slopes[0])):
                out[layer, rows, :] = factor * (g[0] * slope[0] + g[1] * slope[1] + g[2] * slope[2])


def coefficients(sums):
    m0_d, m1_d, q_d, s_d, t_d = (sums[i] for i in range(SUMS))
    m0 = jnp.sum(m0_d, axis=0, keepdims=True)
    m1 = jnp.sum(m1_d, axis=0, keepdims=True)
    c = m1 / m0
    delta = jnp.where(m0_d > 0, m1_d / m0_d, 0.0) - c
    ww = jnp.sum(q_d + delta * delta * m0_d, axis=0, keepdims=True)
    waw = jnp.sum(s_d + delta * (q_d + t_d) + delta * delta * m1_d, axis=0, keepdims=True)
    alpha0 = m0 / m1
    beta = alpha0 * (ww * alpha0 / m0)
    divisor = waw - ww * (ww / m1)
    alpha1 = jnp.where(divisor == 0, 0.0, ww / divisor)
    return (alpha0 + alpha1 * (1.0 + beta))[:, 0:1], (-alpha1 * alpha0)[:, 0:1]


def term_kernel(sums, u1, u2, u3, *terms):
    a, b = coefficients(sums)
    for term, first in zip(terms, first_rows(u1.shape[1])):
        for layer in range(2):
            for start in range(0, term.shape[1], ROWS):
                rows = slice(first + start, first + start + ROWS)
                term[layer, start : start + ROWS, :] = (
                    a * u1[layer, rows, :] + b * u2[layer, rows, :] + u3[layer, rows, :]
                )


def adjoint_kernel(sums, far, near, image, adjoint, held, sem):
    _, even = place()
    a, b = coefficients(sums)
    for side, (own, layer) in enumerate(((far, even), (near, 1 - even))):
        for start in range(0, far.shape[1], ROWS):
            rows = slice(start, start + ROWS)
            held[layer, rows, :] = a * own[1, rows, :] + b * image[side, rows, :]
    copy = pltpu.make_async_copy(held, adjoint, sem)
    copy.start()
    copy.wait()


def in_hbm(x):
    return pltpu.with_memory_space_constraint(x, pltpu.HBM)


def first_rows(total):
    return [total // 8 * sum(EIGHTHS[:i]) for i in range(len(EIGHTHS))]


def close_kernel(start, total, arrived, *rest):
    gradient, held, sem = rest[-3:]
    held[...] = total[...] + arrived[...]
    copy = pltpu.make_async_copy(held, gradient.at[:, pl.ds(start, total.shape[1]), :], sem)
    copy.start()
    copy.wait()


def pairs(size, first):
    out = []
    for i in range(first, size - 1, 2):
        out += [(i, i + 1), (i + 1, i)]
    return out


def gather_sums(sums, fields, slabs):
    steps = [2**k for k in range(2, slabs.bit_length() - 1)] + [1]
    for step in steps:
        arrived = lax.ppermute(sums, "slab", [(i, i ^ step) for i in range(slabs)])
        if step == steps[-2]:
            arrived, *fields = lax.optimization_barrier((arrived, *fields))
        sums = sums + arrived
    return sums, fields


def partners(step, positions, slabs):
    bits = positions.bit_length() - 1
    route = []
    for p in range(positions):
        for s in range(slabs):
            bit = step if s % 2 == 0 else bits - 1 - step
            route.append((p * slabs + s, (p ^ (1 << bit)) * slabs + s))
    return route


def sum_positions(term, positions, slabs):
    arrived = lax.ppermute(term, ("pos", "slab"), partners(0, positions, slabs))
    for step in range(1, positions.bit_length() - 1):
        term = term + arrived
        arrived = lax.ppermute(term, ("pos", "slab"), partners(step, positions, slabs))
    return term, arrived


def local(labels, magnet_mask, reluctivity, rotor_shift, potential, adjoint_load):
    layers, radial, angular = labels.shape
    positions, slabs = lax.axis_size("pos"), lax.axis_size("slab")
    if layers != 2 or slabs < 8 or slabs & (slabs - 1) or radial % (8 * ROWS) or positions < 2 or positions & (positions - 1):
        raise ValueError("unsupported sizes")
    potential, load = potential[0], adjoint_load[0]
    f32 = functools.partial(jax.ShapeDtypeStruct, dtype=jnp.float32)
    plane = (radial, angular)
    vmem = pl.BlockSpec(memory_space=VMEM)
    smem = pl.BlockSpec(memory_space=SMEM)
    hbm = pl.BlockSpec(memory_space=pltpu.HBM)
    far, near, far_potential, near_potential = pl.pallas_call(
        open_kernel,
        out_shape=tuple(pltpu.VMEM((k,) + plane, jnp.float32) for k in (2, 2, 1, 1)),
        in_specs=[hbm, smem, hbm, hbm, hbm],
        out_specs=(vmem,) * 4,
        scratch_shapes=[
            VMEM((2,) + plane, jnp.int32),
            SMEM(reluctivity.shape, jnp.float32),
            pltpu.SemaphoreType.DMA((7,)),
        ],
        compiler_params=params(),
        name="open",
    )(in_hbm(reluctivity), rotor_shift, in_hbm(labels), in_hbm(load), in_hbm(potential))
    far_in = lax.ppermute(far, "slab", pairs(slabs, 1))
    near_in = lax.ppermute(near, "slab", pairs(slabs, 0))
    half = radial // 2
    far_part, near_part, far_early, far_late = pl.pallas_call(
        part_kernel,
        out_shape=tuple(pltpu.VMEM((1, rows, angular), jnp.float32) for rows in (radial, radial, half, half + radial)),
        in_specs=[vmem] * 3,
        out_specs=(vmem,) * 4,
        compiler_params=params(),
        name="part",
    )(far, near, far_potential)
    far_early_in = lax.ppermute(far_early, "slab", pairs(slabs, 1))
    near_part_in = lax.ppermute(near_part, "slab", pairs(slabs, 0))
    far_late_in = lax.ppermute(far_late, "slab", pairs(slabs, 1))
    image, near_image_in, own_sums = pl.pallas_call(
        sums_kernel,
        out_shape=(f32((2,) + plane), f32((1,) + plane), f32((8, 128))),
        in_specs=[vmem] * 7,
        out_specs=(vmem,) * 3,
        compiler_params=params(),
        name="sums",
    )(far, near, far_part, near_part, far_in, near_in, near_part_in)
    sums = pl.pallas_call(
        face_kernel,
        out_shape=f32((SUMS, slabs, 128)),
        in_specs=[vmem] * 5,
        out_specs=vmem,
        compiler_params=params(),
        name="face",
    )(far, far_in, far_early_in, image, own_sums)
    arrived = lax.ppermute(sums, "slab", [(i, i ^ 2) for i in range(slabs)])
    near_potential, arrived = lax.optimization_barrier((near_potential, arrived))
    near_potential = lax.ppermute(near_potential, "slab", pairs(slabs, 0))
    sums = sums + arrived
    fields = pl.pallas_call(
        fields_kernel,
        out_shape=(f32((2,) + plane),) * 3,
        in_specs=[vmem] * 11,
        out_specs=(vmem,) * 3,
        compiler_params=params(),
        name="fields",
    )(far, near, far_in, near_in, image, far_early_in, far_late_in, near_image_in, potential, near_potential, magnet_mask)
    sums, fields = gather_sums(sums, fields, slabs)
    spans = [radial // 8 * k for k in EIGHTHS]
    terms = pl.pallas_call(
        term_kernel,
        out_shape=tuple(f32((2, span, angular)) for span in spans),
        in_specs=[vmem] * 4,
        out_specs=(vmem,) * len(spans),
        compiler_params=params(),
        name="term",
    )(sums, *fields)
    adjoint = pl.pallas_call(
        adjoint_kernel,
        out_shape=pltpu.HBM((2,) + plane, jnp.float32),
        in_specs=[vmem] * 4,
        out_specs=hbm,
        scratch_shapes=[VMEM((2,) + plane, jnp.float32), pltpu.SemaphoreType.DMA(())],
        compiler_params=params(),
        name="adjoint",
    )(sums, far, near, image)
    gradient = ()
    for index, term in enumerate(terms):
        total, arrived = sum_positions(term, positions, slabs)
        gradient = pl.pallas_call(
            functools.partial(close_kernel, first_rows(radial)[index]),
            out_shape=pltpu.HBM((2,) + plane, jnp.float32),
            in_specs=[vmem] * 2 + [hbm] * (index > 0),
            out_specs=hbm,
            scratch_shapes=[VMEM(term.shape, jnp.float32), pltpu.SemaphoreType.DMA(())],
            input_output_aliases={2: 0} if index else {},
            compiler_params=params(),
            name="close",
        )(total, arrived, *((gradient,) if index else ()))
    return gradient, adjoint[None]


def solution(mesh):
    return jax.shard_map(
        local,
        mesh=mesh,
        in_specs=(
            P("slab", None, None),
            P("slab", None, None),
            P(),
            P("pos"),
            P("pos", "slab", None, None),
            P("pos", "slab", None, None),
        ),
        out_specs=(P("slab", None, None), P("pos", "slab", None, None)),
        check_vma=False,
    )
```

```python
import functools

import jax
import jax.numpy as jnp
from jax import lax
from jax.experimental import pallas as pl
from jax.experimental.pallas import tpu as pltpu
from jax.sharding import PartitionSpec as P


ROWS = 16
VMEM = pltpu.VMEM
SMEM = pltpu.SMEM
SUMS = 5
EIGHTHS = (4, 4)


def params():
    return pltpu.CompilerParams(vmem_limit_bytes=40 * 1024 * 1024)


def shifted(ref, index, start, offset):
    total, columns = ref.shape[-2:]
    zero = jnp.zeros((1, columns), jnp.float32)
    if start + offset < 0:
        return jnp.concatenate([zero, ref[index, 0 : ROWS - 1, :]], axis=0)
    if start + offset + ROWS > total:
        return jnp.concatenate([ref[index, start + 1 : total, :], zero], axis=0)
    return ref[index, start + offset : start + offset + ROWS, :]


def turn(value, offset):
    return pltpu.roll(value, offset % value.shape[1], 1)


def in_plane(nu_ref, nu_index, ref, index, start):
    nu = nu_ref[nu_index, start : start + ROWS, :]
    v = ref[index, start : start + ROWS, :]
    total = None
    for offset in (-1, 1):
        across = (nu + turn(nu, offset)) * (v - turn(v, offset))
        total = across if total is None else total + across
        total = total + (nu + shifted(nu_ref, nu_index, start, offset)) * (
            v - shifted(ref, index, start, offset)
        )
    return nu, v, total


def beyond_far():
    slab, _ = place()
    inside = (slab > 0) & (slab < lax.axis_size("slab") - 1)
    return jnp.where(inside, 1.0, 0.0).astype(jnp.float32)


def place():
    slab = lax.axis_index("slab")
    return slab, lax.rem(slab, 2)


def open_kernel(reluctivity, shift, labels, load, potential, far, near, far_potential, near_potential, held, table, sems):
    _, even = place()
    odd = 1 - even
    total = labels.shape[1]
    moves = (
        (labels.at[even], held.at[0]),
        (labels.at[odd], held.at[1]),
        (load.at[even], far.at[1]),
        (load.at[odd], near.at[1]),
        (potential.at[even], far_potential.at[0]),
        (potential.at[odd], near_potential.at[0]),
        (reluctivity, table),
    )
    copies = [pltpu.make_async_copy(src, dst, sems.at[i]) for i, (src, dst) in enumerate(moves)]
    for copy in copies:
        copy.start()
    copies[-1].wait()
    r0, r1, r2, r3 = (table[i] for i in range(4))
    offset = shift[0]
    for side, out in enumerate((far, near)):
        copies[side].wait()
        for start in range(0, total, ROWS):
            rows = slice(start, start + ROWS)
            material = held[side, rows, :]
            if start < total // 2:
                material = pltpu.roll(material, offset, 1)
            out[0, rows, :] = jnp.where(
                material < 2,
                jnp.where(material == 0, r0, r1),
                jnp.where(material == 2, r2, r3),
            )
    for copy in copies[2:-1]:
        copy.wait()


def part_kernel(far, near, far_potential, far_part, near_part, far_early, far_late):
    _, even = place()
    total = far.shape[1]
    half = total // 2
    for own, other, out in ((far, near, far_part), (near, far, near_part)):
        for start in range(0, total, ROWS):
            rows = slice(start, start + ROWS)
            nu, v, total_flux = in_plane(own, 0, own, 1, start)
            total_flux = total_flux + (nu + other[0, rows, :]) * (v - other[1, rows, :])
            out[0, rows, :] = 0.5 * (v + total_flux)
    far_early[0] = far_part[0, pl.ds(pl.multiple_of((1 - even) * half, 8), half), :]
    far_late[0, 0:half, :] = far_part[0, pl.ds(pl.multiple_of(even * half, 8), half), :]
    far_late[0, half : half + total, :] = far_potential[0]


def fold(value):
    return jnp.sum(value.reshape(ROWS // 8, 8, value.shape[1]), axis=0)


def sums_kernel(far, near, far_part, near_part, far_in, near_in, near_part_in, image, near_image_in, sums):
    total, columns = far.shape[1:]
    sides = ((far, far_part, far_in), (near, near_part, near_in))
    end = 1.0 - beyond_far()
    nil = jnp.zeros((8, columns), jnp.float32)
    m0, m1 = nil, nil
    for side, (own, part, halo) in enumerate(sides):
        for start in range(0, total, ROWS):
            rows = slice(start, start + ROWS)
            v = own[1, rows, :]
            flux = 0.5 * (own[0, rows, :] + halo[0, rows, :]) * (v - halo[1, rows, :])
            y = part[0, rows, :] + flux
            image[side, rows, :] = y
            if own is near:
                near_image_in[0, rows, :] = near_part_in[0, rows, :] - flux
            m0 = m0 + fold(v * v)
            m1 = m1 + fold(v * y)
    m0 = jnp.sum(m0, keepdims=True)
    m1 = jnp.sum(m1, keepdims=True)
    c = jnp.where(m0 > 0, m1 / m0, 0.0)
    q, s, t = nil, nil, nil
    for side, (own, _, halo) in enumerate(sides):
        for start in range(0, total, ROWS):
            rows = slice(start, start + ROWS)
            nu, y, total_flux = in_plane(own, 0, image, side, start)
            other = (near, far)[side]
            total_flux = total_flux + (nu + other[0, rows, :]) * (y - image[1 - side, rows, :])
            if own is near:
                total_flux = total_flux + (nu + halo[0, rows, :]) * (y - near_image_in[0, rows, :])
            else:
                total_flux = total_flux + end * (nu * y)
            z = 0.5 * (y + total_flux)
            v = own[1, rows, :]
            w = y - c * v
            u = z - c * y
            q = q + fold(w * w)
            s = s + fold(w * u)
            t = t + fold(v * u)
    for index, value in enumerate((m0, m1, q, s, t, c)):
        value = jnp.sum(value, keepdims=True) if value.shape[0] > 1 else value
        sums[index : index + 1, :] = jnp.broadcast_to(value, (1, sums.shape[1]))


def face_kernel(far, far_in, far_early_in, image, own_sums, sums):
    slab, even = place()
    total, columns = far.shape[1:]
    half = total // 2
    beyond = beyond_far()
    c = own_sums[SUMS : SUMS + 1, 0:1]
    s = jnp.zeros((8, columns), jnp.float32)
    t = s
    for start in range(0, half, ROWS):
        rows = pl.ds(pl.multiple_of(even * half + start, 8), ROWS)
        v = far[1, rows, :]
        y = image[0, rows, :]
        outer_v = far_in[1, rows, :]
        step = v - outer_v
        weight = 0.5 * (far[0, rows, :] + far_in[0, rows, :])
        outer = far_early_in[0, start : start + ROWS, :] - weight * step
        flux = beyond * (weight * (y - outer))
        s = s + fold(((y - c * v) - (outer - c * outer_v)) * flux)
        t = t + fold(step * flux)
    here = lax.broadcasted_iota(jnp.int32, sums.shape[1:], 0) == slab
    added = (None, None, None, s, t)
    for index in range(SUMS):
        value = own_sums[index : index + 1, :]
        if added[index] is not None:
            value = value + jnp.sum(added[index], keepdims=True)
        sums[index] = jnp.where(here, value, 0.0)


def fields_kernel(
    far, near, far_in, near_in, image, far_early_in, far_late_in, near_image_in, potential, near_potential, mask, u1, u2, u3
):
    _, even = place()
    total = far.shape[1]
    scale = 0.25 / lax.axis_size("pos")
    half = total // 2
    beyond_end = beyond_far()
    sides = ((far, even, far_in), (near, 1 - even, near_in))
    for side, (own, layer, halo) in enumerate(sides):
        other = (near, far)[side]
        for start in range(0, total, ROWS):
            rows = slice(start, start + ROWS)
            if own is far:
                piece = slice(start % half, start % half + ROWS)
                early = even == start // half
                part = jnp.where(early, far_early_in[0, piece, :], far_late_in[0, piece, :])
                weight = 0.5 * (far[0, rows, :] + far_in[0, rows, :])
                image_in = beyond_end * (part - weight * (far[1, rows, :] - far_in[1, rows, :]))
                potential_in = far_late_in[0, half + start : half + start + ROWS, :]
            else:
                image_in = near_image_in[0, rows, :]
                potential_in = near_potential[0, rows, :]
            slopes = []
            for ref, index, beyond, inner in (
                (potential, layer, potential_in, potential[1 - layer, rows, :]),
                (own, 1, halo[1, rows, :], other[1, rows, :]),
                (image, side, image_in, image[1 - side, rows, :]),
            ):
                field = ref[index, rows, :]
                slopes.append(
                    (
                        beyond - inner,
                        turn(field, -1) - turn(field, 1),
                        shifted(ref, index, start, 1) - shifted(ref, index, start, -1),
                    )
                )
            weight = scale * (mask[layer, rows, :].astype(jnp.float32) * own[0, rows, :])
            g = [weight * slope for slope in slopes[0]]
            for out, factor, slope in ((u1, 1.0, slopes[1]), (u2, 1.0, slopes[2]), (u3, 0.5, slopes[0])):
                out[layer, rows, :] = factor * (g[0] * slope[0] + g[1] * slope[1] + g[2] * slope[2])


def coefficients(sums):
    m0_d, m1_d, q_d, s_d, t_d = (sums[i] for i in range(SUMS))
    m0 = jnp.sum(m0_d, axis=0, keepdims=True)
    m1 = jnp.sum(m1_d, axis=0, keepdims=True)
    c = m1 / m0
    delta = jnp.where(m0_d > 0, m1_d / m0_d, 0.0) - c
    ww = jnp.sum(q_d + delta * delta * m0_d, axis=0, keepdims=True)
    waw = jnp.sum(s_d + delta * (q_d + t_d) + delta * delta * m1_d, axis=0, keepdims=True)
    alpha0 = m0 / m1
    beta = alpha0 * (ww * alpha0 / m0)
    divisor = waw - ww * (ww / m1)
    alpha1 = jnp.where(divisor == 0, 0.0, ww / divisor)
    return (alpha0 + alpha1 * (1.0 + beta))[:, 0:1], (-alpha1 * alpha0)[:, 0:1]


def term_kernel(sums, u1, u2, u3, *terms):
    a, b = coefficients(sums)
    for term, first in zip(terms, first_rows(u1.shape[1])):
        for layer in range(2):
            for start in range(0, term.shape[1], ROWS):
                rows = slice(first + start, first + start + ROWS)
                term[layer, start : start + ROWS, :] = (
                    a * u1[layer, rows, :] + b * u2[layer, rows, :] + u3[layer, rows, :]
                )


def adjoint_kernel(sums, far, near, image, adjoint, held, sem):
    _, even = place()
    a, b = coefficients(sums)
    for side, (own, layer) in enumerate(((far, even), (near, 1 - even))):
        for start in range(0, far.shape[1], ROWS):
            rows = slice(start, start + ROWS)
            held[layer, rows, :] = a * own[1, rows, :] + b * image[side, rows, :]
    copy = pltpu.make_async_copy(held, adjoint, sem)
    copy.start()
    copy.wait()


def in_hbm(x):
    return pltpu.with_memory_space_constraint(x, pltpu.HBM)


def first_rows(total):
    return [total // 8 * sum(EIGHTHS[:i]) for i in range(len(EIGHTHS))]


def close_kernel(start, total, arrived, *rest):
    gradient, held, sem = rest[-3:]
    held[...] = total[...] + arrived[...]
    copy = pltpu.make_async_copy(held, gradient.at[:, pl.ds(start, total.shape[1]), :], sem)
    copy.start()
    copy.wait()


def pairs(size, first):
    out = []
    for i in range(first, size - 1, 2):
        out += [(i, i + 1), (i + 1, i)]
    return out


def gather_sums(sums, fields, slabs):
    steps = [2**k for k in range(2, slabs.bit_length() - 1)] + [1]
    for step in steps:
        arrived = lax.ppermute(sums, "slab", [(i, i ^ step) for i in range(slabs)])
        if step == steps[-2]:
            arrived, *fields = lax.optimization_barrier((arrived, *fields))
        sums = sums + arrived
    return sums, fields


def partners(step, positions, slabs):
    bits = positions.bit_length() - 1
    route = []
    for p in range(positions):
        for s in range(slabs):
            bit = step if s % 2 == 0 else bits - 1 - step
            route.append((p * slabs + s, (p ^ (1 << bit)) * slabs + s))
    return route


def sum_positions(term, positions, slabs):
    arrived = lax.ppermute(term, ("pos", "slab"), partners(0, positions, slabs))
    for step in range(1, positions.bit_length() - 1):
        term = term + arrived
        arrived = lax.ppermute(term, ("pos", "slab"), partners(step, positions, slabs))
    return term, arrived


def local(labels, magnet_mask, reluctivity, rotor_shift, potential, adjoint_load):
    layers, radial, angular = labels.shape
    positions, slabs = lax.axis_size("pos"), lax.axis_size("slab")
    if layers != 2 or slabs < 8 or slabs & (slabs - 1) or radial % (8 * ROWS) or positions < 2 or positions & (positions - 1):
        raise ValueError("unsupported sizes")
    potential, load = potential[0], adjoint_load[0]
    f32 = functools.partial(jax.ShapeDtypeStruct, dtype=jnp.float32)
    plane = (radial, angular)
    vmem = pl.BlockSpec(memory_space=VMEM)
    smem = pl.BlockSpec(memory_space=SMEM)
    hbm = pl.BlockSpec(memory_space=pltpu.HBM)
    far, near, far_potential, near_potential = pl.pallas_call(
        open_kernel,
        out_shape=tuple(pltpu.VMEM((k,) + plane, jnp.float32) for k in (2, 2, 1, 1)),
        in_specs=[hbm, smem, hbm, hbm, hbm],
        out_specs=(vmem,) * 4,
        scratch_shapes=[
            VMEM((2,) + plane, jnp.int32),
            SMEM(reluctivity.shape, jnp.float32),
            pltpu.SemaphoreType.DMA((7,)),
        ],
        compiler_params=params(),
        name="open",
    )(in_hbm(reluctivity), rotor_shift, in_hbm(labels), in_hbm(load), in_hbm(potential))
    far_in = lax.ppermute(far, "slab", pairs(slabs, 1))
    near_in = lax.ppermute(near, "slab", pairs(slabs, 0))
    half = radial // 2
    far_part, near_part, far_early, far_late = pl.pallas_call(
        part_kernel,
        out_shape=tuple(pltpu.VMEM((1, rows, angular), jnp.float32) for rows in (radial, radial, half, half + radial)),
        in_specs=[vmem] * 3,
        out_specs=(vmem,) * 4,
        compiler_params=params(),
        name="part",
    )(far, near, far_potential)
    far_early_in = lax.ppermute(far_early, "slab", pairs(slabs, 1))
    near_part_in = lax.ppermute(near_part, "slab", pairs(slabs, 0))
    far_late_in = lax.ppermute(far_late, "slab", pairs(slabs, 1))
    image, near_image_in, own_sums = pl.pallas_call(
        sums_kernel,
        out_shape=(f32((2,) + plane), f32((1,) + plane), f32((8, 128))),
        in_specs=[vmem] * 7,
        out_specs=(vmem,) * 3,
        compiler_params=params(),
        name="sums",
    )(far, near, far_part, near_part, far_in, near_in, near_part_in)
    sums = pl.pallas_call(
        face_kernel,
        out_shape=f32((SUMS, slabs, 128)),
        in_specs=[vmem] * 5,
        out_specs=vmem,
        compiler_params=params(),
        name="face",
    )(far, far_in, far_early_in, image, own_sums)
    arrived = lax.ppermute(sums, "slab", [(i, i ^ 2) for i in range(slabs)])
    near_potential, arrived = lax.optimization_barrier((near_potential, arrived))
    near_potential = lax.ppermute(near_potential, "slab", pairs(slabs, 0))
    sums = sums + arrived
    fields = pl.pallas_call(
        fields_kernel,
        out_shape=(f32((2,) + plane),) * 3,
        in_specs=[vmem] * 11,
        out_specs=(vmem,) * 3,
        compiler_params=params(),
        name="fields",
    )(far, near, far_in, near_in, image, far_early_in, far_late_in, near_image_in, potential, near_potential, magnet_mask)
    sums, fields = gather_sums(sums, fields, slabs)
    spans = [radial // 8 * k for k in EIGHTHS]
    terms = pl.pallas_call(
        term_kernel,
        out_shape=tuple(f32((2, span, angular)) for span in spans),
        in_specs=[vmem] * 4,
        out_specs=(vmem,) * len(spans),
        compiler_params=params(),
        name="term",
    )(sums, *fields)
    adjoint = pl.pallas_call(
        adjoint_kernel,
        out_shape=pltpu.HBM((2,) + plane, jnp.float32),
        in_specs=[vmem] * 4,
        out_specs=hbm,
        scratch_shapes=[VMEM((2,) + plane, jnp.float32), pltpu.SemaphoreType.DMA(())],
        compiler_params=params(),
        name="adjoint",
    )(sums, far, near, image)
    gradient = ()
    for index, term in enumerate(terms):
        total, arrived = sum_positions(term, positions, slabs)
        gradient = pl.pallas_call(
            functools.partial(close_kernel, first_rows(radial)[index]),
            out_shape=pltpu.HBM((2,) + plane, jnp.float32),
            in_specs=[vmem] * 2 + [hbm] * (index > 0),
            out_specs=hbm,
            scratch_shapes=[VMEM(term.shape, jnp.float32), pltpu.SemaphoreType.DMA(())],
            input_output_aliases={2: 0} if index else {},
            compiler_params=params(),
            name="close",
        )(total, arrived, *((gradient,) if index else ()))
    return gradient, adjoint[None]


def solution(mesh):
    return jax.shard_map(
        local,
        mesh=mesh,
        in_specs=(
            P("slab", None, None),
            P("slab", None, None),
            P(),
            P("pos"),
            P("pos", "slab", None, None),
            P("pos", "slab", None, None),
        ),
        out_specs=(P("slab", None, None), P("pos", "slab", None, None)),
        check_vma=False,
    )
```

```python
import functools

import jax
import jax.numpy as jnp
from jax import lax
from jax.experimental import pallas as pl
from jax.experimental.pallas import tpu as pltpu
from jax.sharding import PartitionSpec as P


ROWS = 16
VMEM = pltpu.VMEM
SMEM = pltpu.SMEM
SUMS = 5
EIGHTHS = (3, 3, 2)


def params():
    return pltpu.CompilerParams(vmem_limit_bytes=40 * 1024 * 1024)


def shifted(ref, index, start, offset):
    total, columns = ref.shape[-2:]
    zero = jnp.zeros((1, columns), jnp.float32)
    if start + offset < 0:
        return jnp.concatenate([zero, ref[index, 0 : ROWS - 1, :]], axis=0)
    if start + offset + ROWS > total:
        return jnp.concatenate([ref[index, start + 1 : total, :], zero], axis=0)
    return ref[index, start + offset : start + offset + ROWS, :]


def turn(value, offset):
    return pltpu.roll(value, offset % value.shape[1], 1)


def in_plane(nu_ref, nu_index, ref, index, start):
    nu = nu_ref[nu_index, start : start + ROWS, :]
    v = ref[index, start : start + ROWS, :]
    total = None
    for offset in (-1, 1):
        across = (nu + turn(nu, offset)) * (v - turn(v, offset))
        total = across if total is None else total + across
        total = total + (nu + shifted(nu_ref, nu_index, start, offset)) * (
            v - shifted(ref, index, start, offset)
        )
    return nu, v, total


def beyond_far():
    slab, _ = place()
    inside = (slab > 0) & (slab < lax.axis_size("slab") - 1)
    return jnp.where(inside, 1.0, 0.0).astype(jnp.float32)


def place():
    slab = lax.axis_index("slab")
    return slab, lax.rem(slab, 2)


def open_kernel(reluctivity, shift, labels, load, potential, far, near, far_potential, near_potential, held, table, sems):
    _, even = place()
    odd = 1 - even
    total = labels.shape[1]
    moves = (
        (labels.at[even], held.at[0]),
        (labels.at[odd], held.at[1]),
        (load.at[even], far.at[1]),
        (load.at[odd], near.at[1]),
        (potential.at[even], far_potential.at[0]),
        (potential.at[odd], near_potential.at[0]),
        (reluctivity, table),
    )
    copies = [pltpu.make_async_copy(src, dst, sems.at[i]) for i, (src, dst) in enumerate(moves)]
    for copy in copies:
        copy.start()
    copies[-1].wait()
    r0, r1, r2, r3 = (table[i] for i in range(4))
    offset = shift[0]
    for side, out in enumerate((far, near)):
        copies[side].wait()
        for start in range(0, total, ROWS):
            rows = slice(start, start + ROWS)
            material = held[side, rows, :]
            if start < total // 2:
                material = pltpu.roll(material, offset, 1)
            out[0, rows, :] = jnp.where(
                material < 2,
                jnp.where(material == 0, r0, r1),
                jnp.where(material == 2, r2, r3),
            )
    for copy in copies[2:-1]:
        copy.wait()


def part_kernel(far, near, far_potential, far_part, near_part, far_early, far_late):
    _, even = place()
    total = far.shape[1]
    half = total // 2
    for own, other, out in ((far, near, far_part), (near, far, near_part)):
        for start in range(0, total, ROWS):
            rows = slice(start, start + ROWS)
            nu, v, total_flux = in_plane(own, 0, own, 1, start)
            total_flux = total_flux + (nu + other[0, rows, :]) * (v - other[1, rows, :])
            out[0, rows, :] = 0.5 * (v + total_flux)
    far_early[0] = far_part[0, pl.ds(pl.multiple_of((1 - even) * half, 8), half), :]
    far_late[0, 0:half, :] = far_part[0, pl.ds(pl.multiple_of(even * half, 8), half), :]
    far_late[0, half : half + total, :] = far_potential[0]


def fold(value):
    return jnp.sum(value.reshape(ROWS // 8, 8, value.shape[1]), axis=0)


def sums_kernel(far, near, far_part, near_part, far_in, near_in, near_part_in, image, near_image_in, sums):
    total, columns = far.shape[1:]
    sides = ((far, far_part, far_in), (near, near_part, near_in))
    end = 1.0 - beyond_far()
    nil = jnp.zeros((8, columns), jnp.float32)
    m0, m1 = nil, nil
    for side, (own, part, halo) in enumerate(sides):
        for start in range(0, total, ROWS):
            rows = slice(start, start + ROWS)
            v = own[1, rows, :]
            flux = 0.5 * (own[0, rows, :] + halo[0, rows, :]) * (v - halo[1, rows, :])
            y = part[0, rows, :] + flux
            image[side, rows, :] = y
            if own is near:
                near_image_in[0, rows, :] = near_part_in[0, rows, :] - flux
            m0 = m0 + fold(v * v)
            m1 = m1 + fold(v * y)
    m0 = jnp.sum(m0, keepdims=True)
    m1 = jnp.sum(m1, keepdims=True)
    c = jnp.where(m0 > 0, m1 / m0, 0.0)
    q, s, t = nil, nil, nil
    for side, (own, _, halo) in enumerate(sides):
        for start in range(0, total, ROWS):
            rows = slice(start, start + ROWS)
            nu, y, total_flux = in_plane(own, 0, image, side, start)
            other = (near, far)[side]
            total_flux = total_flux + (nu + other[0, rows, :]) * (y - image[1 - side, rows, :])
            if own is near:
                total_flux = total_flux + (nu + halo[0, rows, :]) * (y - near_image_in[0, rows, :])
            else:
                total_flux = total_flux + end * (nu * y)
            z = 0.5 * (y + total_flux)
            v = own[1, rows, :]
            w = y - c * v
            u = z - c * y
            q = q + fold(w * w)
            s = s + fold(w * u)
            t = t + fold(v * u)
    for index, value in enumerate((m0, m1, q, s, t, c)):
        value = jnp.sum(value, keepdims=True) if value.shape[0] > 1 else value
        sums[index : index + 1, :] = jnp.broadcast_to(value, (1, sums.shape[1]))


def face_kernel(far, far_in, far_early_in, image, own_sums, sums):
    slab, even = place()
    total, columns = far.shape[1:]
    half = total // 2
    beyond = beyond_far()
    c = own_sums[SUMS : SUMS + 1, 0:1]
    s = jnp.zeros((8, columns), jnp.float32)
    t = s
    for start in range(0, half, ROWS):
        rows = pl.ds(pl.multiple_of(even * half + start, 8), ROWS)
        v = far[1, rows, :]
        y = image[0, rows, :]
        outer_v = far_in[1, rows, :]
        step = v - outer_v
        weight = 0.5 * (far[0, rows, :] + far_in[0, rows, :])
        outer = far_early_in[0, start : start + ROWS, :] - weight * step
        flux = beyond * (weight * (y - outer))
        s = s + fold(((y - c * v) - (outer - c * outer_v)) * flux)
        t = t + fold(step * flux)
    here = lax.broadcasted_iota(jnp.int32, sums.shape[1:], 0) == slab
    added = (None, None, None, s, t)
    for index in range(SUMS):
        value = own_sums[index : index + 1, :]
        if added[index] is not None:
            value = value + jnp.sum(added[index], keepdims=True)
        sums[index] = jnp.where(here, value, 0.0)


def fields_kernel(
    far, near, far_in, near_in, image, far_early_in, far_late_in, near_image_in, potential, near_potential, mask, u1, u2, u3
):
    _, even = place()
    total = far.shape[1]
    scale = 0.25 / lax.axis_size("pos")
    half = total // 2
    beyond_end = beyond_far()
    sides = ((far, even, far_in), (near, 1 - even, near_in))
    for side, (own, layer, halo) in enumerate(sides):
        other = (near, far)[side]
        for start in range(0, total, ROWS):
            rows = slice(start, start + ROWS)
            if own is far:
                piece = slice(start % half, start % half + ROWS)
                early = even == start // half
                part = jnp.where(early, far_early_in[0, piece, :], far_late_in[0, piece, :])
                weight = 0.5 * (far[0, rows, :] + far_in[0, rows, :])
                image_in = beyond_end * (part - weight * (far[1, rows, :] - far_in[1, rows, :]))
                potential_in = far_late_in[0, half + start : half + start + ROWS, :]
            else:
                image_in = near_image_in[0, rows, :]
                potential_in = near_potential[0, rows, :]
            slopes = []
            for ref, index, beyond, inner in (
                (potential, layer, potential_in, potential[1 - layer, rows, :]),
                (own, 1, halo[1, rows, :], other[1, rows, :]),
                (image, side, image_in, image[1 - side, rows, :]),
            ):
                field = ref[index, rows, :]
                slopes.append(
                    (
                        beyond - inner,
                        turn(field, -1) - turn(field, 1),
                        shifted(ref, index, start, 1) - shifted(ref, index, start, -1),
                    )
                )
            weight = scale * (mask[layer, rows, :].astype(jnp.float32) * own[0, rows, :])
            g = [weight * slope for slope in slopes[0]]
            for out, factor, slope in ((u1, 1.0, slopes[1]), (u2, 1.0, slopes[2]), (u3, 0.5, slopes[0])):
                out[layer, rows, :] = factor * (g[0] * slope[0] + g[1] * slope[1] + g[2] * slope[2])


def coefficients(sums):
    m0_d, m1_d, q_d, s_d, t_d = (sums[i] for i in range(SUMS))
    m0 = jnp.sum(m0_d, axis=0, keepdims=True)
    m1 = jnp.sum(m1_d, axis=0, keepdims=True)
    c = m1 / m0
    delta = jnp.where(m0_d > 0, m1_d / m0_d, 0.0) - c
    ww = jnp.sum(q_d + delta * delta * m0_d, axis=0, keepdims=True)
    waw = jnp.sum(s_d + delta * (q_d + t_d) + delta * delta * m1_d, axis=0, keepdims=True)
    alpha0 = m0 / m1
    beta = alpha0 * (ww * alpha0 / m0)
    divisor = waw - ww * (ww / m1)
    alpha1 = jnp.where(divisor == 0, 0.0, ww / divisor)
    return (alpha0 + alpha1 * (1.0 + beta))[:, 0:1], (-alpha1 * alpha0)[:, 0:1]


def term_kernel(sums, u1, u2, u3, *terms):
    a, b = coefficients(sums)
    for term, first in zip(terms, first_rows(u1.shape[1])):
        for layer in range(2):
            for start in range(0, term.shape[1], ROWS):
                rows = slice(first + start, first + start + ROWS)
                term[layer, start : start + ROWS, :] = (
                    a * u1[layer, rows, :] + b * u2[layer, rows, :] + u3[layer, rows, :]
                )


def adjoint_kernel(sums, far, near, image, adjoint, held, sem):
    _, even = place()
    a, b = coefficients(sums)
    for side, (own, layer) in enumerate(((far, even), (near, 1 - even))):
        for start in range(0, far.shape[1], ROWS):
            rows = slice(start, start + ROWS)
            held[layer, rows, :] = a * own[1, rows, :] + b * image[side, rows, :]
    copy = pltpu.make_async_copy(held, adjoint, sem)
    copy.start()
    copy.wait()


def in_hbm(x):
    return pltpu.with_memory_space_constraint(x, pltpu.HBM)


def first_rows(total):
    return [total // 8 * sum(EIGHTHS[:i]) for i in range(len(EIGHTHS))]


def close_kernel(start, total, arrived, *rest):
    gradient, held, sem = rest[-3:]
    held[...] = total[...] + arrived[...]
    copy = pltpu.make_async_copy(held, gradient.at[:, pl.ds(start, total.shape[1]), :], sem)
    copy.start()
    copy.wait()


def pairs(size, first):
    out = []
    for i in range(first, size - 1, 2):
        out += [(i, i + 1), (i + 1, i)]
    return out


def gather_sums(sums, fields, slabs):
    steps = [2**k for k in range(1, slabs.bit_length() - 2)] + [1]
    for step in steps:
        arrived = lax.ppermute(sums, "slab", [(i, i ^ step) for i in range(slabs)])
        if step == steps[-2]:
            arrived, *fields = lax.optimization_barrier((arrived, *fields))
        sums = sums + arrived
    return sums, fields


def partners(step, positions, slabs):
    bits = positions.bit_length() - 1
    route = []
    for p in range(positions):
        for s in range(slabs):
            bit = step if s % 2 == 0 else bits - 1 - step
            route.append((p * slabs + s, (p ^ (1 << bit)) * slabs + s))
    return route


def sum_positions(term, positions, slabs):
    arrived = lax.ppermute(term, ("pos", "slab"), partners(0, positions, slabs))
    for step in range(1, positions.bit_length() - 1):
        term = term + arrived
        arrived = lax.ppermute(term, ("pos", "slab"), partners(step, positions, slabs))
    return term, arrived


def local(labels, magnet_mask, reluctivity, rotor_shift, potential, adjoint_load):
    layers, radial, angular = labels.shape
    positions, slabs = lax.axis_size("pos"), lax.axis_size("slab")
    if layers != 2 or slabs < 8 or slabs & (slabs - 1) or radial % (8 * ROWS) or positions < 2 or positions & (positions - 1):
        raise ValueError("unsupported sizes")
    potential, load = potential[0], adjoint_load[0]
    f32 = functools.partial(jax.ShapeDtypeStruct, dtype=jnp.float32)
    plane = (radial, angular)
    vmem = pl.BlockSpec(memory_space=VMEM)
    smem = pl.BlockSpec(memory_space=SMEM)
    hbm = pl.BlockSpec(memory_space=pltpu.HBM)
    far, near, far_potential, near_potential = pl.pallas_call(
        open_kernel,
        out_shape=tuple(pltpu.VMEM((k,) + plane, jnp.float32) for k in (2, 2, 1, 1)),
        in_specs=[hbm, smem, hbm, hbm, hbm],
        out_specs=(vmem,) * 4,
        scratch_shapes=[
            VMEM((2,) + plane, jnp.int32),
            SMEM(reluctivity.shape, jnp.float32),
            pltpu.SemaphoreType.DMA((7,)),
        ],
        compiler_params=params(),
        name="open",
    )(in_hbm(reluctivity), rotor_shift, in_hbm(labels), in_hbm(load), in_hbm(potential))
    far_in = lax.ppermute(far, "slab", pairs(slabs, 1))
    near_in = lax.ppermute(near, "slab", pairs(slabs, 0))
    half = radial // 2
    far_part, near_part, far_early, far_late = pl.pallas_call(
        part_kernel,
        out_shape=tuple(pltpu.VMEM((1, rows, angular), jnp.float32) for rows in (radial, radial, half, half + radial)),
        in_specs=[vmem] * 3,
        out_specs=(vmem,) * 4,
        compiler_params=params(),
        name="part",
    )(far, near, far_potential)
    far_early_in = lax.ppermute(far_early, "slab", pairs(slabs, 1))
    near_part_in = lax.ppermute(near_part, "slab", pairs(slabs, 0))
    far_late_in = lax.ppermute(far_late, "slab", pairs(slabs, 1))
    image, near_image_in, own_sums = pl.pallas_call(
        sums_kernel,
        out_shape=(f32((2,) + plane), f32((1,) + plane), f32((8, 128))),
        in_specs=[vmem] * 7,
        out_specs=(vmem,) * 3,
        compiler_params=params(),
        name="sums",
    )(far, near, far_part, near_part, far_in, near_in, near_part_in)
    sums = pl.pallas_call(
        face_kernel,
        out_shape=f32((SUMS, slabs, 128)),
        in_specs=[vmem] * 5,
        out_specs=vmem,
        compiler_params=params(),
        name="face",
    )(far, far_in, far_early_in, image, own_sums)
    arrived = lax.ppermute(sums, "slab", [(i, i ^ (slabs // 2)) for i in range(slabs)])
    near_potential, arrived = lax.optimization_barrier((near_potential, arrived))
    near_potential = lax.ppermute(near_potential, "slab", pairs(slabs, 0))
    sums = sums + arrived
    fields = pl.pallas_call(
        fields_kernel,
        out_shape=(f32((2,) + plane),) * 3,
        in_specs=[vmem] * 11,
        out_specs=(vmem,) * 3,
        compiler_params=params(),
        name="fields",
    )(far, near, far_in, near_in, image, far_early_in, far_late_in, near_image_in, potential, near_potential, magnet_mask)
    sums, fields = gather_sums(sums, fields, slabs)
    spans = [radial // 8 * k for k in EIGHTHS]
    terms = pl.pallas_call(
        term_kernel,
        out_shape=tuple(f32((2, span, angular)) for span in spans),
        in_specs=[vmem] * 4,
        out_specs=(vmem,) * len(spans),
        compiler_params=params(),
        name="term",
    )(sums, *fields)
    adjoint = pl.pallas_call(
        adjoint_kernel,
        out_shape=pltpu.HBM((2,) + plane, jnp.float32),
        in_specs=[vmem] * 4,
        out_specs=hbm,
        scratch_shapes=[VMEM((2,) + plane, jnp.float32), pltpu.SemaphoreType.DMA(())],
        compiler_params=params(),
        name="adjoint",
    )(sums, far, near, image)
    gradient = ()
    for index, term in enumerate(terms):
        total, arrived = sum_positions(term, positions, slabs)
        gradient = pl.pallas_call(
            functools.partial(close_kernel, first_rows(radial)[index]),
            out_shape=pltpu.HBM((2,) + plane, jnp.float32),
            in_specs=[vmem] * 2 + [hbm] * (index > 0),
            out_specs=hbm,
            scratch_shapes=[VMEM(term.shape, jnp.float32), pltpu.SemaphoreType.DMA(())],
            input_output_aliases={2: 0} if index else {},
            compiler_params=params(),
            name="close",
        )(total, arrived, *((gradient,) if index else ()))
    return gradient, adjoint[None]


def solution(mesh):
    return jax.shard_map(
        local,
        mesh=mesh,
        in_specs=(
            P("slab", None, None),
            P("slab", None, None),
            P(),
            P("pos"),
            P("pos", "slab", None, None),
            P("pos", "slab", None, None),
        ),
        out_specs=(P("slab", None, None), P("pos", "slab", None, None)),
        check_vma=False,
    )
```

```python
import functools

import jax
import jax.numpy as jnp
from jax import lax
from jax.experimental import pallas as pl
from jax.experimental.pallas import tpu as pltpu
from jax.sharding import PartitionSpec as P


ROWS = 16
VMEM = pltpu.VMEM
SMEM = pltpu.SMEM
SUMS = 5
EIGHTHS = (4, 2, 2)


def params():
    return pltpu.CompilerParams(vmem_limit_bytes=40 * 1024 * 1024)


def shifted(ref, index, start, offset):
    total, columns = ref.shape[-2:]
    zero = jnp.zeros((1, columns), jnp.float32)
    if start + offset < 0:
        return jnp.concatenate([zero, ref[index, 0 : ROWS - 1, :]], axis=0)
    if start + offset + ROWS > total:
        return jnp.concatenate([ref[index, start + 1 : total, :], zero], axis=0)
    return ref[index, start + offset : start + offset + ROWS, :]


def turn(value, offset):
    return pltpu.roll(value, offset % value.shape[1], 1)


def in_plane(nu_ref, nu_index, ref, index, start):
    nu = nu_ref[nu_index, start : start + ROWS, :]
    v = ref[index, start : start + ROWS, :]
    total = None
    for offset in (-1, 1):
        across = (nu + turn(nu, offset)) * (v - turn(v, offset))
        total = across if total is None else total + across
        total = total + (nu + shifted(nu_ref, nu_index, start, offset)) * (
            v - shifted(ref, index, start, offset)
        )
    return nu, v, total


def beyond_far():
    slab, _ = place()
    inside = (slab > 0) & (slab < lax.axis_size("slab") - 1)
    return jnp.where(inside, 1.0, 0.0).astype(jnp.float32)


def place():
    slab = lax.axis_index("slab")
    return slab, lax.rem(slab, 2)


def open_kernel(reluctivity, shift, labels, load, potential, far, near, far_potential, near_potential, held, table, sems):
    _, even = place()
    odd = 1 - even
    total = labels.shape[1]
    moves = (
        (labels.at[even], held.at[0]),
        (labels.at[odd], held.at[1]),
        (load.at[even], far.at[1]),
        (load.at[odd], near.at[1]),
        (potential.at[even], far_potential.at[0]),
        (potential.at[odd], near_potential.at[0]),
        (reluctivity, table),
    )
    copies = [pltpu.make_async_copy(src, dst, sems.at[i]) for i, (src, dst) in enumerate(moves)]
    for copy in copies:
        copy.start()
    copies[-1].wait()
    r0, r1, r2, r3 = (table[i] for i in range(4))
    offset = shift[0]
    for side, out in enumerate((far, near)):
        copies[side].wait()
        for start in range(0, total, ROWS):
            rows = slice(start, start + ROWS)
            material = held[side, rows, :]
            if start < total // 2:
                material = pltpu.roll(material, offset, 1)
            out[0, rows, :] = jnp.where(
                material < 2,
                jnp.where(material == 0, r0, r1),
                jnp.where(material == 2, r2, r3),
            )
    for copy in copies[2:-1]:
        copy.wait()


def part_kernel(far, near, far_potential, far_part, near_part, far_early, far_late):
    _, even = place()
    total = far.shape[1]
    half = total // 2
    for own, other, out in ((far, near, far_part), (near, far, near_part)):
        for start in range(0, total, ROWS):
            rows = slice(start, start + ROWS)
            nu, v, total_flux = in_plane(own, 0, own, 1, start)
            total_flux = total_flux + (nu + other[0, rows, :]) * (v - other[1, rows, :])
            out[0, rows, :] = 0.5 * (v + total_flux)
    far_early[0] = far_part[0, pl.ds(pl.multiple_of((1 - even) * half, 8), half), :]
    far_late[0, 0:half, :] = far_part[0, pl.ds(pl.multiple_of(even * half, 8), half), :]
    far_late[0, half : half + total, :] = far_potential[0]


def fold(value):
    return jnp.sum(value.reshape(ROWS // 8, 8, value.shape[1]), axis=0)


def sums_kernel(far, near, far_part, near_part, far_in, near_in, near_part_in, image, near_image_in, sums):
    total, columns = far.shape[1:]
    sides = ((far, far_part, far_in), (near, near_part, near_in))
    end = 1.0 - beyond_far()
    nil = jnp.zeros((8, columns), jnp.float32)
    m0, m1 = nil, nil
    for side, (own, part, halo) in enumerate(sides):
        for start in range(0, total, ROWS):
            rows = slice(start, start + ROWS)
            v = own[1, rows, :]
            flux = 0.5 * (own[0, rows, :] + halo[0, rows, :]) * (v - halo[1, rows, :])
            y = part[0, rows, :] + flux
            image[side, rows, :] = y
            if own is near:
                near_image_in[0, rows, :] = near_part_in[0, rows, :] - flux
            m0 = m0 + fold(v * v)
            m1 = m1 + fold(v * y)
    m0 = jnp.sum(m0, keepdims=True)
    m1 = jnp.sum(m1, keepdims=True)
    c = jnp.where(m0 > 0, m1 / m0, 0.0)
    q, s, t = nil, nil, nil
    for side, (own, _, halo) in enumerate(sides):
        for start in range(0, total, ROWS):
            rows = slice(start, start + ROWS)
            nu, y, total_flux = in_plane(own, 0, image, side, start)
            other = (near, far)[side]
            total_flux = total_flux + (nu + other[0, rows, :]) * (y - image[1 - side, rows, :])
            if own is near:
                total_flux = total_flux + (nu + halo[0, rows, :]) * (y - near_image_in[0, rows, :])
            else:
                total_flux = total_flux + end * (nu * y)
            z = 0.5 * (y + total_flux)
            v = own[1, rows, :]
            w = y - c * v
            u = z - c * y
            q = q + fold(w * w)
            s = s + fold(w * u)
            t = t + fold(v * u)
    for index, value in enumerate((m0, m1, q, s, t, c)):
        value = jnp.sum(value, keepdims=True) if value.shape[0] > 1 else value
        sums[index : index + 1, :] = jnp.broadcast_to(value, (1, sums.shape[1]))


def face_kernel(far, far_in, far_early_in, image, own_sums, sums):
    slab, even = place()
    total, columns = far.shape[1:]
    half = total // 2
    beyond = beyond_far()
    c = own_sums[SUMS : SUMS + 1, 0:1]
    s = jnp.zeros((8, columns), jnp.float32)
    t = s
    for start in range(0, half, ROWS):
        rows = pl.ds(pl.multiple_of(even * half + start, 8), ROWS)
        v = far[1, rows, :]
        y = image[0, rows, :]
        outer_v = far_in[1, rows, :]
        step = v - outer_v
        weight = 0.5 * (far[0, rows, :] + far_in[0, rows, :])
        outer = far_early_in[0, start : start + ROWS, :] - weight * step
        flux = beyond * (weight * (y - outer))
        s = s + fold(((y - c * v) - (outer - c * outer_v)) * flux)
        t = t + fold(step * flux)
    here = lax.broadcasted_iota(jnp.int32, sums.shape[1:], 0) == slab
    added = (None, None, None, s, t)
    for index in range(SUMS):
        value = own_sums[index : index + 1, :]
        if added[index] is not None:
            value = value + jnp.sum(added[index], keepdims=True)
        sums[index] = jnp.where(here, value, 0.0)


def fields_kernel(
    far, near, far_in, near_in, image, far_early_in, far_late_in, near_image_in, potential, near_potential, mask, u1, u2, u3
):
    _, even = place()
    total = far.shape[1]
    scale = 0.25 / lax.axis_size("pos")
    half = total // 2
    beyond_end = beyond_far()
    sides = ((far, even, far_in), (near, 1 - even, near_in))
    for side, (own, layer, halo) in enumerate(sides):
        other = (near, far)[side]
        for start in range(0, total, ROWS):
            rows = slice(start, start + ROWS)
            if own is far:
                piece = slice(start % half, start % half + ROWS)
                early = even == start // half
                part = jnp.where(early, far_early_in[0, piece, :], far_late_in[0, piece, :])
                weight = 0.5 * (far[0, rows, :] + far_in[0, rows, :])
                image_in = beyond_end * (part - weight * (far[1, rows, :] - far_in[1, rows, :]))
                potential_in = far_late_in[0, half + start : half + start + ROWS, :]
            else:
                image_in = near_image_in[0, rows, :]
                potential_in = near_potential[0, rows, :]
            slopes = []
            for ref, index, beyond, inner in (
                (potential, layer, potential_in, potential[1 - layer, rows, :]),
                (own, 1, halo[1, rows, :], other[1, rows, :]),
                (image, side, image_in, image[1 - side, rows, :]),
            ):
                field = ref[index, rows, :]
                slopes.append(
                    (
                        beyond - inner,
                        turn(field, -1) - turn(field, 1),
                        shifted(ref, index, start, 1) - shifted(ref, index, start, -1),
                    )
                )
            weight = scale * (mask[layer, rows, :].astype(jnp.float32) * own[0, rows, :])
            g = [weight * slope for slope in slopes[0]]
            for out, factor, slope in ((u1, 1.0, slopes[1]), (u2, 1.0, slopes[2]), (u3, 0.5, slopes[0])):
                out[layer, rows, :] = factor * (g[0] * slope[0] + g[1] * slope[1] + g[2] * slope[2])


def coefficients(sums):
    m0_d, m1_d, q_d, s_d, t_d = (sums[i] for i in range(SUMS))
    m0 = jnp.sum(m0_d, axis=0, keepdims=True)
    m1 = jnp.sum(m1_d, axis=0, keepdims=True)
    c = m1 / m0
    delta = jnp.where(m0_d > 0, m1_d / m0_d, 0.0) - c
    ww = jnp.sum(q_d + delta * delta * m0_d, axis=0, keepdims=True)
    waw = jnp.sum(s_d + delta * (q_d + t_d) + delta * delta * m1_d, axis=0, keepdims=True)
    alpha0 = m0 / m1
    beta = alpha0 * (ww * alpha0 / m0)
    divisor = waw - ww * (ww / m1)
    alpha1 = jnp.where(divisor == 0, 0.0, ww / divisor)
    return (alpha0 + alpha1 * (1.0 + beta))[:, 0:1], (-alpha1 * alpha0)[:, 0:1]


def term_kernel(sums, u1, u2, u3, *terms):
    a, b = coefficients(sums)
    for term, first in zip(terms, first_rows(u1.shape[1])):
        for layer in range(2):
            for start in range(0, term.shape[1], ROWS):
                rows = slice(first + start, first + start + ROWS)
                term[layer, start : start + ROWS, :] = (
                    a * u1[layer, rows, :] + b * u2[layer, rows, :] + u3[layer, rows, :]
                )


def adjoint_kernel(sums, far, near, image, adjoint, held, sem):
    _, even = place()
    a, b = coefficients(sums)
    for side, (own, layer) in enumerate(((far, even), (near, 1 - even))):
        for start in range(0, far.shape[1], ROWS):
            rows = slice(start, start + ROWS)
            held[layer, rows, :] = a * own[1, rows, :] + b * image[side, rows, :]
    copy = pltpu.make_async_copy(held, adjoint, sem)
    copy.start()
    copy.wait()


def in_hbm(x):
    return pltpu.with_memory_space_constraint(x, pltpu.HBM)


def first_rows(total):
    return [total // 8 * sum(EIGHTHS[:i]) for i in range(len(EIGHTHS))]


def close_kernel(start, total, arrived, *rest):
    gradient, held, sem = rest[-3:]
    held[...] = total[...] + arrived[...]
    copy = pltpu.make_async_copy(held, gradient.at[:, pl.ds(start, total.shape[1]), :], sem)
    copy.start()
    copy.wait()


def pairs(size, first):
    out = []
    for i in range(first, size - 1, 2):
        out += [(i, i + 1), (i + 1, i)]
    return out


def gather_sums(sums, fields, slabs):
    steps = [2**k for k in range(2, slabs.bit_length() - 1)] + [1]
    for step in steps:
        arrived = lax.ppermute(sums, "slab", [(i, i ^ step) for i in range(slabs)])
        if step == steps[-2]:
            arrived, *fields = lax.optimization_barrier((arrived, *fields))
        sums = sums + arrived
    return sums, fields


def partners(step, positions, slabs):
    bits = positions.bit_length() - 1
    route = []
    for p in range(positions):
        for s in range(slabs):
            bit = step if s % 2 == 0 else bits - 1 - step
            route.append((p * slabs + s, (p ^ (1 << bit)) * slabs + s))
    return route


def sum_positions(term, positions, slabs):
    arrived = lax.ppermute(term, ("pos", "slab"), partners(0, positions, slabs))
    for step in range(1, positions.bit_length() - 1):
        term = term + arrived
        arrived = lax.ppermute(term, ("pos", "slab"), partners(step, positions, slabs))
    return term, arrived


def local(labels, magnet_mask, reluctivity, rotor_shift, potential, adjoint_load):
    layers, radial, angular = labels.shape
    positions, slabs = lax.axis_size("pos"), lax.axis_size("slab")
    if layers != 2 or slabs < 8 or slabs & (slabs - 1) or radial % (8 * ROWS) or positions < 2 or positions & (positions - 1):
        raise ValueError("unsupported sizes")
    potential, load = potential[0], adjoint_load[0]
    f32 = functools.partial(jax.ShapeDtypeStruct, dtype=jnp.float32)
    plane = (radial, angular)
    vmem = pl.BlockSpec(memory_space=VMEM)
    smem = pl.BlockSpec(memory_space=SMEM)
    hbm = pl.BlockSpec(memory_space=pltpu.HBM)
    far, near, far_potential, near_potential = pl.pallas_call(
        open_kernel,
        out_shape=tuple(pltpu.VMEM((k,) + plane, jnp.float32) for k in (2, 2, 1, 1)),
        in_specs=[hbm, smem, hbm, hbm, hbm],
        out_specs=(vmem,) * 4,
        scratch_shapes=[
            VMEM((2,) + plane, jnp.int32),
            SMEM(reluctivity.shape, jnp.float32),
            pltpu.SemaphoreType.DMA((7,)),
        ],
        compiler_params=params(),
        name="open",
    )(in_hbm(reluctivity), rotor_shift, in_hbm(labels), in_hbm(load), in_hbm(potential))
    far_in = lax.ppermute(far, "slab", pairs(slabs, 1))
    near_in = lax.ppermute(near, "slab", pairs(slabs, 0))
    half = radial // 2
    far_part, near_part, far_early, far_late = pl.pallas_call(
        part_kernel,
        out_shape=tuple(pltpu.VMEM((1, rows, angular), jnp.float32) for rows in (radial, radial, half, half + radial)),
        in_specs=[vmem] * 3,
        out_specs=(vmem,) * 4,
        compiler_params=params(),
        name="part",
    )(far, near, far_potential)
    far_early_in = lax.ppermute(far_early, "slab", pairs(slabs, 1))
    near_part_in = lax.ppermute(near_part, "slab", pairs(slabs, 0))
    far_late_in = lax.ppermute(far_late, "slab", pairs(slabs, 1))
    image, near_image_in, own_sums = pl.pallas_call(
        sums_kernel,
        out_shape=(f32((2,) + plane), f32((1,) + plane), f32((8, 128))),
        in_specs=[vmem] * 7,
        out_specs=(vmem,) * 3,
        compiler_params=params(),
        name="sums",
    )(far, near, far_part, near_part, far_in, near_in, near_part_in)
    sums = pl.pallas_call(
        face_kernel,
        out_shape=f32((SUMS, slabs, 128)),
        in_specs=[vmem] * 5,
        out_specs=vmem,
        compiler_params=params(),
        name="face",
    )(far, far_in, far_early_in, image, own_sums)
    arrived = lax.ppermute(sums, "slab", [(i, i ^ 2) for i in range(slabs)])
    near_potential, arrived = lax.optimization_barrier((near_potential, arrived))
    near_potential = lax.ppermute(near_potential, "slab", pairs(slabs, 0))
    sums = sums + arrived
    fields = pl.pallas_call(
        fields_kernel,
        out_shape=(f32((2,) + plane),) * 3,
        in_specs=[vmem] * 11,
        out_specs=(vmem,) * 3,
        compiler_params=params(),
        name="fields",
    )(far, near, far_in, near_in, image, far_early_in, far_late_in, near_image_in, potential, near_potential, magnet_mask)
    sums, fields = gather_sums(sums, fields, slabs)
    spans = [radial // 8 * k for k in EIGHTHS]
    terms = pl.pallas_call(
        term_kernel,
        out_shape=tuple(f32((2, span, angular)) for span in spans),
        in_specs=[vmem] * 4,
        out_specs=(vmem,) * len(spans),
        compiler_params=params(),
        name="term",
    )(sums, *fields)
    adjoint = pl.pallas_call(
        adjoint_kernel,
        out_shape=pltpu.HBM((2,) + plane, jnp.float32),
        in_specs=[vmem] * 4,
        out_specs=hbm,
        scratch_shapes=[VMEM((2,) + plane, jnp.float32), pltpu.SemaphoreType.DMA(())],
        compiler_params=params(),
        name="adjoint",
    )(sums, far, near, image)
    gradient = ()
    for index, term in enumerate(terms):
        total, arrived = sum_positions(term, positions, slabs)
        gradient = pl.pallas_call(
            functools.partial(close_kernel, first_rows(radial)[index]),
            out_shape=pltpu.HBM((2,) + plane, jnp.float32),
            in_specs=[vmem] * 2 + [hbm] * (index > 0),
            out_specs=hbm,
            scratch_shapes=[VMEM(term.shape, jnp.float32), pltpu.SemaphoreType.DMA(())],
            input_output_aliases={2: 0} if index else {},
            compiler_params=params(),
            name="close",
        )(total, arrived, *((gradient,) if index else ()))
    return gradient, adjoint[None]


def solution(mesh):
    return jax.shard_map(
        local,
        mesh=mesh,
        in_specs=(
            P("slab", None, None),
            P("slab", None, None),
            P(),
            P("pos"),
            P("pos", "slab", None, None),
            P("pos", "slab", None, None),
        ),
        out_specs=(P("slab", None, None), P("pos", "slab", None, None)),
        check_vma=False,
    )
```

```python
import functools

import jax
import jax.numpy as jnp
from jax import lax
from jax.experimental import pallas as pl
from jax.experimental.pallas import tpu as pltpu
from jax.sharding import PartitionSpec as P


ROWS = 32
VMEM = pltpu.VMEM
SMEM = pltpu.SMEM
SUMS = 5
EIGHTHS = (3, 3, 2)


def params():
    return pltpu.CompilerParams(vmem_limit_bytes=40 * 1024 * 1024)


def shifted(ref, index, start, offset):
    total, columns = ref.shape[-2:]
    zero = jnp.zeros((1, columns), jnp.float32)
    if start + offset < 0:
        return jnp.concatenate([zero, ref[index, 0 : ROWS - 1, :]], axis=0)
    if start + offset + ROWS > total:
        return jnp.concatenate([ref[index, start + 1 : total, :], zero], axis=0)
    return ref[index, start + offset : start + offset + ROWS, :]


def turn(value, offset):
    return pltpu.roll(value, offset % value.shape[1], 1)


def in_plane(nu_ref, nu_index, ref, index, start):
    nu = nu_ref[nu_index, start : start + ROWS, :]
    v = ref[index, start : start + ROWS, :]
    total = None
    for offset in (-1, 1):
        across = (nu + turn(nu, offset)) * (v - turn(v, offset))
        total = across if total is None else total + across
        total = total + (nu + shifted(nu_ref, nu_index, start, offset)) * (
            v - shifted(ref, index, start, offset)
        )
    return nu, v, total


def beyond_far():
    slab, _ = place()
    inside = (slab > 0) & (slab < lax.axis_size("slab") - 1)
    return jnp.where(inside, 1.0, 0.0).astype(jnp.float32)


def place():
    slab = lax.axis_index("slab")
    return slab, lax.rem(slab, 2)


def open_kernel(reluctivity, shift, labels, load, potential, far, near, far_potential, near_potential, held, table, sems):
    _, even = place()
    odd = 1 - even
    total = labels.shape[1]
    moves = (
        (labels.at[even], held.at[0]),
        (labels.at[odd], held.at[1]),
        (load.at[even], far.at[1]),
        (load.at[odd], near.at[1]),
        (potential.at[even], far_potential.at[0]),
        (potential.at[odd], near_potential.at[0]),
        (reluctivity, table),
    )
    copies = [pltpu.make_async_copy(src, dst, sems.at[i]) for i, (src, dst) in enumerate(moves)]
    for copy in copies:
        copy.start()
    copies[-1].wait()
    r0, r1, r2, r3 = (table[i] for i in range(4))
    offset = shift[0]
    for side, out in enumerate((far, near)):
        copies[side].wait()
        for start in range(0, total, ROWS):
            rows = slice(start, start + ROWS)
            material = held[side, rows, :]
            if start < total // 2:
                material = pltpu.roll(material, offset, 1)
            out[0, rows, :] = jnp.where(
                material < 2,
                jnp.where(material == 0, r0, r1),
                jnp.where(material == 2, r2, r3),
            )
    for copy in copies[2:-1]:
        copy.wait()


def part_kernel(far, near, far_potential, far_part, near_part, far_early, far_late):
    _, even = place()
    total = far.shape[1]
    half = total // 2
    for own, other, out in ((far, near, far_part), (near, far, near_part)):
        for start in range(0, total, ROWS):
            rows = slice(start, start + ROWS)
            nu, v, total_flux = in_plane(own, 0, own, 1, start)
            total_flux = total_flux + (nu + other[0, rows, :]) * (v - other[1, rows, :])
            out[0, rows, :] = 0.5 * (v + total_flux)
    far_early[0] = far_part[0, pl.ds(pl.multiple_of((1 - even) * half, 8), half), :]
    far_late[0, 0:half, :] = far_part[0, pl.ds(pl.multiple_of(even * half, 8), half), :]
    far_late[0, half : half + total, :] = far_potential[0]


def fold(value):
    return jnp.sum(value.reshape(ROWS // 8, 8, value.shape[1]), axis=0)


def sums_kernel(far, near, far_part, near_part, far_in, near_in, near_part_in, image, near_image_in, sums):
    total, columns = far.shape[1:]
    sides = ((far, far_part, far_in), (near, near_part, near_in))
    end = 1.0 - beyond_far()
    nil = jnp.zeros((8, columns), jnp.float32)
    m0, m1 = nil, nil
    for side, (own, part, halo) in enumerate(sides):
        for start in range(0, total, ROWS):
            rows = slice(start, start + ROWS)
            v = own[1, rows, :]
            flux = 0.5 * (own[0, rows, :] + halo[0, rows, :]) * (v - halo[1, rows, :])
            y = part[0, rows, :] + flux
            image[side, rows, :] = y
            if own is near:
                near_image_in[0, rows, :] = near_part_in[0, rows, :] - flux
            m0 = m0 + fold(v * v)
            m1 = m1 + fold(v * y)
    m0 = jnp.sum(m0, keepdims=True)
    m1 = jnp.sum(m1, keepdims=True)
    c = jnp.where(m0 > 0, m1 / m0, 0.0)
    q, s, t = nil, nil, nil
    for side, (own, _, halo) in enumerate(sides):
        for start in range(0, total, ROWS):
            rows = slice(start, start + ROWS)
            nu, y, total_flux = in_plane(own, 0, image, side, start)
            other = (near, far)[side]
            total_flux = total_flux + (nu + other[0, rows, :]) * (y - image[1 - side, rows, :])
            if own is near:
                total_flux = total_flux + (nu + halo[0, rows, :]) * (y - near_image_in[0, rows, :])
            else:
                total_flux = total_flux + end * (nu * y)
            z = 0.5 * (y + total_flux)
            v = own[1, rows, :]
            w = y - c * v
            u = z - c * y
            q = q + fold(w * w)
            s = s + fold(w * u)
            t = t + fold(v * u)
    for index, value in enumerate((m0, m1, q, s, t, c)):
        value = jnp.sum(value, keepdims=True) if value.shape[0] > 1 else value
        sums[index : index + 1, :] = jnp.broadcast_to(value, (1, sums.shape[1]))


def face_kernel(far, far_in, far_early_in, image, own_sums, sums):
    slab, even = place()
    total, columns = far.shape[1:]
    half = total // 2
    beyond = beyond_far()
    c = own_sums[SUMS : SUMS + 1, 0:1]
    s = jnp.zeros((8, columns), jnp.float32)
    t = s
    for start in range(0, half, ROWS):
        rows = pl.ds(pl.multiple_of(even * half + start, 8), ROWS)
        v = far[1, rows, :]
        y = image[0, rows, :]
        outer_v = far_in[1, rows, :]
        step = v - outer_v
        weight = 0.5 * (far[0, rows, :] + far_in[0, rows, :])
        outer = far_early_in[0, start : start + ROWS, :] - weight * step
        flux = beyond * (weight * (y - outer))
        s = s + fold(((y - c * v) - (outer - c * outer_v)) * flux)
        t = t + fold(step * flux)
    here = lax.broadcasted_iota(jnp.int32, sums.shape[1:], 0) == slab
    added = (None, None, None, s, t)
    for index in range(SUMS):
        value = own_sums[index : index + 1, :]
        if added[index] is not None:
            value = value + jnp.sum(added[index], keepdims=True)
        sums[index] = jnp.where(here, value, 0.0)


def fields_kernel(
    far, near, far_in, near_in, image, far_early_in, far_late_in, near_image_in, potential, near_potential, mask, u1, u2, u3
):
    _, even = place()
    total = far.shape[1]
    scale = 0.25 / lax.axis_size("pos")
    half = total // 2
    beyond_end = beyond_far()
    sides = ((far, even, far_in), (near, 1 - even, near_in))
    for side, (own, layer, halo) in enumerate(sides):
        other = (near, far)[side]
        for start in range(0, total, ROWS):
            rows = slice(start, start + ROWS)
            if own is far:
                piece = slice(start % half, start % half + ROWS)
                early = even == start // half
                part = jnp.where(early, far_early_in[0, piece, :], far_late_in[0, piece, :])
                weight = 0.5 * (far[0, rows, :] + far_in[0, rows, :])
                image_in = beyond_end * (part - weight * (far[1, rows, :] - far_in[1, rows, :]))
                potential_in = far_late_in[0, half + start : half + start + ROWS, :]
            else:
                image_in = near_image_in[0, rows, :]
                potential_in = near_potential[0, rows, :]
            slopes = []
            for ref, index, beyond, inner in (
                (potential, layer, potential_in, potential[1 - layer, rows, :]),
                (own, 1, halo[1, rows, :], other[1, rows, :]),
                (image, side, image_in, image[1 - side, rows, :]),
            ):
                field = ref[index, rows, :]
                slopes.append(
                    (
                        beyond - inner,
                        turn(field, -1) - turn(field, 1),
                        shifted(ref, index, start, 1) - shifted(ref, index, start, -1),
                    )
                )
            weight = scale * (mask[layer, rows, :].astype(jnp.float32) * own[0, rows, :])
            g = [weight * slope for slope in slopes[0]]
            for out, factor, slope in ((u1, 1.0, slopes[1]), (u2, 1.0, slopes[2]), (u3, 0.5, slopes[0])):
                out[layer, rows, :] = factor * (g[0] * slope[0] + g[1] * slope[1] + g[2] * slope[2])


def coefficients(sums):
    m0_d, m1_d, q_d, s_d, t_d = (sums[i] for i in range(SUMS))
    m0 = jnp.sum(m0_d, axis=0, keepdims=True)
    m1 = jnp.sum(m1_d, axis=0, keepdims=True)
    c = m1 / m0
    delta = jnp.where(m0_d > 0, m1_d / m0_d, 0.0) - c
    ww = jnp.sum(q_d + delta * delta * m0_d, axis=0, keepdims=True)
    waw = jnp.sum(s_d + delta * (q_d + t_d) + delta * delta * m1_d, axis=0, keepdims=True)
    alpha0 = m0 / m1
    beta = alpha0 * (ww * alpha0 / m0)
    divisor = waw - ww * (ww / m1)
    alpha1 = jnp.where(divisor == 0, 0.0, ww / divisor)
    return (alpha0 + alpha1 * (1.0 + beta))[:, 0:1], (-alpha1 * alpha0)[:, 0:1]


def term_kernel(sums, u1, u2, u3, *terms):
    a, b = coefficients(sums)
    for term, first in zip(terms, first_rows(u1.shape[1])):
        for layer in range(2):
            for start in range(0, term.shape[1], ROWS):
                rows = slice(first + start, first + start + ROWS)
                term[layer, start : start + ROWS, :] = (
                    a * u1[layer, rows, :] + b * u2[layer, rows, :] + u3[layer, rows, :]
                )


def adjoint_kernel(sums, far, near, image, adjoint, held, sem):
    _, even = place()
    a, b = coefficients(sums)
    for side, (own, layer) in enumerate(((far, even), (near, 1 - even))):
        for start in range(0, far.shape[1], ROWS):
            rows = slice(start, start + ROWS)
            held[layer, rows, :] = a * own[1, rows, :] + b * image[side, rows, :]
    copy = pltpu.make_async_copy(held, adjoint, sem)
    copy.start()
    copy.wait()


def in_hbm(x):
    return pltpu.with_memory_space_constraint(x, pltpu.HBM)


def first_rows(total):
    return [total // 8 * sum(EIGHTHS[:i]) for i in range(len(EIGHTHS))]


def close_kernel(start, total, arrived, *rest):
    gradient, held, sem = rest[-3:]
    held[...] = total[...] + arrived[...]
    copy = pltpu.make_async_copy(held, gradient.at[:, pl.ds(start, total.shape[1]), :], sem)
    copy.start()
    copy.wait()


def pairs(size, first):
    out = []
    for i in range(first, size - 1, 2):
        out += [(i, i + 1), (i + 1, i)]
    return out


def gather_sums(sums, fields, slabs):
    steps = [2**k for k in range(2, slabs.bit_length() - 1)] + [1]
    for step in steps:
        arrived = lax.ppermute(sums, "slab", [(i, i ^ step) for i in range(slabs)])
        if step == steps[-2]:
            arrived, *fields = lax.optimization_barrier((arrived, *fields))
        sums = sums + arrived
    return sums, fields


def partners(step, positions, slabs):
    bits = positions.bit_length() - 1
    route = []
    for p in range(positions):
        for s in range(slabs):
            bit = step if s % 2 == 0 else bits - 1 - step
            route.append((p * slabs + s, (p ^ (1 << bit)) * slabs + s))
    return route


def sum_positions(term, positions, slabs):
    arrived = lax.ppermute(term, ("pos", "slab"), partners(0, positions, slabs))
    for step in range(1, positions.bit_length() - 1):
        term = term + arrived
        arrived = lax.ppermute(term, ("pos", "slab"), partners(step, positions, slabs))
    return term, arrived


def local(labels, magnet_mask, reluctivity, rotor_shift, potential, adjoint_load):
    layers, radial, angular = labels.shape
    positions, slabs = lax.axis_size("pos"), lax.axis_size("slab")
    if layers != 2 or slabs < 8 or slabs & (slabs - 1) or radial % (8 * ROWS) or positions < 2 or positions & (positions - 1):
        raise ValueError("unsupported sizes")
    potential, load = potential[0], adjoint_load[0]
    f32 = functools.partial(jax.ShapeDtypeStruct, dtype=jnp.float32)
    plane = (radial, angular)
    vmem = pl.BlockSpec(memory_space=VMEM)
    smem = pl.BlockSpec(memory_space=SMEM)
    hbm = pl.BlockSpec(memory_space=pltpu.HBM)
    far, near, far_potential, near_potential = pl.pallas_call(
        open_kernel,
        out_shape=tuple(pltpu.VMEM((k,) + plane, jnp.float32) for k in (2, 2, 1, 1)),
        in_specs=[hbm, smem, hbm, hbm, hbm],
        out_specs=(vmem,) * 4,
        scratch_shapes=[
            VMEM((2,) + plane, jnp.int32),
            SMEM(reluctivity.shape, jnp.float32),
            pltpu.SemaphoreType.DMA((7,)),
        ],
        compiler_params=params(),
        name="open",
    )(in_hbm(reluctivity), rotor_shift, in_hbm(labels), in_hbm(load), in_hbm(potential))
    far_in = lax.ppermute(far, "slab", pairs(slabs, 1))
    near_in = lax.ppermute(near, "slab", pairs(slabs, 0))
    half = radial // 2
    far_part, near_part, far_early, far_late = pl.pallas_call(
        part_kernel,
        out_shape=tuple(pltpu.VMEM((1, rows, angular), jnp.float32) for rows in (radial, radial, half, half + radial)),
        in_specs=[vmem] * 3,
        out_specs=(vmem,) * 4,
        compiler_params=params(),
        name="part",
    )(far, near, far_potential)
    far_early_in = lax.ppermute(far_early, "slab", pairs(slabs, 1))
    near_part_in = lax.ppermute(near_part, "slab", pairs(slabs, 0))
    far_late_in = lax.ppermute(far_late, "slab", pairs(slabs, 1))
    image, near_image_in, own_sums = pl.pallas_call(
        sums_kernel,
        out_shape=(f32((2,) + plane), f32((1,) + plane), f32((8, 128))),
        in_specs=[vmem] * 7,
        out_specs=(vmem,) * 3,
        compiler_params=params(),
        name="sums",
    )(far, near, far_part, near_part, far_in, near_in, near_part_in)
    sums = pl.pallas_call(
        face_kernel,
        out_shape=f32((SUMS, slabs, 128)),
        in_specs=[vmem] * 5,
        out_specs=vmem,
        compiler_params=params(),
        name="face",
    )(far, far_in, far_early_in, image, own_sums)
    arrived = lax.ppermute(sums, "slab", [(i, i ^ 2) for i in range(slabs)])
    near_potential, arrived = lax.optimization_barrier((near_potential, arrived))
    near_potential = lax.ppermute(near_potential, "slab", pairs(slabs, 0))
    sums = sums + arrived
    fields = pl.pallas_call(
        fields_kernel,
        out_shape=(f32((2,) + plane),) * 3,
        in_specs=[vmem] * 11,
        out_specs=(vmem,) * 3,
        compiler_params=params(),
        name="fields",
    )(far, near, far_in, near_in, image, far_early_in, far_late_in, near_image_in, potential, near_potential, magnet_mask)
    sums, fields = gather_sums(sums, fields, slabs)
    spans = [radial // 8 * k for k in EIGHTHS]
    terms = pl.pallas_call(
        term_kernel,
        out_shape=tuple(f32((2, span, angular)) for span in spans),
        in_specs=[vmem] * 4,
        out_specs=(vmem,) * len(spans),
        compiler_params=params(),
        name="term",
    )(sums, *fields)
    adjoint = pl.pallas_call(
        adjoint_kernel,
        out_shape=pltpu.HBM((2,) + plane, jnp.float32),
        in_specs=[vmem] * 4,
        out_specs=hbm,
        scratch_shapes=[VMEM((2,) + plane, jnp.float32), pltpu.SemaphoreType.DMA(())],
        compiler_params=params(),
        name="adjoint",
    )(sums, far, near, image)
    gradient = ()
    for index, term in enumerate(terms):
        total, arrived = sum_positions(term, positions, slabs)
        gradient = pl.pallas_call(
            functools.partial(close_kernel, first_rows(radial)[index]),
            out_shape=pltpu.HBM((2,) + plane, jnp.float32),
            in_specs=[vmem] * 2 + [hbm] * (index > 0),
            out_specs=hbm,
            scratch_shapes=[VMEM(term.shape, jnp.float32), pltpu.SemaphoreType.DMA(())],
            input_output_aliases={2: 0} if index else {},
            compiler_params=params(),
            name="close",
        )(total, arrived, *((gradient,) if index else ()))
    return gradient, adjoint[None]


def solution(mesh):
    return jax.shard_map(
        local,
        mesh=mesh,
        in_specs=(
            P("slab", None, None),
            P("slab", None, None),
            P(),
            P("pos"),
            P("pos", "slab", None, None),
            P("pos", "slab", None, None),
        ),
        out_specs=(P("slab", None, None), P("pos", "slab", None, None)),
        check_vma=False,
    )
```
